128 devices in a mesh: mem: 4 (over x_hi, core), pts: 32 (over x_lo, y, z).
Axes of the slice: x: 4 (x_hi: 2, x_lo: 2; x = x_hi * 2 + x_lo), y: 4, z: 4, core: 2. Of those that a mesh axis runs over, the one named last changes fastest.
Arguments:
- latent: bfloat16 [8, 65536, 1024], P('mem', 'pts'), may hold values from -6 to 6
- head_weight: bfloat16 [102, 1024], replicated, may hold values from -0.1875 to 0.1875
- head_bias: bfloat16 [102], replicated, may hold values from -3 to 3
- targets: float32 [102, 65536], P(None, 'pts'), may hold values from -6 to 6
- cell_area: float32 [65536], P('pts'), may hold values from 0.3 to 3
- field_level: int32 [102], replicated, may hold values from 0 to 12
- source: int32 [65536], P('pts'), may hold values from 0 to 65535, as said below
Outputs:
- latent_grad: bfloat16 [8, 65536, 1024], P('mem', 'pts')
- weight_grad: float32 [102, 1024], replicated
- bias_grad: float32 [102], replicated
The draws below stay inside these ranges and needn't reach their ends.
Inputs may be any that keep to these rules, and one draw needn't show every extreme that they name: source is a permutation of the grid points; slot s of the block of 2048 slots of pts index j (s counted from 0 inside the block) holds a point of the grid block of pts index s mod (32), that is, a grid index in that block's range of 2048 indices.
All inputs are finite; a program needn't handle non-finite values.
Results may differ from the reference program's by a relative error of at most 0.0085.
Values may be sent and summed in bfloat16 or wider, within the bound.
A program may use at most 64 MiB of HBM per device.

```python
import math
import jax
import jax.numpy as jnp
from jax import lax

M = 8
F = 102
L = 1024
P_DEV = 2048
NPTS = 65536


def draw_source(key, part):
    key = jax.random.fold_in(key, 7)
    shards = NPTS // P_DEV
    keys = jax.random.split(key, shards)
    shuffled = jax.vmap(lambda subkey: jax.random.permutation(subkey, P_DEV))(keys)
    shuffled = shuffled.astype(jnp.int32) + (jnp.arange(shards, dtype=jnp.int32) * P_DEV)[:, None]
    arranged = shuffled.reshape(shards, shards, P_DEV // shards).transpose(1, 2, 0)
    return arranged.reshape(NPTS).astype(jnp.int32)


def set_ends(array, rng, least, top_value):
    shape = array.shape
    index_at = [jax.random.randint(jax.random.fold_in(rng, axis), (), 0, shape[axis]) for axis in range(len(shape))]
    array = array.at[tuple(index_at)].set(least)
    longest = shape.index(max(shape))
    index_at[longest] = (index_at[longest] + 1) % shape[longest]
    return array.at[tuple(index_at)].set(top_value)


def shard_levels(key, shape, cuts, least, top_value):
    level, own = 1.0, jax.random.fold_in(key, 6)
    for dim, shards_of in cuts:
        steps = jnp.exp(jax.random.uniform(jax.random.fold_in(own, dim), (shards_of,), jnp.float32, least / len(cuts), top_value / len(cuts)))
        level = level * jnp.repeat(steps, shape[dim] // shards_of).reshape([-1 if axis == dim else 1 for axis in range(len(shape))])
    return level


def noise(rng, dims, deviation, reach, cuts=(), held_as=jnp.bfloat16):
    factor_of = shard_levels(rng, dims, cuts, -0.22, 0.18) if cuts else 1.0
    array = jax.random.normal(rng, dims, jnp.float32) * deviation * factor_of
    return jnp.minimum(jnp.maximum(array, -reach), reach).astype(held_as)


def setup_inputs(seed: int = 0) -> dict:
    streams_of = jax.random.split(jax.random.key(seed), 8)
    return {
        "latent": noise(streams_of[0], (M, NPTS, L), 1.0, 6.0, ((0, 4), (1, 32))),
        "head_weight": noise(streams_of[1], (F, L), L ** -0.5, 0.1875),
        "head_bias": noise(streams_of[2], (F,), 0.5, 3.0),
        "targets": noise(streams_of[3], (F, NPTS), 1.0, 6.0, ((1, 32),), jnp.float32),
        "cell_area": jnp.clip(jnp.exp(math.log(3.0) - 2.3025851 * jax.random.uniform(streams_of[4], (NPTS,), jnp.float32) ** shard_levels(streams_of[4], (NPTS,), ((0, 32),), -0.2, 0.2)), 0.3, 3.0),
        "field_level": set_ends(jax.random.randint(streams_of[5], (F,), 0, 13), jax.random.fold_in(streams_of[5], 1), 0, 12).astype(jnp.int32),
        "source": draw_source(jax.random.fold_in(streams_of[7], 71), 0),
    }


FAIR_ALPHA = 0.95
SMOOTH_WIDTH = 0.25

def smooth_sign(diff):
    return diff * lax.rsqrt(diff * diff + SMOOTH_WIDTH * SMOOTH_WIDTH)

def crps_grad(own_rows, members, target_slot, area_slot, weight):
    total = members.shape[0]
    own = own_rows.astype(jnp.float32)
    fair = smooth_sign(own - target_slot[None].astype(jnp.float32)) / total
    spread = jnp.zeros(own.shape, jnp.float32)
    for member in range(total):
        spread = spread + smooth_sign(own - members[member].astype(jnp.float32)[None])
    coeff = (1.0 - (1.0 - FAIR_ALPHA) / total) / (total * (total - 1))
    grad = fair - coeff * spread
    scaled = total * weight[None, :, None] * area_slot[None, None, :] * grad
    return scaled.astype(jnp.bfloat16)

def reference(latent, head_weight, head_bias, targets, cell_area, field_level, source):
    index = source.astype(jnp.int32)
    target_slot = jnp.take(targets, index, axis=1)
    area_slot = jnp.take(cell_area, index)
    weight = (field_level.astype(jnp.float32) + 1.0) / 7.0
    bias = head_bias.astype(jnp.float32)

    def forward(latent_member):
        prod = jnp.dot(head_weight, latent_member.T, preferred_element_type=jnp.float32)
        return (prod + bias[:, None]).astype(jnp.bfloat16)
    predicted = lax.map(forward, latent)
    member_grad = crps_grad(predicted, predicted, target_slot, area_slot, weight)

    def backward(grad_member):
        return jnp.dot(grad_member.T, head_weight, preferred_element_type=jnp.float32).astype(jnp.bfloat16)
    latent_grad = lax.map(backward, member_grad)

    def accumulate(carry, pair):
        grad_member, latent_member = pair
        return (carry + jnp.dot(grad_member, latent_member, preferred_element_type=jnp.float32), None)
    summed, unused = lax.scan(accumulate, jnp.zeros(head_weight.shape, jnp.float32), (member_grad, latent))
    norm_factor = float(M * NPTS) ** (-0.5)
    weight_grad = summed * norm_factor
    bias_grad = lax.optimization_barrier(jnp.sum(member_grad.astype(jnp.float32), axis=(0, 2))) * norm_factor
    return (latent_grad, weight_grad, bias_grad)
```

```python
import jax
import jax.numpy as jnp
from jax import lax
from jax.experimental import pallas as pl
from jax.experimental.pallas import tpu as pltpu
from jax.sharding import PartitionSpec as P

M = 8
F = 102
L = 1024
FP = 104
FB = 112
MAIN = 96
SLOTS = 2048
HALF = 1024
CH = 256
NK = HALF // CH
ROWS = 208
PTS = 32
GROUP = 64
OWN = 52
MESH = pl.DeviceIdType.MESH

FAIR_ALPHA = 0.95
SMOOTH_WIDTH = 0.25
SPREAD = (1.0 - (1.0 - FAIR_ALPHA) / M) / (M - 1)


def smooth_sign(diff):
    return diff * lax.rsqrt(diff * diff + SMOOTH_WIDTH * SMOOTH_WIDTH)


def crps_rows(own, far, target, scale):
    spread = [None] * len(own)

    def add(at, term):
        spread[at] = term if spread[at] is None else spread[at] + term

    for a in range(len(own)):
        for b in range(a + 1, len(own)):
            q = smooth_sign(own[a] - own[b])
            add(a, q)
            add(b, -q)
        for other in far:
            add(a, smooth_sign(own[a] - other))
    return [
        (scale * (smooth_sign(own[a] - target) - SPREAD * spread[a])).astype(jnp.bfloat16)
        for a in range(len(own))
    ]


def column(row, rows):
    n = row.shape[1]
    at = lax.broadcasted_iota(jnp.int32, (rows, n), 0)
    lane = lax.broadcasted_iota(jnp.int32, (rows, n), 1)
    return jnp.sum(jnp.where(at == lane, row, 0.0), axis=1, keepdims=True)


def main_kernel(
    latent, w_ref, bias_ref, level_ref, tgt, area_ref, src_ref,
    g_ref, ws_ref,
    lat, wpad, tv, tt, last8, asked, tq, rq, tslot, bcol, wcol,
    psend, pmate, prem, gsend, acc, brow, wt, wc, rs, ag,
    lat_sem, tgt_sem, ask_s, ask_r, tq_s, tq_r,
    ps_far, pr_far, ps_mate, pr_mate, gs, gr, core_s, core_r, ar_s, ar_r,
):
    i = lax.axis_index("mem")
    pts = lax.axis_index("pts")
    xh = lax.div(i, 2)
    c = lax.rem(i, 2)
    xl = lax.div(pts, 16)
    me = xh * PTS + pts
    mate = (xh * 2 + (1 - c), pts)
    far = ((1 - xh) * 2 + c, pts)
    far_mate = ((1 - xh) * 2 + (1 - c), pts)
    halves = (c, 1 - c)

    def lat_copy(e, k):
        off = pl.multiple_of(halves[e] * HALF + k * CH, CH)
        return pltpu.make_async_copy(
            latent.at[:, pl.ds(off, CH)], lat.at[e, k], lat_sem.at[e * NK + k]
        )

    tgt_copy = pltpu.make_async_copy(tgt, tv, tgt_sem)
    for k in range(NK):
        for e in range(2):
            lat_copy(e, k).start()
        if k == 0:
            tgt_copy.start()

    barrier = pltpu.get_barrier_semaphore()

    def group_device(n):
        q = lax.rem(me + n, GROUP)
        q_xh = lax.div(q, PTS)
        q_pts = lax.rem(q, PTS)
        return q, q_xh, q_pts, (q_xh * 2 + c, q_pts)

    pl.semaphore_signal(barrier, inc=1, device_id=far_mate, device_id_type=MESH)
    pl.semaphore_signal(barrier, inc=1, device_id=mate, device_id_type=MESH)

    def greet(n, _):
        pl.semaphore_signal(barrier, inc=1, device_id=group_device(n)[3], device_id_type=MESH)
        return 0

    lax.fori_loop(1, GROUP, greet, 0)

    wpad[...] = jnp.zeros_like(wpad)
    wpad[0:F, :] = w_ref[...]
    bcol[...] = jnp.broadcast_to(column(bias_ref[...].astype(jnp.float32), FP), bcol.shape)
    level = (level_ref[...].astype(jnp.float32) + 1.0) / 7.0
    wcol[...] = jnp.broadcast_to(column(level, FP), wcol.shape)
    acc[...] = jnp.zeros_like(acc)
    brow[...] = jnp.zeros_like(brow)

    pl.semaphore_wait(barrier, GROUP + 1)

    def owner_of(n):
        p = lax.rem(pts + n, PTS)
        differ = lax.rem(lax.div(p, 16) + xl, 2)
        return p, (lax.rem(xh + c * differ, 2) * 2 + c, p)

    def ask(n, _):
        pltpu.make_async_remote_copy(
            src_ref=src_ref.at[pl.ds(pl.multiple_of(8 * c, 8), 8)],
            dst_ref=asked.at[pts],
            send_sem=ask_s,
            recv_sem=ask_r,
            device_id=owner_of(n)[1],
            device_id_type=MESH,
        ).start()
        return 0

    lax.fori_loop(1, PTS, ask, 0)
    asked[pts] = src_ref[pl.ds(pl.multiple_of(8 * c, 8), 8), :]

    def far_copy(e, k):
        return pltpu.make_async_remote_copy(
            src_ref=psend.at[e, k],
            dst_ref=prem.at[e, k],
            send_sem=ps_far.at[e * NK + k],
            recv_sem=pr_far.at[e * NK + k],
            device_id=far if e == 0 else far_mate,
            device_id_type=MESH,
        )

    def mate_copy(k):
        return pltpu.make_async_remote_copy(
            src_ref=psend.at[1, k],
            dst_ref=pmate.at[k],
            send_sem=ps_mate.at[k],
            recv_sem=pr_mate.at[k],
            device_id=mate,
            device_id_type=MESH,
        )

    def predict(e, k):
        lat_copy(e, k).wait()
        rest = []
        for m in range(2):
            pred = lax.dot_general(
                wpad[...], lat[e, k, m], (((1,), (1,)), ((), ())),
                preferred_element_type=jnp.float32,
            )[0:FP]
            pred = pred + bcol[:, 0:1]
            psend[e, k, m * MAIN : (m + 1) * MAIN, :] = pred[0:MAIN].astype(jnp.bfloat16)
            rest.append(pred[MAIN:FP])
        psend[e, k, 2 * MAIN :, :] = jnp.concatenate(rest, axis=0).astype(jnp.bfloat16)
        far_copy(e, k).start()
        if e == 1:
            mate_copy(k).start()

    for e in range(2):
        predict(e, 0)

    tgt_copy.wait()
    tt[FP:128, :] = jnp.zeros((128 - FP, SLOTS), jnp.bfloat16)
    tt[128 + FP :, :] = jnp.zeros((128 - FP, SLOTS), jnp.bfloat16)
    last8[...] = jnp.zeros_like(last8)
    last8[0 : F - MAIN, :] = tv[MAIN:F, :]
    last8[F - MAIN : F - MAIN + 1, :] = area_ref[...]

    def split(value, at):
        high = value.astype(jnp.bfloat16)
        tt[at : at + value.shape[0], :] = high
        low = (value - high.astype(jnp.float32)).astype(jnp.bfloat16)
        tt[128 + at : 128 + at + value.shape[0], :] = low

    for at in range(0, MAIN, 32):
        split(tv[at : at + 32, :], at)
    split(last8[...], MAIN)

    def asked_bytes(sem):
        return pltpu.make_async_copy(
            asked.at[pl.ds(0, PTS - 1)], asked.at[pl.ds(0, PTS - 1)], sem
        )

    asked_bytes(ask_r).wait()
    found = asked[...].reshape(PTS * 8, 128) - pts * SLOTS
    lane = lax.broadcasted_iota(jnp.int32, (PTS * 8, 128), 1)
    row = lax.broadcasted_iota(jnp.int32, (PTS * 8, 128), 0)
    found = jnp.where(lax.rem(lane, 32) == pts, found, 0)
    spread_row = lax.broadcasted_iota(jnp.int32, (128, 128), 0)
    spread_lane = lax.broadcasted_iota(jnp.int32, (128, 128), 1)
    spread = jnp.where(lax.div(spread_row, 32) == lax.div(spread_lane, 32), 1.0, 0.0)
    spread = spread.astype(jnp.bfloat16)
    high = lax.shift_right_logical(found, 6).astype(jnp.float32).astype(jnp.bfloat16)
    low = lax.bitwise_and(found, 63).astype(jnp.float32).astype(jnp.bfloat16)
    wide = 64.0 * jnp.dot(high, spread, preferred_element_type=jnp.float32) + jnp.dot(
        low, spread, preferred_element_type=jnp.float32
    )
    wide = jnp.where(lax.rem(lane, 32) == lax.rem(row, 32), wide, 0.0)
    wanted = jnp.sum(wide.reshape(8, 32, 128), axis=1)
    for half in range(4):
        cols = jnp.concatenate(
            [column(wanted[2 * half + b : 2 * half + b + 1, :], 128) for b in range(2)], axis=0
        ).astype(jnp.int32)
        place = lax.broadcasted_iota(jnp.int32, (256, SLOTS), 1)
        onehot = jnp.where(place == cols, 1.0, 0.0).astype(jnp.bfloat16)
        got = lax.dot_general(
            onehot, tt[...], (((1,), (1,)), ((), ())), preferred_element_type=jnp.float32
        )
        got = got[:, 0:128] + got[:, 128:256]
        tq[2 * half : 2 * half + 2] = got.reshape(2, 4, 4, 8, 128)

    def answer(n, _):
        p, device = owner_of(n)
        pltpu.make_async_remote_copy(
            src_ref=tq.at[lax.div(p, 4), :, lax.rem(p, 4)],
            dst_ref=rq.at[:, pts],
            send_sem=tq_s,
            recv_sem=tq_r,
            device_id=device,
            device_id_type=MESH,
        ).start()
        return 0

    lax.fori_loop(1, PTS, answer, 0)
    rq[:, pts] = tq[lax.div(pts, 4), :, lax.rem(pts, 4)]

    for k in range(1, NK):
        for e in range(2):
            predict(e, k)

    def rq_bytes(sem):
        return pltpu.make_async_copy(
            rq.at[:, pl.ds(0, PTS - 1)], rq.at[:, pl.ds(0, PTS - 1)], sem
        )

    rq_bytes(tq_r).wait()
    for r in range(8):
        rows = jnp.concatenate([rq[a, :, r, :] for a in range(4)], axis=0)
        tslot[:, 128 * r : 128 * (r + 1)] = rows.T[0:FP]

    def grad_copy(k):
        return pltpu.make_async_remote_copy(
            src_ref=gsend.at[k],
            dst_ref=g_ref.at[c, k],
            send_sem=gs.at[k],
            recv_sem=gr.at[k],
            device_id=mate,
            device_id_type=MESH,
        )

    def crps_chunk(k):
        buffers = (psend.at[0, k], pmate.at[k], prem.at[0, k], prem.at[1, k])

        def members(m, rows, lanes):
            return [buffer[rows, lanes].astype(jnp.float32) for buffer in buffers]

        for part in range(CH // 128):
            lanes = slice(128 * part, 128 * (part + 1))
            at = k * CH + 128 * part

            def step(t, _):
                rows = pl.ds(pl.multiple_of(16 * t, 16), 16)
                own, away = [], []
                for m in range(2):
                    place = pl.ds(pl.multiple_of(m * MAIN + 16 * t, 16), 16)
                    four = members(m, place, lanes)
                    own += four[0:2]
                    away += four[2:4]
                scale = wcol[rows, :] * tslot[F : F + 1, at : at + 128]
                grads = crps_rows(own, away, tslot[rows, at : at + 128], scale)
                for m in range(2):
                    g_ref[c, k, m, rows, lanes] = grads[2 * m]
                    gsend[k, m, rows, lanes] = grads[2 * m + 1]
                return 0

            lax.fori_loop(0, MAIN // 16, step, 0)
            tail = members(0, slice(2 * MAIN, ROWS), lanes)
            own, away = [], []
            for m in range(2):
                four = [value[8 * m : 8 * m + 8] for value in tail]
                own += four[0:2]
                away += four[2:4]
            scale = wcol[MAIN:FP, :] * tslot[F : F + 1, at : at + 128]
            grads = crps_rows(own, away, tslot[MAIN:FP, at : at + 128], scale)
            none = jnp.zeros((8, 128), jnp.float32)
            for m in range(2):
                for n, out in ((0, g_ref.at[c, k, m]), (1, gsend.at[k, m])):
                    full = jnp.concatenate([grads[2 * m + n].astype(jnp.float32), none], axis=0)
                    out[MAIN:FB, lanes] = full.astype(jnp.bfloat16)

    ones = jnp.ones((8, CH), jnp.bfloat16)

    def accumulate(e, k):
        for m in range(2):
            grad = g_ref[halves[e], k, m]
            acc[...] += jnp.dot(grad, lat[e, k, m], preferred_element_type=jnp.float32)
            brow[:, 0:FB] += lax.dot_general(
                ones, grad, (((1,), (1,)), ((), ())), preferred_element_type=jnp.float32
            )

    for k in range(NK):
        mate_copy(k).wait_recv()
        far_copy(0, k).wait_recv()
        far_copy(1, k).wait_recv()
        crps_chunk(k)
        grad_copy(k).start()
        accumulate(0, k)
        if k > 0:
            grad_copy(k - 1).wait_recv()
            accumulate(1, k - 1)
    grad_copy(NK - 1).wait_recv()
    accumulate(1, NK - 1)

    def tile_value(h, o):
        t, lb = o // 4, 4 * h + o % 4
        value = acc[8 * t : 8 * t + 8, 128 * lb : 128 * lb + 128]
        if t == 12 and lb == 0:
            at = lax.broadcasted_iota(jnp.int32, (8, 128), 0)
            value = value + jnp.where(at == F - MAIN, brow[...], 0.0)
        return value

    for h in range(2):
        for o in range(OWN):
            wt[h, o] = tile_value(h, o)
    pair = pltpu.make_async_remote_copy(
        src_ref=wt.at[1 - c], dst_ref=wc, send_sem=core_s.at[0], recv_sem=core_r.at[0],
        device_id=mate, device_id_type=MESH,
    )
    pair.start()
    pair.wait()
    wc[...] += wt[c]

    def owner_rank(q_xh, q_pts):
        x = q_xh * 2 + lax.div(q_pts, 16)
        y = lax.rem(lax.div(q_pts, 4), 4)
        z = lax.rem(q_pts, 4)
        owns = jnp.logical_or(z < 3, x == y)
        rank = z * 16 + x + jnp.where(z < 3, y * 4, 0)
        return owns, rank

    owns, rank = owner_rank(xh, pts)

    def scatter(n, _):
        q, q_xh, q_pts, device = group_device(n)
        q_owns, q_rank = owner_rank(q_xh, q_pts)

        @pl.when(q_owns)
        def _():
            pltpu.make_async_remote_copy(
                src_ref=wc.at[q_rank], dst_ref=rs.at[me], send_sem=ar_s.at[0],
                recv_sem=ar_r.at[0], device_id=device, device_id_type=MESH,
            ).start()

        return 0

    lax.fori_loop(1, GROUP, scatter, 0)

    def tiles(ref, count, sem):
        return pltpu.make_async_copy(ref.at[pl.ds(0, count)], ref.at[pl.ds(0, count)], sem)

    @pl.when(owns)
    def _():
        rs[me] = wc[rank]
        tiles(rs, GROUP - 1, ar_r.at[0]).wait()
        ag[c, rank] = jnp.sum(rs[...], axis=0)

        def gather(n, _):
            pltpu.make_async_remote_copy(
                src_ref=ag.at[c, rank], dst_ref=ag.at[c, rank], send_sem=ar_s.at[1],
                recv_sem=ar_r.at[1], device_id=group_device(n)[3], device_id_type=MESH,
            ).start()
            return 0

        lax.fori_loop(1, GROUP, gather, 0)
        tiles(wc, OWN - 1, ar_s.at[0]).wait()
        tiles(wc, OWN - 1, ar_r.at[1]).wait()
        tiles(rs, GROUP - 1, ar_s.at[1]).wait()

    @pl.when(jnp.logical_not(owns))
    def _():
        tiles(wc, OWN, ar_s.at[0]).wait()
        tiles(wc, OWN, ar_r.at[1]).wait()

    back = pltpu.make_async_remote_copy(
        src_ref=ag.at[c], dst_ref=ag.at[c], send_sem=core_s.at[1], recv_sem=core_r.at[1],
        device_id=mate, device_id_type=MESH,
    )
    back.start()
    for k in range(NK):
        far_copy(0, k).wait_send()
        far_copy(1, k).wait_send()
        mate_copy(k).wait_send()
        grad_copy(k).wait_send()
    asked_bytes(ask_s).wait()
    rq_bytes(tq_s).wait()
    back.wait()
    for h in range(2):
        for o in range(OWN):
            t, lb = o // 4, 4 * h + o % 4
            ws_ref[8 * t : 8 * t + 8, 128 * lb : 128 * lb + 128] = ag[h, o]


def latent_kernel(g_ref, w_ref, ws_ref, lg_ref, wg_ref, bg_ref, wpad):
    first = jnp.logical_and(pl.program_id(0) == 0, pl.program_id(1) == 0)
    norm = float(M * SLOTS * PTS) ** (-0.5)

    @pl.when(first)
    def _():
        wpad[...] = jnp.zeros_like(wpad)
        wpad[0:F, :] = w_ref[...]
        wg_ref[...] = ws_ref[0:F, :] * norm
        bg_ref[...] = ws_ref[F : F + 1, 0:F] * norm

    for part in range(2):
        lg_ref[0, part * CH : (part + 1) * CH, :] = lax.dot_general(
            g_ref[0, part, 0], wpad[...], (((0,), (0,)), ((), ())),
            preferred_element_type=jnp.float32,
        ).astype(jnp.bfloat16)


def per_device(latent, head_weight, head_bias, targets, cell_area, field_level, source):
    vmem = pl.BlockSpec(memory_space=pltpu.VMEM)
    hbm = pl.BlockSpec(memory_space=pl.ANY)
    bf16, f32 = jnp.bfloat16, jnp.float32
    dma = pltpu.SemaphoreType.DMA
    grads, sums = pl.pallas_call(
        main_kernel,
        out_shape=(
            jax.ShapeDtypeStruct((2, NK, 2, FB, CH), bf16),
            jax.ShapeDtypeStruct((FP, L), f32),
        ),
        in_specs=[hbm, vmem, vmem, vmem, hbm, vmem, vmem],
        out_specs=(vmem, vmem),
        scratch_shapes=[
            pltpu.VMEM((2, NK, 2, CH, L), bf16),
            pltpu.VMEM((FB, L), bf16),
            pltpu.VMEM((F, SLOTS), f32),
            pltpu.VMEM((256, SLOTS), bf16),
            pltpu.VMEM((8, SLOTS), f32),
            pltpu.VMEM((PTS, 8, 128), jnp.int32),
            pltpu.VMEM((8, 4, 4, 8, 128), f32),
            pltpu.VMEM((4, PTS, 8, 128), f32),
            pltpu.VMEM((FP, HALF), f32),
            pltpu.VMEM((FP, 128), f32),
            pltpu.VMEM((FP, 128), f32),
            pltpu.VMEM((2, NK, ROWS, CH), bf16),
            pltpu.VMEM((NK, ROWS, CH), bf16),
            pltpu.VMEM((2, NK, ROWS, CH), bf16),
            pltpu.VMEM((NK, 2, FB, CH), bf16),
            pltpu.VMEM((FB, L), f32),
            pltpu.VMEM((8, 128), f32),
            pltpu.VMEM((2, OWN, 8, 128), f32),
            pltpu.VMEM((OWN, 8, 128), f32),
            pltpu.VMEM((GROUP, 8, 128), f32),
            pltpu.VMEM((2, OWN, 8, 128), f32),
            dma((2 * NK,)),
            dma,
            dma, dma, dma, dma,
            dma((2 * NK,)), dma((2 * NK,)),
            dma((NK,)), dma((NK,)),
            dma((NK,)), dma((NK,)),
            dma((2,)), dma((2,)),
            dma((2,)), dma((2,)),
        ],
        compiler_params=pltpu.CompilerParams(
            collective_id=0, has_side_effects=True, vmem_limit_bytes=48 * 2**20
        ),
    )(
        latent, head_weight, head_bias.reshape(1, F), field_level.reshape(1, F), targets,
        cell_area.reshape(1, SLOTS), source.reshape(16, 128),
    )
    per = SLOTS // (2 * CH)
    latent_grad, weight_grad, bias_grad = pl.pallas_call(
        latent_kernel,
        grid=(2, per),
        in_specs=[
            pl.BlockSpec((1, 2, 1, FB, CH), lambda m, s: (s // 2, s % 2, m, 0, 0)),
            pl.BlockSpec((F, L), lambda m, s: (0, 0)),
            pl.BlockSpec((FP, L), lambda m, s: (0, 0)),
        ],
        out_specs=(
            pl.BlockSpec((1, 2 * CH, L), lambda m, s: (m, s, 0)),
            pl.BlockSpec((F, L), lambda m, s: (0, 0)),
            pl.BlockSpec((1, F), lambda m, s: (0, 0)),
        ),
        out_shape=(
            jax.ShapeDtypeStruct((2, SLOTS, L), bf16),
            jax.ShapeDtypeStruct((F, L), f32),
            jax.ShapeDtypeStruct((1, F), f32),
        ),
        scratch_shapes=[pltpu.VMEM((FB, L), bf16)],
        compiler_params=pltpu.CompilerParams(vmem_limit_bytes=32 * 2**20),
    )(grads, head_weight, sums)
    return latent_grad, weight_grad, bias_grad.reshape(F)


def solution(mesh):
    return jax.shard_map(
        per_device,
        mesh=mesh,
        in_specs=(P("mem", "pts", None), P(), P(), P(None, "pts"), P("pts"), P(), P("pts")),
        out_specs=(P("mem", "pts", None), P(), P()),
        check_vma=False,
    )
```

```python
import jax
import jax.numpy as jnp
from jax import lax
from jax.experimental import pallas as pl
from jax.experimental.pallas import tpu as pltpu
from jax.sharding import PartitionSpec as P

M = 8
F = 102
L = 1024
FP = 104
FB = 112
MAIN = 96
SLOTS = 2048
HALF = 1024
CH = 256
NK = HALF // CH
ROWS = 208
PTS = 32
GROUP = 64
TILE = 16
TILES = (FB // TILE) * (L // 128)
CHIPS = 64
VMEM = 57_000_000
MESH = pl.DeviceIdType.MESH

FAIR_ALPHA = 0.95
SMOOTH_WIDTH = 0.25
SPREAD = (1.0 - (1.0 - FAIR_ALPHA) / M) / (M - 1)


def smooth_sign(diff):
    return diff * lax.rsqrt(diff * diff + SMOOTH_WIDTH * SMOOTH_WIDTH)


def crps_rows(own, far, target, scale):
    spread = [None] * len(own)

    def add(at, term):
        spread[at] = term if spread[at] is None else spread[at] + term

    for a in range(len(own)):
        for b in range(a + 1, len(own)):
            q = smooth_sign(own[a] - own[b])
            add(a, q)
            add(b, -q)
        for other in far:
            add(a, smooth_sign(own[a] - other))
    return [
        (scale * (smooth_sign(own[a] - target) - SPREAD * spread[a])).astype(jnp.bfloat16)
        for a in range(len(own))
    ]


def column(row, rows):
    n = row.shape[1]
    at = lax.broadcasted_iota(jnp.int32, (rows, n), 0)
    lane = lax.broadcasted_iota(jnp.int32, (rows, n), 1)
    return jnp.sum(jnp.where(at == lane, row, 0.0), axis=1, keepdims=True)


def main_kernel(
    latent, w_hbm, bias_hbm, level_hbm, tgt, area_hbm, src_hbm,
    g_out, ag,
    lat, w_ref, bias_ref, level_ref, area_ref, src_ref,
    wpad, tv, tt, last8, asked, tq, rq, tslot, bcol, wcol,
    psend, pmate, prem, g_ref, gsend, acc, brow, rs, sent,
    lat_sem, small_sem, tgt_sem, ask_s, ask_r, tq_s, tq_r,
    ps_far, pr_far, ps_mate, pr_mate, gs, gr, go, ar_s, ar_r,
):
    i = lax.axis_index("mem")
    pts = lax.axis_index("pts")
    xh = lax.div(i, 2)
    c = lax.rem(i, 2)
    xl = lax.div(pts, 16)
    me = xh * PTS + pts
    mate = (xh * 2 + (1 - c), pts)
    far = ((1 - xh) * 2 + c, pts)
    far_mate = ((1 - xh) * 2 + (1 - c), pts)
    halves = (c, 1 - c)

    def lat_copy(e, k):
        off = pl.multiple_of(halves[e] * HALF + k * CH, CH)
        return pltpu.make_async_copy(
            latent.at[:, pl.ds(off, CH)], lat.at[e, k], lat_sem.at[e * NK + k]
        )

    small = [
        pltpu.make_async_copy(src, dst, small_sem.at[n])
        for n, (src, dst) in enumerate(
            (
                (w_hbm, w_ref), (bias_hbm, bias_ref), (level_hbm, level_ref),
                (area_hbm, area_ref), (src_hbm, src_ref),
            )
        )
    ]
    tgt_copy = pltpu.make_async_copy(tgt, tv, tgt_sem)
    for copy in small:
        copy.start()
    for k in range(NK):
        for e in range(2):
            lat_copy(e, k).start()
        if k == 0:
            tgt_copy.start()

    barrier = pltpu.get_barrier_semaphore()

    def group_device(n):
        q = lax.rem(me + n, GROUP)
        q_xh = lax.div(q, PTS)
        q_pts = lax.rem(q, PTS)
        return q, q_xh, q_pts, (q_xh * 2 + c, q_pts)

    pl.semaphore_signal(barrier, inc=1, device_id=far_mate, device_id_type=MESH)
    pl.semaphore_signal(barrier, inc=1, device_id=mate, device_id_type=MESH)

    def greet(n, _):
        pl.semaphore_signal(barrier, inc=1, device_id=group_device(n)[3], device_id_type=MESH)
        return 0

    lax.fori_loop(1, GROUP, greet, 0)

    for copy in small:
        copy.wait()
    wpad[...] = jnp.zeros_like(wpad)
    wpad[0:F, :] = w_ref[...]
    bcol[...] = jnp.broadcast_to(column(bias_ref[...].astype(jnp.float32), FP), bcol.shape)
    level = (level_ref[...].astype(jnp.float32) + 1.0) / 7.0
    wcol[...] = jnp.broadcast_to(column(level, FP), wcol.shape)
    acc[...] = jnp.zeros_like(acc)
    brow[...] = jnp.zeros_like(brow)

    def far_copy(e, k):
        return pltpu.make_async_remote_copy(
            src_ref=psend.at[e, k],
            dst_ref=prem.at[e, k],
            send_sem=ps_far.at[e * NK + k],
            recv_sem=pr_far.at[e * NK + k],
            device_id=far if e == 0 else far_mate,
            device_id_type=MESH,
        )

    def mate_copy(k):
        return pltpu.make_async_remote_copy(
            src_ref=psend.at[1, k],
            dst_ref=pmate.at[k],
            send_sem=ps_mate.at[k],
            recv_sem=pr_mate.at[k],
            device_id=mate,
            device_id_type=MESH,
        )

    def predict(e, k):
        lat_copy(e, k).wait()
        rest = []
        for m in range(2):
            pred = lax.dot_general(
                wpad[...], lat[e, k, m], (((1,), (1,)), ((), ())),
                preferred_element_type=jnp.float32,
            )[0:FP]
            pred = pred + bcol[:, 0:1]
            psend[e, k, m * MAIN : (m + 1) * MAIN, :] = pred[0:MAIN].astype(jnp.bfloat16)
            rest.append(pred[MAIN:FP])
        psend[e, k, 2 * MAIN :, :] = jnp.concatenate(rest, axis=0).astype(jnp.bfloat16)

    def send(e, k):
        far_copy(e, k).start()
        if e == 1:
            mate_copy(k).start()

    for e in range(2):
        predict(e, 0)

    tgt_copy.wait()
    tt[FP:128, :] = jnp.zeros((128 - FP, SLOTS), jnp.bfloat16)
    tt[128 + FP :, :] = jnp.zeros((128 - FP, SLOTS), jnp.bfloat16)
    last8[...] = jnp.zeros_like(last8)
    last8[0 : F - MAIN, :] = tv[MAIN:F, :]
    last8[F - MAIN : F - MAIN + 1, :] = area_ref[...]

    def split(value, at):
        high = value.astype(jnp.bfloat16)
        tt[at : at + value.shape[0], :] = high
        low = (value - high.astype(jnp.float32)).astype(jnp.bfloat16)
        tt[128 + at : 128 + at + value.shape[0], :] = low

    for at in range(0, MAIN, 32):
        split(tv[at : at + 32, :], at)
    split(last8[...], MAIN)

    pl.semaphore_wait(barrier, GROUP + 1)
    for e in range(2):
        send(e, 0)

    def owner_of(n):
        p = lax.rem(pts + n, PTS)
        differ = lax.rem(lax.div(p, 16) + xl, 2)
        return p, (lax.rem(xh + c * differ, 2) * 2 + c, p)

    def ask(n, _):
        pltpu.make_async_remote_copy(
            src_ref=src_ref.at[pl.ds(pl.multiple_of(8 * c, 8), 8)],
            dst_ref=asked.at[pts],
            send_sem=ask_s,
            recv_sem=ask_r,
            device_id=owner_of(n)[1],
            device_id_type=MESH,
        ).start()
        return 0

    lax.fori_loop(1, PTS, ask, 0)
    asked[pts] = src_ref[pl.ds(pl.multiple_of(8 * c, 8), 8), :]

    for k in range(1, NK):
        for e in range(2):
            predict(e, k)
            send(e, k)

    def asked_bytes(sem):
        return pltpu.make_async_copy(
            asked.at[pl.ds(0, PTS - 1)], asked.at[pl.ds(0, PTS - 1)], sem
        )

    asked_bytes(ask_r).wait()
    found = asked[...].reshape(PTS * 8, 128) - pts * SLOTS
    lane = lax.broadcasted_iota(jnp.int32, (PTS * 8, 128), 1)
    row = lax.broadcasted_iota(jnp.int32, (PTS * 8, 128), 0)
    found = jnp.where(lax.rem(lane, 32) == pts, found, 0)
    spread_row = lax.broadcasted_iota(jnp.int32, (128, 128), 0)
    spread_lane = lax.broadcasted_iota(jnp.int32, (128, 128), 1)
    spread = jnp.where(lax.div(spread_row, 32) == lax.div(spread_lane, 32), 1.0, 0.0)
    spread = spread.astype(jnp.bfloat16)
    high = lax.shift_right_logical(found, 6).astype(jnp.float32).astype(jnp.bfloat16)
    low = lax.bitwise_and(found, 63).astype(jnp.float32).astype(jnp.bfloat16)
    wide = 64.0 * jnp.dot(high, spread, preferred_element_type=jnp.float32) + jnp.dot(
        low, spread, preferred_element_type=jnp.float32
    )
    wide = jnp.where(lax.rem(lane, 32) == lax.rem(row, 32), wide, 0.0)
    wanted = jnp.sum(wide.reshape(8, 32, 128), axis=1)
    for half in range(4):
        cols = jnp.concatenate(
            [column(wanted[2 * half + b : 2 * half + b + 1, :], 128) for b in range(2)], axis=0
        ).astype(jnp.int32)
        place = lax.broadcasted_iota(jnp.int32, (256, SLOTS), 1)
        onehot = jnp.where(place == cols, 1.0, 0.0).astype(jnp.bfloat16)
        got = lax.dot_general(
            onehot, tt[...], (((1,), (1,)), ((), ())), preferred_element_type=jnp.float32
        )
        got = got[:, 0:128] + got[:, 128:256]
        tq[2 * half : 2 * half + 2] = got.reshape(2, 4, 4, 8, 128)

    def answer(n, _):
        p, device = owner_of(n)
        pltpu.make_async_remote_copy(
            src_ref=tq.at[lax.div(p, 4), :, lax.rem(p, 4)],
            dst_ref=rq.at[:, pts],
            send_sem=tq_s,
            recv_sem=tq_r,
            device_id=device,
            device_id_type=MESH,
        ).start()
        return 0

    lax.fori_loop(1, PTS, answer, 0)
    rq[:, pts] = tq[lax.div(pts, 4), :, lax.rem(pts, 4)]

    def rq_bytes(sem):
        return pltpu.make_async_copy(
            rq.at[:, pl.ds(0, PTS - 1)], rq.at[:, pl.ds(0, PTS - 1)], sem
        )

    rq_bytes(tq_r).wait()
    for r in range(8):
        rows = jnp.concatenate([rq[a, :, r, :] for a in range(4)], axis=0)
        tslot[:, 128 * r : 128 * (r + 1)] = rows.T[0:FP]

    def grad_copy(k):
        return pltpu.make_async_remote_copy(
            src_ref=gsend.at[k],
            dst_ref=g_ref.at[c, k],
            send_sem=gs.at[k],
            recv_sem=gr.at[k],
            device_id=mate,
            device_id_type=MESH,
        )

    def crps_chunk(k):
        buffers = (psend.at[0, k], pmate.at[k], prem.at[0, k], prem.at[1, k])

        def members(m, rows, lanes):
            return [buffer[rows, lanes].astype(jnp.float32) for buffer in buffers]

        for part in range(CH // 128):
            lanes = slice(128 * part, 128 * (part + 1))
            at = k * CH + 128 * part

            def step(t, _):
                rows = pl.ds(pl.multiple_of(16 * t, 16), 16)
                own, away = [], []
                for m in range(2):
                    place = pl.ds(pl.multiple_of(m * MAIN + 16 * t, 16), 16)
                    four = members(m, place, lanes)
                    own += four[0:2]
                    away += four[2:4]
                scale = wcol[rows, :] * tslot[F : F + 1, at : at + 128]
                grads = crps_rows(own, away, tslot[rows, at : at + 128], scale)
                for m in range(2):
                    g_ref[c, k, m, rows, lanes] = grads[2 * m]
                    gsend[k, m, rows, lanes] = grads[2 * m + 1]
                return 0

            lax.fori_loop(0, MAIN // 16, step, 0)
            tail = members(0, slice(2 * MAIN, ROWS), lanes)
            own, away = [], []
            for m in range(2):
                four = [value[8 * m : 8 * m + 8] for value in tail]
                own += four[0:2]
                away += four[2:4]
            scale = wcol[MAIN:FP, :] * tslot[F : F + 1, at : at + 128]
            grads = crps_rows(own, away, tslot[MAIN:FP, at : at + 128], scale)
            none = jnp.zeros((8, 128), jnp.float32)
            for m in range(2):
                for n, out in ((0, g_ref.at[c, k, m]), (1, gsend.at[k, m])):
                    full = jnp.concatenate([grads[2 * m + n].astype(jnp.float32), none], axis=0)
                    out[MAIN:FB, lanes] = full.astype(jnp.bfloat16)

    def keep(e, k):
        return pltpu.make_async_copy(
            g_ref.at[halves[e], k], g_out.at[halves[e], k], go.at[e * NK + k]
        )

    ones = jnp.ones((8, CH), jnp.bfloat16)

    def accumulate(e, k):
        keep(e, k).start()
        for m in range(2):
            grad = g_ref[halves[e], k, m]
            acc[...] += jnp.dot(grad, lat[e, k, m], preferred_element_type=jnp.float32)
            brow[:, 0:FB] += lax.dot_general(
                ones, grad, (((1,), (1,)), ((), ())), preferred_element_type=jnp.float32
            )

    for k in range(NK):
        mate_copy(k).wait_recv()
        far_copy(0, k).wait_recv()
        far_copy(1, k).wait_recv()
        crps_chunk(k)
        grad_copy(k).start()
        accumulate(0, k)
        if k > 0:
            grad_copy(k - 1).wait_recv()
            accumulate(1, k - 1)
    grad_copy(NK - 1).wait_recv()
    accumulate(1, NK - 1)

    at = lax.broadcasted_iota(jnp.int32, (8, 128), 0)
    acc[MAIN:FP, 0:128] += jnp.where(at == F - MAIN, brow[...], 0.0)
    x = xh * 2 + xl
    y = lax.rem(lax.div(pts, 4), 4)
    z = lax.rem(pts, 4)
    chip = z * 16 + y * 4 + x
    slot = chip * 2 + c
    has_tile = chip < TILES
    owns = jnp.logical_and(has_tile, lax.rem(x + y + z, 2) == c)

    def other_chip(n):
        q = lax.rem(chip + 1 + lax.rem(n + 41, CHIPS - 1), CHIPS)
        q_x, q_y, q_z = lax.rem(q, 4), lax.rem(lax.div(q, 4), 4), lax.div(q, 16)
        q_mem, q_pts = lax.div(q_x, 2) * 2, lax.rem(q_x, 2) * 16 + q_y * 4 + q_z
        return q, q_mem, q_pts, lax.rem(q_x + q_y + q_z, 2)

    def acc_tile(q):
        rows = pl.ds(pl.multiple_of(lax.div(q, 8) * TILE, TILE), TILE)
        return rows, pl.ds(pl.multiple_of(lax.rem(q, 8) * 128, 128), 128)

    def give(q, device):
        rows, lanes = acc_tile(q)
        pltpu.make_async_remote_copy(
            src_ref=acc.at[rows, lanes], dst_ref=rs.at[slot], send_sem=ar_s.at[0],
            recv_sem=ar_r.at[0], device_id=device, device_id_type=MESH,
        ).start()

    def scatter(n, _):
        q, q_mem, q_pts, q_core = other_chip(n)

        @pl.when(q < TILES)
        def _():
            give(q, (q_mem + q_core, q_pts))

        return 0

    lax.fori_loop(0, CHIPS - 1, scatter, 0)

    @pl.when(jnp.logical_and(has_tile, jnp.logical_not(owns)))
    def _():
        give(chip, mate)

    def tiles(ref, count, sem):
        return pltpu.make_async_copy(ref.at[pl.ds(0, count)], ref.at[pl.ds(0, count)], sem)

    @pl.when(owns)
    def _():
        rows, lanes = acc_tile(chip)
        rs[slot] = acc[rows, lanes]
        tiles(rs, 2 * CHIPS - 1, ar_r.at[0]).wait()
        ag[chip] = jnp.sum(rs[...], axis=0).astype(jnp.bfloat16)

        def share(device):
            pltpu.make_async_remote_copy(
                src_ref=ag.at[chip], dst_ref=ag.at[chip], send_sem=ar_s.at[1],
                recv_sem=ar_r.at[1], device_id=device, device_id_type=MESH,
            ).start()

        def gather(n, _):
            _, q_mem, q_pts, _ = other_chip(n)
            for core in range(2):
                share((q_mem + core, q_pts))
            return 0

        lax.fori_loop(0, CHIPS - 1, gather, 0)
        share(mate)

    for k in range(NK):
        far_copy(0, k).wait_send()
        far_copy(1, k).wait_send()
        mate_copy(k).wait_send()
        grad_copy(k).wait_send()
        keep(0, k).wait()
        keep(1, k).wait()
    asked_bytes(ask_s).wait()
    rq_bytes(tq_s).wait()

    @pl.when(owns)
    def _():
        tiles(rs, TILES - 1, ar_s.at[0]).wait()
        tiles(ag, TILES - 1, ar_r.at[1]).wait()
        tiles(sent, 2 * CHIPS - 1, ar_s.at[1]).wait()

    @pl.when(jnp.logical_not(owns))
    def _():
        tiles(rs, TILES, ar_s.at[0]).wait()
        tiles(ag, TILES, ar_r.at[1]).wait()


def output_kernel(
    g_hbm, w_hbm, ag_ref, lg_out, wg_ref, bg_ref, g_ref, w_ref, wpad, lg, g_sem, w_sem, out_sem
):
    norm = float(M * SLOTS * PTS) ** (-0.5)
    w_copy = pltpu.make_async_copy(w_hbm, w_ref, w_sem)
    w_copy.start()
    blocks = [(h, k) for h in range(2) for k in range(NK)]
    loads = [
        pltpu.make_async_copy(g_hbm.at[h, k], g_ref.at[h, k], g_sem.at[n])
        for n, (h, k) in enumerate(blocks)
    ]
    for load in loads:
        load.start()
    wpad[...] = jnp.zeros_like(wpad)
    w_copy.wait()
    wpad[0:F, :] = w_ref[...]
    stores = []
    for n, (h, k) in enumerate(blocks):
        loads[n].wait()
        for m in range(2):
            part = pl.ds(h * HALF + k * CH, CH)
            lg[m, part, :] = lax.dot_general(
                g_ref[h, k, m], wpad[...], (((0,), (0,)), ((), ())),
                preferred_element_type=jnp.float32,
            ).astype(jnp.bfloat16)
            store = pltpu.make_async_copy(
                lg.at[m, part], lg_out.at[m, part], out_sem.at[2 * n + m]
            )
            store.start()
            stores.append(store)
    for q in range(TILES):
        t, lb = q // 8, q % 8
        rows = min(F, TILE * (t + 1)) - TILE * t
        tile = ag_ref[q].astype(jnp.float32) * norm
        wg_ref[TILE * t : TILE * t + rows, 128 * lb : 128 * (lb + 1)] = tile[0:rows]
        if t == MAIN // TILE and lb == 0:
            bg_ref[...] = tile[F - MAIN : F - MAIN + 1, 0:F]
    for store in stores:
        store.wait()


def per_device(latent, head_weight, head_bias, targets, cell_area, field_level, source):
    vmem = pl.BlockSpec(memory_space=pltpu.VMEM)
    hbm = pl.BlockSpec(memory_space=pltpu.HBM)
    bf16, f32 = jnp.bfloat16, jnp.float32
    dma = pltpu.SemaphoreType.DMA
    grads, sums = pl.pallas_call(
        main_kernel,
        out_shape=(
            jax.ShapeDtypeStruct((2, NK, 2, FB, CH), bf16),
            jax.ShapeDtypeStruct((TILES, TILE, 128), bf16),
        ),
        in_specs=[hbm] * 7,
        out_specs=(hbm, vmem),
        scratch_shapes=[
            pltpu.VMEM((2, NK, 2, CH, L), bf16),
            pltpu.VMEM((F, L), bf16),
            pltpu.VMEM((1, F), bf16),
            pltpu.VMEM((1, F), jnp.int32),
            pltpu.VMEM((1, SLOTS), f32),
            pltpu.VMEM((16, 128), jnp.int32),
            pltpu.VMEM((FB, L), bf16),
            pltpu.VMEM((F, SLOTS), f32),
            pltpu.VMEM((256, SLOTS), bf16),
            pltpu.VMEM((8, SLOTS), f32),
            pltpu.VMEM((PTS, 8, 128), jnp.int32),
            pltpu.VMEM((8, 4, 4, 8, 128), f32),
            pltpu.VMEM((4, PTS, 8, 128), f32),
            pltpu.VMEM((FP, HALF), f32),
            pltpu.VMEM((FP, 128), f32),
            pltpu.VMEM((FP, 128), f32),
            pltpu.VMEM((2, NK, ROWS, CH), bf16),
            pltpu.VMEM((NK, ROWS, CH), bf16),
            pltpu.VMEM((2, NK, ROWS, CH), bf16),
            pltpu.VMEM((2, NK, 2, FB, CH), bf16),
            pltpu.VMEM((NK, 2, FB, CH), bf16),
            pltpu.VMEM((FB, L), f32),
            pltpu.VMEM((8, 128), f32),
            pltpu.VMEM((2 * CHIPS, TILE, 128), f32),
            pltpu.VMEM((2 * CHIPS, TILE, 128), bf16),
            dma((2 * NK,)),
            dma((5,)),
            dma,
            dma, dma, dma, dma,
            dma((2 * NK,)), dma((2 * NK,)),
            dma((NK,)), dma((NK,)),
            dma((NK,)), dma((NK,)),
            dma((2 * NK,)),
            dma((2,)), dma((2,)),
        ],
        compiler_params=pltpu.CompilerParams(
            collective_id=0, has_side_effects=True, vmem_limit_bytes=VMEM
        ),
    )(
        latent, head_weight, head_bias.reshape(1, F), field_level.reshape(1, F), targets,
        cell_area.reshape(1, SLOTS), source.reshape(16, 128),
    )
    latent_grad, weight_grad, bias_grad = pl.pallas_call(
        output_kernel,
        in_specs=[hbm, hbm, vmem],
        out_specs=(hbm, vmem, vmem),
        out_shape=(
            jax.ShapeDtypeStruct((2, SLOTS, L), bf16),
            jax.ShapeDtypeStruct((F, L), f32),
            jax.ShapeDtypeStruct((1, F), f32),
        ),
        scratch_shapes=[
            pltpu.VMEM((2, NK, 2, FB, CH), bf16),
            pltpu.VMEM((F, L), bf16),
            pltpu.VMEM((FB, L), bf16),
            pltpu.VMEM((2, SLOTS, L), bf16),
            dma((2 * NK,)),
            dma,
            dma((4 * NK,)),
        ],
        compiler_params=pltpu.CompilerParams(vmem_limit_bytes=VMEM),
    )(grads, head_weight, sums)
    return latent_grad, weight_grad, bias_grad.reshape(F)


def solution(mesh):
    return jax.shard_map(
        per_device,
        mesh=mesh,
        in_specs=(P("mem", "pts", None), P(), P(), P(None, "pts"), P("pts"), P(), P("pts")),
        out_specs=(P("mem", "pts", None), P(), P()),
        check_vma=False,
    )
```

```python
import jax
import jax.numpy as jnp
from jax import lax
from jax.experimental import pallas as pl
from jax.experimental.pallas import tpu as pltpu
from jax.sharding import PartitionSpec as P

M = 8
F = 102
L = 1024
FP = 104
FB = 112
MAIN = 96
SLOTS = 2048
HALF = 1024
CH = 256
NK = HALF // CH
ROWS = 208
PTS = 32
GROUP = 64
TILE = 16
WIDE = L // 2
TILES = (FB // TILE) * (WIDE // 128)
CHIPS = 64
VMEM = 57_000_000
ORDER = (0, 2, 1, 3)
MESH = pl.DeviceIdType.MESH

FAIR_ALPHA = 0.95
SMOOTH_WIDTH = 0.25
SPREAD = (1.0 - (1.0 - FAIR_ALPHA) / M) / (M - 1)


def smooth_sign(diff):
    return diff * lax.rsqrt(diff * diff + SMOOTH_WIDTH * SMOOTH_WIDTH)


def crps_rows(own, far, target, scale):
    spread = [None] * len(own)

    def add(at, term):
        spread[at] = term if spread[at] is None else spread[at] + term

    for a in range(len(own)):
        for b in range(a + 1, len(own)):
            q = smooth_sign(own[a] - own[b])
            add(a, q)
            add(b, -q)
        for other in far:
            add(a, smooth_sign(own[a] - other))
    return [
        (scale * (smooth_sign(own[a] - target) - SPREAD * spread[a])).astype(jnp.bfloat16)
        for a in range(len(own))
    ]


def column(row, rows):
    n = row.shape[1]
    at = lax.broadcasted_iota(jnp.int32, (rows, n), 0)
    lane = lax.broadcasted_iota(jnp.int32, (rows, n), 1)
    return jnp.sum(jnp.where(at == lane, row, 0.0), axis=1, keepdims=True)


def main_kernel(
    latent, w_hbm, bias_hbm, level_hbm, tgt, area_hbm, src_hbm,
    g_out, ag,
    lat, w_ref, bias_ref, level_ref, area_ref, src_ref,
    wpad, tv, tt, last8, asked, tq, rq, tslot, bcol, wcol,
    psend, pmate, prem, gl, gx, mlat, acc, bsum, rs, sent,
    lat_sem, small_sem, tgt_sem, ask_s, ask_r, tq_s, tq_r,
    ps_far, pr_far, ps_mate, pr_mate, ms, mr, gs, gr, go, ar_s, ar_r,
):
    i = lax.axis_index("mem")
    pts = lax.axis_index("pts")
    xh = lax.div(i, 2)
    c = lax.rem(i, 2)
    xl = lax.div(pts, 16)
    me = xh * PTS + pts
    mate = (xh * 2 + (1 - c), pts)
    far = ((1 - xh) * 2 + c, pts)
    far_mate = ((1 - xh) * 2 + (1 - c), pts)
    halves = (c, 1 - c)

    def lat_copy(e, k):
        off = pl.multiple_of(halves[e] * HALF + k * CH, CH)
        return pltpu.make_async_copy(
            latent.at[:, pl.ds(off, CH)], lat.at[e, k], lat_sem.at[e * NK + k]
        )

    small = [
        pltpu.make_async_copy(src, dst, small_sem.at[n])
        for n, (src, dst) in enumerate(
            (
                (w_hbm, w_ref), (bias_hbm, bias_ref), (level_hbm, level_ref),
                (area_hbm, area_ref), (src_hbm, src_ref),
            )
        )
    ]
    tgt_copy = pltpu.make_async_copy(tgt, tv, tgt_sem)
    for copy in small:
        copy.start()
    for k in range(NK):
        for e in range(2):
            lat_copy(e, k).start()
        if k == 0:
            tgt_copy.start()

    barrier = pltpu.get_barrier_semaphore()

    def group_device(n):
        q = lax.rem(me + n, GROUP)
        q_xh = lax.div(q, PTS)
        q_pts = lax.rem(q, PTS)
        return q, q_xh, q_pts, (q_xh * 2 + c, q_pts)

    pl.semaphore_signal(barrier, inc=1, device_id=far_mate, device_id_type=MESH)
    pl.semaphore_signal(barrier, inc=1, device_id=mate, device_id_type=MESH)

    def greet(n, _):
        pl.semaphore_signal(barrier, inc=1, device_id=group_device(n)[3], device_id_type=MESH)
        return 0

    lax.fori_loop(1, GROUP, greet, 0)

    for copy in small:
        copy.wait()
    wpad[...] = jnp.zeros_like(wpad)
    wpad[0:F, :] = w_ref[...]
    bcol[...] = jnp.broadcast_to(column(bias_ref[...].astype(jnp.float32), FP), bcol.shape)
    level = (level_ref[...].astype(jnp.float32) + 1.0) / 7.0
    wcol[...] = jnp.broadcast_to(column(level, FP), wcol.shape)
    acc[...] = jnp.zeros_like(acc)
    bsum[...] = jnp.zeros_like(bsum)

    def far_copy(e, k):
        return pltpu.make_async_remote_copy(
            src_ref=psend.at[e, k],
            dst_ref=prem.at[e, k],
            send_sem=ps_far.at[e * NK + k],
            recv_sem=pr_far.at[e * NK + k],
            device_id=far if e == 0 else far_mate,
            device_id_type=MESH,
        )

    def mate_copy(k):
        return pltpu.make_async_remote_copy(
            src_ref=psend.at[1, k],
            dst_ref=pmate.at[k],
            send_sem=ps_mate.at[k],
            recv_sem=pr_mate.at[k],
            device_id=mate,
            device_id_type=MESH,
        )

    def predict(e, k):
        lat_copy(e, k).wait()
        rest = []
        for m in range(2):
            pred = lax.dot_general(
                wpad[...], lat[e, k, m], (((1,), (1,)), ((), ())),
                preferred_element_type=jnp.float32,
            )[0:FP]
            pred = pred + bcol[:, 0:1]
            psend[e, k, m * MAIN : (m + 1) * MAIN, :] = pred[0:MAIN].astype(jnp.bfloat16)
            rest.append(pred[MAIN:FP])
        psend[e, k, 2 * MAIN :, :] = jnp.concatenate(rest, axis=0).astype(jnp.bfloat16)

    def send(e, k):
        far_copy(e, k).start()
        if e == 1:
            mate_copy(k).start()

    for e in range(2):
        predict(e, 0)

    pl.semaphore_wait(barrier, GROUP + 1)
    for e in range(2):
        send(e, 0)

    def owner_of(n):
        p = lax.rem(pts + n, PTS)
        differ = lax.rem(lax.div(p, 16) + xl, 2)
        return p, (lax.rem(xh + c * differ, 2) * 2 + c, p)

    def ask(n, _):
        pltpu.make_async_remote_copy(
            src_ref=src_ref.at[pl.ds(pl.multiple_of(8 * c, 8), 8)],
            dst_ref=asked.at[pts],
            send_sem=ask_s,
            recv_sem=ask_r,
            device_id=owner_of(n)[1],
            device_id_type=MESH,
        ).start()
        return 0

    lax.fori_loop(1, PTS, ask, 0)
    asked[pts] = src_ref[pl.ds(pl.multiple_of(8 * c, 8), 8), :]

    for e in range(2):
        predict(e, 1)
        send(e, 1)

    def lend(e, k):
        lanes = pl.ds(pl.multiple_of((1 - c) * WIDE, WIDE), WIDE)
        return pltpu.make_async_remote_copy(
            src_ref=lat.at[e, k, :, :, lanes],
            dst_ref=mlat.at[1 - e, k],
            send_sem=ms.at[e * NK + k],
            recv_sem=mr.at[(1 - e) * NK + k],
            device_id=mate,
            device_id_type=MESH,
        )

    def lent(e, k):
        return pltpu.make_async_copy(mlat.at[e, k], mlat.at[e, k], mr.at[e * NK + k])

    for e in range(2):
        lend(e, 0).start()

    tgt_copy.wait()
    tt[FP:128, :] = jnp.zeros((128 - FP, SLOTS), jnp.bfloat16)
    tt[128 + FP :, :] = jnp.zeros((128 - FP, SLOTS), jnp.bfloat16)
    last8[...] = jnp.zeros_like(last8)
    last8[0 : F - MAIN, :] = tv[MAIN:F, :]
    last8[F - MAIN : F - MAIN + 1, :] = area_ref[...]

    def split(value, at):
        high = value.astype(jnp.bfloat16)
        tt[at : at + value.shape[0], :] = high
        low = (value - high.astype(jnp.float32)).astype(jnp.bfloat16)
        tt[128 + at : 128 + at + value.shape[0], :] = low

    for at in range(0, MAIN, 32):
        split(tv[at : at + 32, :], at)
    split(last8[...], MAIN)


    def asked_bytes(sem):
        return pltpu.make_async_copy(
            asked.at[pl.ds(0, PTS - 1)], asked.at[pl.ds(0, PTS - 1)], sem
        )

    asked_bytes(ask_r).wait()
    found = asked[...].reshape(PTS * 8, 128) - pts * SLOTS
    lane = lax.broadcasted_iota(jnp.int32, (PTS * 8, 128), 1)
    row = lax.broadcasted_iota(jnp.int32, (PTS * 8, 128), 0)
    found = jnp.where(lax.rem(lane, 32) == pts, found, 0)
    spread_row = lax.broadcasted_iota(jnp.int32, (128, 128), 0)
    spread_lane = lax.broadcasted_iota(jnp.int32, (128, 128), 1)
    spread = jnp.where(lax.div(spread_row, 32) == lax.div(spread_lane, 32), 1.0, 0.0)
    spread = spread.astype(jnp.bfloat16)
    high = lax.shift_right_logical(found, 6).astype(jnp.float32).astype(jnp.bfloat16)
    low = lax.bitwise_and(found, 63).astype(jnp.float32).astype(jnp.bfloat16)
    wide = 64.0 * jnp.dot(high, spread, preferred_element_type=jnp.float32) + jnp.dot(
        low, spread, preferred_element_type=jnp.float32
    )
    wide = jnp.where(lax.rem(lane, 32) == lax.rem(row, 32), wide, 0.0)
    wanted = jnp.sum(wide.reshape(8, 32, 128), axis=1)
    for half in range(4):
        cols = jnp.concatenate(
            [column(wanted[2 * half + b : 2 * half + b + 1, :], 128) for b in range(2)], axis=0
        ).astype(jnp.int32)
        place = lax.broadcasted_iota(jnp.int32, (256, SLOTS), 1)
        onehot = jnp.where(place == cols, 1.0, 0.0).astype(jnp.bfloat16)
        got = lax.dot_general(
            onehot, tt[...], (((1,), (1,)), ((), ())), preferred_element_type=jnp.float32
        )
        got = got[:, 0:128] + got[:, 128:256]
        tq[2 * half : 2 * half + 2] = got.reshape(2, 4, 4, 8, 128)

    def answer(n, _):
        p, device = owner_of(n)
        pltpu.make_async_remote_copy(
            src_ref=tq.at[lax.div(p, 4), :, lax.rem(p, 4)],
            dst_ref=rq.at[:, pts],
            send_sem=tq_s,
            recv_sem=tq_r,
            device_id=device,
            device_id_type=MESH,
        ).start()
        return 0

    lax.fori_loop(1, PTS, answer, 0)
    rq[:, pts] = tq[lax.div(pts, 4), :, lax.rem(pts, 4)]

    for k in range(2, NK):
        for e in range(2):
            predict(e, k)
            send(e, k)
    for k in range(1, NK):
        for e in range(2):
            lend(e, k).start()

    def rq_bytes(sem):
        return pltpu.make_async_copy(
            rq.at[:, pl.ds(0, PTS - 1)], rq.at[:, pl.ds(0, PTS - 1)], sem
        )

    rq_bytes(tq_r).wait()
    for r in range(8):
        rows = jnp.concatenate([rq[a, :, r, :] for a in range(4)], axis=0)
        tslot[:, 128 * r : 128 * (r + 1)] = rows.T[0:FP]

    def grad_copy(k):
        return pltpu.make_async_remote_copy(
            src_ref=gl.at[k],
            dst_ref=gx.at[k],
            send_sem=gs.at[k],
            recv_sem=gr.at[k],
            device_id=mate,
            device_id_type=MESH,
        )

    def crps_chunk(k):
        buffers = (psend.at[0, k], pmate.at[k], prem.at[0, k], prem.at[1, k])

        def members(m, rows, lanes):
            return [buffer[rows, lanes].astype(jnp.float32) for buffer in buffers]

        for part in range(CH // 128):
            lanes = slice(128 * part, 128 * (part + 1))
            at = k * CH + 128 * part

            def step(t, _):
                rows = pl.ds(pl.multiple_of(16 * t, 16), 16)
                own, away = [], []
                for m in range(2):
                    place = pl.ds(pl.multiple_of(m * MAIN + 16 * t, 16), 16)
                    four = members(m, place, lanes)
                    own += four[0:2]
                    away += four[2:4]
                scale = wcol[rows, :] * tslot[F : F + 1, at : at + 128]
                grads = crps_rows(own, away, tslot[rows, at : at + 128], scale)
                for n in range(4):
                    gl[k, ORDER[n], rows, lanes] = grads[n]
                bsum[rows, :] += sum(grad.astype(jnp.float32) for grad in grads)
                return 0

            lax.fori_loop(0, MAIN // 16, step, 0)
            tail = members(0, slice(2 * MAIN, ROWS), lanes)
            own, away = [], []
            for m in range(2):
                four = [value[8 * m : 8 * m + 8] for value in tail]
                own += four[0:2]
                away += four[2:4]
            scale = wcol[MAIN:FP, :] * tslot[F : F + 1, at : at + 128]
            grads = crps_rows(own, away, tslot[MAIN:FP, at : at + 128], scale)
            none = jnp.zeros((8, 128), jnp.float32)
            for n in range(4):
                full = jnp.concatenate([grads[n].astype(jnp.float32), none], axis=0)
                gl[k, ORDER[n], MAIN:FB, lanes] = full.astype(jnp.bfloat16)
            bsum[MAIN:FP, :] += sum(grad.astype(jnp.float32) for grad in grads)

    def keep(e, k):
        own = gl.at[k, 0:2] if e == 0 else gx.at[k, 2:4]
        return pltpu.make_async_copy(own, g_out.at[halves[e], k], go.at[e * NK + k])

    def accumulate(e, k):
        keep(e, k).start()
        lent(e, k).wait()
        lanes = pl.ds(pl.multiple_of(c * WIDE, WIDE), WIDE)
        for m in range(2):
            own, other = (gl[k, m], gl[k, 2 + m]) if e == 0 else (gx[k, 2 + m], gx[k, m])
            acc[...] += jnp.dot(
                own, lat[e, k, m, :, lanes], preferred_element_type=jnp.float32
            ) + jnp.dot(other, mlat[e, k, m], preferred_element_type=jnp.float32)

    for k in range(NK):
        mate_copy(k).wait_recv()
        far_copy(0, k).wait_recv()
        far_copy(1, k).wait_recv()
        crps_chunk(k)
        grad_copy(k).start()
        accumulate(0, k)
        if k > 0:
            grad_copy(k - 1).wait_recv()
            accumulate(1, k - 1)
    grad_copy(NK - 1).wait_recv()
    accumulate(1, NK - 1)

    at = lax.broadcasted_iota(jnp.int32, (FP, 128), 0)
    lane_at = lax.broadcasted_iota(jnp.int32, (FP, 128), 1)
    bias = jnp.sum(bsum[...], axis=1, keepdims=True)
    bias = jnp.sum(jnp.where(at == lane_at, bias, 0.0), axis=0, keepdims=True)
    acc[MAIN:FP, 0:128] += jnp.where(at[0 : FP - MAIN] == F - MAIN, bias, 0.0)
    y = lax.rem(lax.div(pts, 4), 4)
    z = lax.rem(pts, 4)
    x = xh * 2 + xl
    slot = z * 16 + y * 4 + x

    def tile_at(q_xh, q_y, q_z):
        full = lax.div(q_z, 3) * lax.div(q_y, 2) == 0
        return q_z * 8 + q_y * 2 + q_xh, full, lax.rem(c + q_y + q_z, 2)

    tile, full, tile_xl = tile_at(xh, y, z)
    owns = jnp.logical_and(full, tile_xl == xl)

    def acc_tile(q):
        rows = pl.ds(pl.multiple_of(lax.div(q, 4) * TILE, TILE), TILE)
        return rows, pl.ds(pl.multiple_of(lax.rem(q, 4) * 128, 128), 128)

    ys = [lax.rem(y + d, 4) for d in range(4)]
    xs = [lax.rem(x + d, 4) for d in range(4)]
    far_first = (2, 1, 3, 0)

    def scatter(n, _):
        q_z = lax.rem(z + n + 2, 4)
        for dy in far_first:
            for q_xh in (1 - xh, xh):
                q, q_full, q_xl = tile_at(q_xh, ys[dy], q_z)
                there = q_full
                if dy == 0 and q_xh is xh:
                    there = jnp.logical_and(there, jnp.logical_or(n != 2, q_xl != xl))

                @pl.when(there)
                def _(q=q, q_xh=q_xh, q_xl=q_xl, dy=dy):
                    rows, lanes = acc_tile(q)
                    pltpu.make_async_remote_copy(
                        src_ref=acc.at[rows, lanes], dst_ref=rs.at[slot], send_sem=ar_s.at[0],
                        recv_sem=ar_r.at[0],
                        device_id=(q_xh * 2 + c, q_xl * 16 + ys[dy] * 4 + q_z),
                        device_id_type=MESH,
                    ).start()

        return 0

    lax.fori_loop(0, 4, scatter, 0)

    def tiles(ref, count, sem):
        return pltpu.make_async_copy(ref.at[pl.ds(0, count)], ref.at[pl.ds(0, count)], sem)

    @pl.when(owns)
    def _():
        rows, lanes = acc_tile(tile)
        rs[slot] = acc[rows, lanes]
        tiles(rs, CHIPS - 1, ar_r.at[0]).wait()
        mine = c * TILES + tile
        ag[mine] = jnp.sum(rs[...], axis=0).astype(jnp.bfloat16)

        def share(device):
            pltpu.make_async_remote_copy(
                src_ref=ag.at[mine], dst_ref=ag.at[mine], send_sem=ar_s.at[1],
                recv_sem=ar_r.at[1], device_id=device, device_id_type=MESH,
            ).start()

        def gather(n, _):
            q_z = lax.rem(z + n + 2, 4)

            def chip(dy, dx):
                q_mem = lax.div(xs[dx], 2) * 2
                q_pts = lax.rem(xs[dx], 2) * 16 + ys[dy] * 4 + q_z
                for core in range(2):
                    share((q_mem + core, q_pts))

            for dy in far_first:
                for dx in far_first:
                    if dy == 0 and dx == 0:
                        pl.when(n != 2)(lambda: chip(0, 0))
                    else:
                        chip(dy, dx)
            return 0

        lax.fori_loop(0, 4, gather, 0)
        share(mate)

    for k in range(NK):
        for e in range(2):
            far_copy(e, k).wait_send()
            lend(e, k).wait_send()
            keep(e, k).wait()
        mate_copy(k).wait_send()
        grad_copy(k).wait_send()
    asked_bytes(ask_s).wait()
    rq_bytes(tq_s).wait()

    @pl.when(owns)
    def _():
        tiles(rs, TILES - 1, ar_s.at[0]).wait()
        tiles(ag, 2 * TILES - 1, ar_r.at[1]).wait()
        tiles(sent, 2 * CHIPS - 1, ar_s.at[1]).wait()

    @pl.when(jnp.logical_not(owns))
    def _():
        tiles(rs, TILES, ar_s.at[0]).wait()
        tiles(ag, 2 * TILES, ar_r.at[1]).wait()


def output_kernel(
    g_hbm, w_hbm, ag_hbm, lg_out, wg_out, bg_out,
    g_ref, w_ref, ag_ref, wpad, lg, wg, bg, g_sem, small_sem, out_sem,
):
    norm = float(M * SLOTS * PTS) ** (-0.5)
    w_copy = pltpu.make_async_copy(w_hbm, w_ref, small_sem.at[0])
    w_copy.start()
    ag_copy = pltpu.make_async_copy(ag_hbm, ag_ref, small_sem.at[1])
    blocks = [(h, k) for h in range(2) for k in range(NK)]
    loads = [
        pltpu.make_async_copy(g_hbm.at[h, k], g_ref.at[h, k], g_sem.at[n])
        for n, (h, k) in enumerate(blocks)
    ]
    for load in loads:
        load.start()
    ag_copy.start()
    wpad[...] = jnp.zeros_like(wpad)
    w_copy.wait()
    wpad[0:F, :] = w_ref[...]
    stores = []
    for n, (h, k) in enumerate(blocks):
        loads[n].wait()
        for m in range(2):
            part = pl.ds(h * HALF + k * CH, CH)
            lg[m, part, :] = lax.dot_general(
                g_ref[h, k, m], wpad[...], (((0,), (0,)), ((), ())),
                preferred_element_type=jnp.float32,
            ).astype(jnp.bfloat16)
            store = pltpu.make_async_copy(
                lg.at[m, part], lg_out.at[m, part], out_sem.at[2 * n + m]
            )
            store.start()
            stores.append(store)
        if n == 1:
            ag_copy.wait()
            for q in range(2 * TILES):
                t, lb = q % TILES // 4, q // TILES * 4 + q % 4
                rows = min(F, TILE * (t + 1)) - TILE * t
                tile = ag_ref[q].astype(jnp.float32) * norm
                wg[TILE * t : TILE * t + rows, 128 * lb : 128 * (lb + 1)] = tile[0:rows]
            last = MAIN // TILE * 4
            pair = ag_ref[last].astype(jnp.float32) + ag_ref[TILES + last].astype(jnp.float32)
            bg[...] = pair[F - MAIN : F - MAIN + 1, 0:F] * norm
            for src, dst in ((wg, wg_out), (bg, bg_out)):
                store = pltpu.make_async_copy(src, dst, out_sem.at[4 * NK + (src is bg)])
                store.start()
                stores.append(store)
    for store in stores:
        store.wait()


def per_device(latent, head_weight, head_bias, targets, cell_area, field_level, source):
    vmem = pl.BlockSpec(memory_space=pltpu.VMEM)
    hbm = pl.BlockSpec(memory_space=pltpu.HBM)
    bf16, f32 = jnp.bfloat16, jnp.float32
    dma = pltpu.SemaphoreType.DMA
    grads, sums = pl.pallas_call(
        main_kernel,
        out_shape=(
            jax.ShapeDtypeStruct((2, NK, 2, FB, CH), bf16),
            jax.ShapeDtypeStruct((2 * TILES, TILE, 128), bf16),
        ),
        in_specs=[hbm] * 7,
        out_specs=(hbm, vmem),
        scratch_shapes=[
            pltpu.VMEM((2, NK, 2, CH, L), bf16),
            pltpu.VMEM((F, L), bf16),
            pltpu.VMEM((1, F), bf16),
            pltpu.VMEM((1, F), jnp.int32),
            pltpu.VMEM((1, SLOTS), f32),
            pltpu.VMEM((16, 128), jnp.int32),
            pltpu.VMEM((FB, L), bf16),
            pltpu.VMEM((F, SLOTS), f32),
            pltpu.VMEM((256, SLOTS), bf16),
            pltpu.VMEM((8, SLOTS), f32),
            pltpu.VMEM((PTS, 8, 128), jnp.int32),
            pltpu.VMEM((8, 4, 4, 8, 128), f32),
            pltpu.VMEM((4, PTS, 8, 128), f32),
            pltpu.VMEM((FP, HALF), f32),
            pltpu.VMEM((FP, 128), f32),
            pltpu.VMEM((FP, 128), f32),
            pltpu.VMEM((2, NK, ROWS, CH), bf16),
            pltpu.VMEM((NK, ROWS, CH), bf16),
            pltpu.VMEM((2, NK, ROWS, CH), bf16),
            pltpu.VMEM((NK, 4, FB, CH), bf16),
            pltpu.VMEM((NK, 4, FB, CH), bf16),
            pltpu.VMEM((2, NK, 2, CH, WIDE), bf16),
            pltpu.VMEM((FB, WIDE), f32),
            pltpu.VMEM((FP, 128), f32),
            pltpu.VMEM((CHIPS, TILE, 128), f32),
            pltpu.VMEM((2 * CHIPS, TILE, 128), bf16),
            dma((2 * NK,)),
            dma((5,)),
            dma,
            dma, dma, dma, dma,
            dma((2 * NK,)), dma((2 * NK,)),
            dma((NK,)), dma((NK,)),
            dma((2 * NK,)), dma((2 * NK,)),
            dma((NK,)), dma((NK,)),
            dma((2 * NK,)),
            dma((2,)), dma((2,)),
        ],
        compiler_params=pltpu.CompilerParams(
            collective_id=0, has_side_effects=True, vmem_limit_bytes=VMEM
        ),
    )(
        latent, head_weight, head_bias.reshape(1, F), field_level.reshape(1, F), targets,
        cell_area.reshape(1, SLOTS), source.reshape(16, 128),
    )
    latent_grad, weight_grad, bias_grad = pl.pallas_call(
        output_kernel,
        in_specs=[hbm] * 3,
        out_specs=(hbm, hbm, hbm),
        out_shape=(
            jax.ShapeDtypeStruct((2, SLOTS, L), bf16),
            jax.ShapeDtypeStruct((F, L), f32),
            jax.ShapeDtypeStruct((1, F), f32),
        ),
        scratch_shapes=[
            pltpu.VMEM((2, NK, 2, FB, CH), bf16),
            pltpu.VMEM((F, L), bf16),
            pltpu.VMEM((2 * TILES, TILE, 128), bf16),
            pltpu.VMEM((FB, L), bf16),
            pltpu.VMEM((2, SLOTS, L), bf16),
            pltpu.VMEM((F, L), f32),
            pltpu.VMEM((1, F), f32),
            dma((2 * NK,)),
            dma((2,)),
            dma((4 * NK + 2,)),
        ],
        compiler_params=pltpu.CompilerParams(vmem_limit_bytes=VMEM),
    )(grads, head_weight, sums)
    return latent_grad, weight_grad, bias_grad.reshape(F)


def solution(mesh):
    return jax.shard_map(
        per_device,
        mesh=mesh,
        in_specs=(P("mem", "pts", None), P(), P(), P(None, "pts"), P("pts"), P(), P("pts")),
        out_specs=(P("mem", "pts", None), P(), P()),
        check_vma=False,
    )
```

```python
import jax
import jax.numpy as jnp
from jax import lax
from jax.experimental import pallas as pl
from jax.experimental.pallas import tpu as pltpu
from jax.sharding import PartitionSpec as P

M = 8
F = 102
L = 1024
FP = 104
FB = 112
MAIN = 96
SLOTS = 2048
HALF = 1024
CH = 256
NK = HALF // CH
ROWS = 208
PTS = 32
GROUP = 64
TILE = 16
WIDE = L // 2
TILES = (FB // TILE) * (WIDE // 128)
CHIPS = 64
VMEM = 40 * 2**20
EARLY = 2
ORDER = (0, 2, 1, 3)
MESH = pl.DeviceIdType.MESH

FAIR_ALPHA = 0.95
SMOOTH_WIDTH = 0.25
SPREAD = (1.0 - (1.0 - FAIR_ALPHA) / M) / (M - 1)


def smooth_sign(diff):
    return diff * lax.rsqrt(diff * diff + SMOOTH_WIDTH * SMOOTH_WIDTH)


def pair_sums(own, far):
    spread = [None] * len(own)

    def add(at, term):
        spread[at] = term if spread[at] is None else spread[at] + term

    for a in range(len(own)):
        for b in range(a + 1, len(own)):
            q = smooth_sign(own[a] - own[b])
            add(a, q)
            add(b, -q)
        for other in far:
            add(a, smooth_sign(own[a] - other))
    return spread


def gradients(own, spread, target, scale):
    return [
        (scale * (smooth_sign(value - target) - SPREAD * others)).astype(jnp.bfloat16)
        for value, others in zip(own, spread, strict=True)
    ]


def column(row, rows):
    n = row.shape[1]
    at = lax.broadcasted_iota(jnp.int32, (rows, n), 0)
    lane = lax.broadcasted_iota(jnp.int32, (rows, n), 1)
    return jnp.sum(jnp.where(at == lane, row, 0.0), axis=1, keepdims=True)


def main_kernel(
    latent, w_hbm, bias_hbm, level_hbm, tgt, area_hbm, src_hbm,
    lg, ag,
    lat, w_ref, bias_ref, level_ref, area_ref, src_ref,
    wpad, tv, tt, last8, asked, tq, rq, tslot, bcol, wcol,
    psend, pmate, prem, gl, gx, mlat, acc, bsum, rs, sent, sp,
    lat_sem, small_sem, tgt_sem, ask_s, ask_r, tq_s, tq_r,
    ps_far, pr_far, ps_mate, pr_mate, ms, mr, gs, gr, ar_s, ar_r,
):
    i = lax.axis_index("mem")
    pts = lax.axis_index("pts")
    xh = lax.div(i, 2)
    c = lax.rem(i, 2)
    xl = lax.div(pts, 16)
    me = xh * PTS + pts
    mate = (xh * 2 + (1 - c), pts)
    far = ((1 - xh) * 2 + c, pts)
    far_mate = ((1 - xh) * 2 + (1 - c), pts)
    halves = (c, 1 - c)

    def lat_copy(e, k):
        off = pl.multiple_of(halves[e] * HALF + k * CH, CH)
        return pltpu.make_async_copy(
            latent.at[:, pl.ds(off, CH)], lat.at[e, k], lat_sem.at[e * NK + k]
        )

    small = [
        pltpu.make_async_copy(src, dst, small_sem.at[n])
        for n, (src, dst) in enumerate(
            (
                (w_hbm, w_ref), (bias_hbm, bias_ref), (level_hbm, level_ref),
                (area_hbm, area_ref), (src_hbm, src_ref),
            )
        )
    ]
    tgt_copy = pltpu.make_async_copy(tgt, tv, tgt_sem)
    for copy in small:
        copy.start()
    for k in range(NK):
        for e in range(2):
            lat_copy(e, k).start()
        if k == 0:
            tgt_copy.start()

    barrier = pltpu.get_barrier_semaphore()

    def group_device(n):
        q = lax.rem(me + n, GROUP)
        q_xh = lax.div(q, PTS)
        q_pts = lax.rem(q, PTS)
        return q, q_xh, q_pts, (q_xh * 2 + c, q_pts)

    pl.semaphore_signal(barrier, inc=1, device_id=far_mate, device_id_type=MESH)
    pl.semaphore_signal(barrier, inc=1, device_id=mate, device_id_type=MESH)

    def greet(n, _):
        pl.semaphore_signal(barrier, inc=1, device_id=group_device(n)[3], device_id_type=MESH)
        return 0

    lax.fori_loop(1, GROUP, greet, 0)

    for copy in small:
        copy.wait()
    wpad[...] = jnp.zeros_like(wpad)
    wpad[0:F, :] = w_ref[...]
    bcol[...] = jnp.broadcast_to(column(bias_ref[...].astype(jnp.float32), FP), bcol.shape)
    level = (level_ref[...].astype(jnp.float32) + 1.0) / 7.0
    wcol[...] = jnp.broadcast_to(column(level, FP), wcol.shape)
    acc[...] = jnp.zeros_like(acc)
    bsum[...] = jnp.zeros_like(bsum)

    def far_copy(e, k):
        return pltpu.make_async_remote_copy(
            src_ref=psend.at[e, k],
            dst_ref=prem.at[e, k],
            send_sem=ps_far.at[e * NK + k],
            recv_sem=pr_far.at[e * NK + k],
            device_id=far if e == 0 else far_mate,
            device_id_type=MESH,
        )

    def mate_copy(k):
        return pltpu.make_async_remote_copy(
            src_ref=psend.at[1, k],
            dst_ref=pmate.at[k],
            send_sem=ps_mate.at[k],
            recv_sem=pr_mate.at[k],
            device_id=mate,
            device_id_type=MESH,
        )

    def predict(e, k):
        lat_copy(e, k).wait()
        rest = []
        for m in range(2):
            pred = lax.dot_general(
                wpad[...], lat[e, k, m], (((1,), (1,)), ((), ())),
                preferred_element_type=jnp.float32,
            )[0:FP]
            pred = pred + bcol[:, 0:1]
            psend[e, k, m * MAIN : (m + 1) * MAIN, :] = pred[0:MAIN].astype(jnp.bfloat16)
            rest.append(pred[MAIN:FP])
        psend[e, k, 2 * MAIN :, :] = jnp.concatenate(rest, axis=0).astype(jnp.bfloat16)

    def send(e, k):
        far_copy(e, k).start()
        if e == 1:
            mate_copy(k).start()

    for e in range(2):
        predict(e, 0)

    pl.semaphore_wait(barrier, GROUP + 1)
    for e in range(2):
        send(e, 0)

    def owner_of(n):
        p = lax.rem(pts + n, PTS)
        differ = lax.rem(lax.div(p, 16) + xl, 2)
        return p, (lax.rem(xh + c * differ, 2) * 2 + c, p)

    def ask(n, _):
        pltpu.make_async_remote_copy(
            src_ref=src_ref.at[pl.ds(pl.multiple_of(8 * c, 8), 8)],
            dst_ref=asked.at[pts],
            send_sem=ask_s,
            recv_sem=ask_r,
            device_id=owner_of(n)[1],
            device_id_type=MESH,
        ).start()
        return 0

    lax.fori_loop(1, PTS, ask, 0)
    asked[pts] = src_ref[pl.ds(pl.multiple_of(8 * c, 8), 8), :]

    for e in range(2):
        predict(e, 1)
        send(e, 1)

    def lend(e, k):
        lanes = pl.ds(pl.multiple_of((1 - c) * WIDE, WIDE), WIDE)
        return pltpu.make_async_remote_copy(
            src_ref=lat.at[e, k, :, :, lanes],
            dst_ref=mlat.at[1 - e, k],
            send_sem=ms.at[e * NK + k],
            recv_sem=mr.at[(1 - e) * NK + k],
            device_id=mate,
            device_id_type=MESH,
        )

    def lent(e, k):
        return pltpu.make_async_copy(mlat.at[e, k], mlat.at[e, k], mr.at[e * NK + k])

    for e in range(2):
        lend(e, 0).start()

    tgt_copy.wait()
    tt[FP:128, :] = jnp.zeros((128 - FP, SLOTS), jnp.bfloat16)
    tt[128 + FP :, :] = jnp.zeros((128 - FP, SLOTS), jnp.bfloat16)
    last8[...] = jnp.zeros_like(last8)
    last8[0 : F - MAIN, :] = tv[MAIN:F, :]
    last8[F - MAIN : F - MAIN + 1, :] = area_ref[...]

    def split(value, at):
        high = value.astype(jnp.bfloat16)
        tt[at : at + value.shape[0], :] = high
        low = (value - high.astype(jnp.float32)).astype(jnp.bfloat16)
        tt[128 + at : 128 + at + value.shape[0], :] = low

    for at in range(0, MAIN, 32):
        split(tv[at : at + 32, :], at)
    split(last8[...], MAIN)


    def asked_bytes(sem):
        return pltpu.make_async_copy(
            asked.at[pl.ds(0, PTS - 1)], asked.at[pl.ds(0, PTS - 1)], sem
        )

    asked_bytes(ask_r).wait()
    found = asked[...].reshape(PTS * 8, 128) - pts * SLOTS
    lane = lax.broadcasted_iota(jnp.int32, (PTS * 8, 128), 1)
    row = lax.broadcasted_iota(jnp.int32, (PTS * 8, 128), 0)
    found = jnp.where(lax.rem(lane, 32) == pts, found, 0)
    spread_row = lax.broadcasted_iota(jnp.int32, (128, 128), 0)
    spread_lane = lax.broadcasted_iota(jnp.int32, (128, 128), 1)
    spread = jnp.where(lax.div(spread_row, 32) == lax.div(spread_lane, 32), 1.0, 0.0)
    spread = spread.astype(jnp.bfloat16)
    high = lax.shift_right_logical(found, 6).astype(jnp.float32).astype(jnp.bfloat16)
    low = lax.bitwise_and(found, 63).astype(jnp.float32).astype(jnp.bfloat16)
    wide = 64.0 * jnp.dot(high, spread, preferred_element_type=jnp.float32) + jnp.dot(
        low, spread, preferred_element_type=jnp.float32
    )
    wide = jnp.where(lax.rem(lane, 32) == lax.rem(row, 32), wide, 0.0)
    wanted = jnp.sum(wide.reshape(8, 32, 128), axis=1)
    for half in range(4):
        cols = jnp.concatenate(
            [column(wanted[2 * half + b : 2 * half + b + 1, :], 128) for b in range(2)], axis=0
        ).astype(jnp.int32)
        place = lax.broadcasted_iota(jnp.int32, (256, SLOTS), 1)
        onehot = jnp.where(place == cols, 1.0, 0.0).astype(jnp.bfloat16)
        got = lax.dot_general(
            onehot, tt[...], (((1,), (1,)), ((), ())), preferred_element_type=jnp.float32
        )
        got = got[:, 0:128] + got[:, 128:256]
        tq[2 * half : 2 * half + 2] = got.reshape(2, 4, 4, 8, 128)

    def answer(n, _):
        p, device = owner_of(n)
        pltpu.make_async_remote_copy(
            src_ref=tq.at[lax.div(p, 4), :, lax.rem(p, 4)],
            dst_ref=rq.at[:, pts],
            send_sem=tq_s,
            recv_sem=tq_r,
            device_id=device,
            device_id_type=MESH,
        ).start()
        return 0

    lax.fori_loop(1, PTS, answer, 0)
    rq[:, pts] = tq[lax.div(pts, 4), :, lax.rem(pts, 4)]

    for k in range(2, NK):
        for e in range(2):
            predict(e, k)
            send(e, k)
    for k in range(1, NK):
        for e in range(2):
            lend(e, k).start()

    def grad_copy(k):
        return pltpu.make_async_remote_copy(
            src_ref=gl.at[k],
            dst_ref=gx.at[k],
            send_sem=gs.at[k],
            recv_sem=gr.at[k],
            device_id=mate,
            device_id_type=MESH,
        )

    def near_buffers(k):
        return psend.at[0, k], pmate.at[k]

    def far_buffers(k):
        return prem.at[0, k], prem.at[1, k]

    def main_rows(buffers, t, lanes):
        return [
            buffer[pl.ds(pl.multiple_of(m * MAIN + 16 * t, 16), 16), lanes].astype(jnp.float32)
            for m in range(2)
            for buffer in buffers
        ]

    def rest_rows(buffers, lanes):
        rest = [buffer[2 * MAIN : ROWS, lanes].astype(jnp.float32) for buffer in buffers]
        return [value[8 * m : 8 * m + 8] for m in range(2) for value in rest]

    def blocks(k):
        for part in range(CH // 128):
            yield slice(128 * part, 128 * (part + 1)), k * CH + 128 * part

    def pairs_chunk(k):
        mate_copy(k).wait_recv()
        far_copy(0, k).wait_recv()
        far_copy(1, k).wait_recv()
        for lanes, at in blocks(k):

            def step(t, _):
                sums = pair_sums(
                    main_rows(near_buffers(k), t, lanes), main_rows(far_buffers(k), t, lanes)
                )
                for n in range(4):
                    sp[n, pl.ds(pl.multiple_of(16 * t, 16), 16), at : at + 128] = sums[n]
                return 0

            lax.fori_loop(0, MAIN // 16, step, 0)
            sums = pair_sums(rest_rows(near_buffers(k), lanes), rest_rows(far_buffers(k), lanes))
            for n in range(4):
                sp[n, MAIN:FP, at : at + 128] = sums[n]

    def grads_chunk(k):
        for lanes, at in blocks(k):

            def grads_of(own, rows):
                return gradients(
                    own, [sp[n, rows, at : at + 128] for n in range(4)],
                    tslot[rows, at : at + 128], wcol[rows, :] * tslot[F : F + 1, at : at + 128],
                )

            def step(t, _):
                rows = pl.ds(pl.multiple_of(16 * t, 16), 16)
                grads = grads_of(main_rows(near_buffers(k), t, lanes), rows)
                for n in range(4):
                    gl[k, ORDER[n], rows, lanes] = grads[n]
                bsum[rows, :] += sum(grad.astype(jnp.float32) for grad in grads)
                return 0

            lax.fori_loop(0, MAIN // 16, step, 0)
            grads = grads_of(rest_rows(near_buffers(k), lanes), slice(MAIN, FP))
            none = jnp.zeros((8, 128), jnp.float32)
            for n in range(4):
                full = jnp.concatenate([grads[n].astype(jnp.float32), none], axis=0)
                gl[k, ORDER[n], MAIN:FB, lanes] = full.astype(jnp.bfloat16)
            bsum[MAIN:FP, :] += sum(grad.astype(jnp.float32) for grad in grads)

    def own_grads(e, k, m):
        return gl[k, m] if e == 0 else gx[k, 2 + m]

    def latent_grad(e, k):
        for m in range(2):
            part = pl.ds(pl.multiple_of(halves[e] * HALF + k * CH, CH), CH)
            lg[m, part, :] = lax.dot_general(
                own_grads(e, k, m), wpad[...], (((0,), (0,)), ((), ())),
                preferred_element_type=jnp.float32,
            ).astype(jnp.bfloat16)

    def accumulate(e, k):
        lent(e, k).wait()
        lanes = pl.ds(pl.multiple_of(c * WIDE, WIDE), WIDE)
        for m in range(2):
            own, other = (gl[k, m], gl[k, 2 + m]) if e == 0 else (gx[k, 2 + m], gx[k, m])
            acc[...] += jnp.dot(
                own, lat[e, k, m, :, lanes], preferred_element_type=jnp.float32
            ) + jnp.dot(other, mlat[e, k, m], preferred_element_type=jnp.float32)

    for k in range(EARLY):
        pairs_chunk(k)

    def rq_bytes(sem):
        return pltpu.make_async_copy(
            rq.at[:, pl.ds(0, PTS - 1)], rq.at[:, pl.ds(0, PTS - 1)], sem
        )

    rq_bytes(tq_r).wait()
    for r in range(8):
        rows = jnp.concatenate([rq[a, :, r, :] for a in range(4)], axis=0)
        tslot[:, 128 * r : 128 * (r + 1)] = rows.T[0:FP]

    for k in range(NK):
        if k >= EARLY:
            pairs_chunk(k)
        grads_chunk(k)
        grad_copy(k).start()
        accumulate(0, k)
        if k > 0:
            grad_copy(k - 1).wait_recv()
            accumulate(1, k - 1)
    grad_copy(NK - 1).wait_recv()
    accumulate(1, NK - 1)

    at = lax.broadcasted_iota(jnp.int32, (FP, 128), 0)
    lane_at = lax.broadcasted_iota(jnp.int32, (FP, 128), 1)
    bias = jnp.sum(bsum[...], axis=1, keepdims=True)
    bias = jnp.sum(jnp.where(at == lane_at, bias, 0.0), axis=0, keepdims=True)
    acc[MAIN:FP, 0:128] += jnp.where(at[0 : FP - MAIN] == F - MAIN, bias, 0.0)
    y = lax.rem(lax.div(pts, 4), 4)
    z = lax.rem(pts, 4)
    x = xh * 2 + xl
    slot = z * 16 + y * 4 + x

    def tile_at(q_xh, q_y, q_z):
        full = lax.div(q_z, 3) * lax.div(q_y, 2) == 0
        return q_z * 8 + q_y * 2 + q_xh, full, lax.rem(c + q_y + q_z, 2)

    tile, full, tile_xl = tile_at(xh, y, z)
    owns = jnp.logical_and(full, tile_xl == xl)

    def acc_tile(q):
        rows = pl.ds(pl.multiple_of(lax.div(q, 4) * TILE, TILE), TILE)
        return rows, pl.ds(pl.multiple_of(lax.rem(q, 4) * 128, 128), 128)

    ys = [lax.rem(y + d, 4) for d in range(4)]
    xs = [lax.rem(x + d, 4) for d in range(4)]
    far_first = (2, 1, 3, 0)

    def scatter(n, _):
        q_z = lax.rem(z + n + 2, 4)
        for dy in far_first:
            for q_xh in (1 - xh, xh):
                q, q_full, q_xl = tile_at(q_xh, ys[dy], q_z)
                there = q_full
                if dy == 0 and q_xh is xh:
                    there = jnp.logical_and(there, jnp.logical_or(n != 2, q_xl != xl))

                @pl.when(there)
                def _(q=q, q_xh=q_xh, q_xl=q_xl, dy=dy):
                    rows, lanes = acc_tile(q)
                    pltpu.make_async_remote_copy(
                        src_ref=acc.at[rows, lanes], dst_ref=rs.at[slot], send_sem=ar_s.at[0],
                        recv_sem=ar_r.at[0],
                        device_id=(q_xh * 2 + c, q_xl * 16 + ys[dy] * 4 + q_z),
                        device_id_type=MESH,
                    ).start()

        return 0

    lax.fori_loop(0, 4, scatter, 0)
    for e in range(2):
        for k in range(NK):
            latent_grad(e, k)

    def tiles(ref, count, sem):
        return pltpu.make_async_copy(ref.at[pl.ds(0, count)], ref.at[pl.ds(0, count)], sem)

    @pl.when(owns)
    def _():
        rows, lanes = acc_tile(tile)
        rs[slot] = acc[rows, lanes]
        tiles(rs, CHIPS - 1, ar_r.at[0]).wait()
        mine = c * TILES + tile
        ag[mine] = jnp.sum(rs[...], axis=0).astype(jnp.bfloat16)

        def share(device):
            pltpu.make_async_remote_copy(
                src_ref=ag.at[mine], dst_ref=ag.at[mine], send_sem=ar_s.at[1],
                recv_sem=ar_r.at[1], device_id=device, device_id_type=MESH,
            ).start()

        def gather(n, _):
            q_z = lax.rem(z + n + 2, 4)

            def chip(dy, dx):
                q_mem = lax.div(xs[dx], 2) * 2
                q_pts = lax.rem(xs[dx], 2) * 16 + ys[dy] * 4 + q_z
                for core in range(2):
                    share((q_mem + core, q_pts))

            for dy in far_first:
                for dx in far_first:
                    if dy == 0 and dx == 0:
                        pl.when(n != 2)(lambda: chip(0, 0))
                    else:
                        chip(dy, dx)
            return 0

        lax.fori_loop(0, 4, gather, 0)
        share(mate)

    for k in range(NK):
        for e in range(2):
            far_copy(e, k).wait_send()
            lend(e, k).wait_send()
        mate_copy(k).wait_send()
        grad_copy(k).wait_send()
    asked_bytes(ask_s).wait()
    rq_bytes(tq_s).wait()

    @pl.when(owns)
    def _():
        tiles(rs, TILES - 1, ar_s.at[0]).wait()
        tiles(ag, 2 * TILES - 1, ar_r.at[1]).wait()
        tiles(sent, 2 * CHIPS - 1, ar_s.at[1]).wait()

    @pl.when(jnp.logical_not(owns))
    def _():
        tiles(rs, TILES, ar_s.at[0]).wait()
        tiles(ag, 2 * TILES, ar_r.at[1]).wait()


def output_kernel(lg, ag, lg_out, wg_out, bg_out, wg, bg, sem):
    norm = float(M * SLOTS * PTS) ** (-0.5)
    parts = 4
    size = SLOTS // parts
    copies = [
        pltpu.make_async_copy(
            lg.at[m, pl.ds(size * n, size)], lg_out.at[m, pl.ds(size * n, size)],
            sem.at[parts * m + n],
        )
        for m in range(2) for n in range(parts)
    ]
    for copy in copies:
        copy.start()
    for q in range(2 * TILES):
        t, lb = q % TILES // 4, q // TILES * 4 + q % 4
        rows = min(F, TILE * (t + 1)) - TILE * t
        tile_sum = ag[q].astype(jnp.float32) * norm
        wg[TILE * t : TILE * t + rows, 128 * lb : 128 * (lb + 1)] = tile_sum[0:rows]
    last = MAIN // TILE * 4
    pair = ag[last].astype(jnp.float32) + ag[TILES + last].astype(jnp.float32)
    bg[...] = pair[F - MAIN : F - MAIN + 1, 0:F] * norm
    for n, (src, dst) in enumerate(((wg, wg_out), (bg, bg_out))):
        copies.append(pltpu.make_async_copy(src, dst, sem.at[2 * parts + n]))
        copies[-1].start()
    for copy in copies:
        copy.wait()


def per_device(latent, head_weight, head_bias, targets, cell_area, field_level, source):
    vmem = pl.BlockSpec(memory_space=pltpu.VMEM)
    hbm = pl.BlockSpec(memory_space=pltpu.HBM)
    bf16, f32 = jnp.bfloat16, jnp.float32
    dma = pltpu.SemaphoreType.DMA
    operands = (
        latent, head_weight, head_bias.reshape(1, F), field_level.reshape(1, F), targets,
        cell_area.reshape(1, SLOTS), source.reshape(16, 128),
    )
    latents, sums = pl.pallas_call(
        main_kernel,
        out_shape=(
            pltpu.VMEM((2, SLOTS, L), bf16),
            pltpu.VMEM((2 * TILES, TILE, 128), bf16),
        ),
        in_specs=[hbm] * 7,
        out_specs=(vmem, vmem),
        scratch_shapes=[
            pltpu.VMEM((2, NK, 2, CH, L), bf16),
            pltpu.VMEM((F, L), bf16),
            pltpu.VMEM((1, F), bf16),
            pltpu.VMEM((1, F), jnp.int32),
            pltpu.VMEM((1, SLOTS), f32),
            pltpu.VMEM((16, 128), jnp.int32),
            pltpu.VMEM((FB, L), bf16),
            pltpu.VMEM((F, SLOTS), f32),
            pltpu.VMEM((256, SLOTS), bf16),
            pltpu.VMEM((8, SLOTS), f32),
            pltpu.VMEM((PTS, 8, 128), jnp.int32),
            pltpu.VMEM((8, 4, 4, 8, 128), f32),
            pltpu.VMEM((4, PTS, 8, 128), f32),
            pltpu.VMEM((FP, HALF), f32),
            pltpu.VMEM((FP, 128), f32),
            pltpu.VMEM((FP, 128), f32),
            pltpu.VMEM((2, NK, ROWS, CH), bf16),
            pltpu.VMEM((NK, ROWS, CH), bf16),
            pltpu.VMEM((2, NK, ROWS, CH), bf16),
            pltpu.VMEM((NK, 4, FB, CH), bf16),
            pltpu.VMEM((NK, 4, FB, CH), bf16),
            pltpu.VMEM((2, NK, 2, CH, WIDE), bf16),
            pltpu.VMEM((FB, WIDE), f32),
            pltpu.VMEM((FP, 128), f32),
            pltpu.VMEM((CHIPS, TILE, 128), f32),
            pltpu.VMEM((2 * CHIPS, TILE, 128), bf16),
            pltpu.VMEM((4, FP, HALF), f32),
            dma((2 * NK,)),
            dma((5,)),
            dma,
            dma, dma, dma, dma,
            dma((2 * NK,)), dma((2 * NK,)),
            dma((NK,)), dma((NK,)),
            dma((2 * NK,)), dma((2 * NK,)),
            dma((NK,)), dma((NK,)),
            dma((2,)), dma((2,)),
        ],
        compiler_params=pltpu.CompilerParams(
            collective_id=0, has_side_effects=True, vmem_limit_bytes=VMEM
        ),
    )(*(pltpu.with_memory_space_constraint(x, pltpu.HBM) for x in operands))
    latent_grad, weight_grad, bias_grad = pl.pallas_call(
        output_kernel,
        in_specs=[vmem, vmem],
        out_specs=(hbm, hbm, hbm),
        out_shape=(
            jax.ShapeDtypeStruct((2, SLOTS, L), bf16),
            jax.ShapeDtypeStruct((F, L), f32),
            jax.ShapeDtypeStruct((1, F), f32),
        ),
        scratch_shapes=[pltpu.VMEM((F, L), f32), pltpu.VMEM((1, F), f32), dma((10,))],
        compiler_params=pltpu.CompilerParams(vmem_limit_bytes=8 * 2**20),
    )(latents, sums)
    return latent_grad, weight_grad, bias_grad.reshape(F)


def solution(mesh):
    return jax.shard_map(
        per_device,
        mesh=mesh,
        in_specs=(P("mem", "pts", None), P(), P(), P(None, "pts"), P("pts"), P(), P("pts")),
        out_specs=(P("mem", "pts", None), P(), P()),
        check_vma=False,
    )
```

```python
import jax
import jax.numpy as jnp
from jax import lax
from jax.experimental import pallas as pl
from jax.experimental.pallas import tpu as pltpu
from jax.sharding import PartitionSpec as P

M = 8
F = 102
L = 1024
FP = 104
FB = 112
MAIN = 96
SLOTS = 2048
HALF = 1024
CH = 256
NK = HALF // CH
ROWS = 208
PTS = 32
GROUP = 64
TILE = 16
WIDE = L // 2
TILES = (FB // TILE) * (WIDE // 128)
CHIPS = 64
VMEM = 40 * 2**20
EARLY = 2
ORDER = (0, 2, 1, 3)
MESH = pl.DeviceIdType.MESH

FAIR_ALPHA = 0.95
SMOOTH_WIDTH = 0.25
SPREAD = (1.0 - (1.0 - FAIR_ALPHA) / M) / (M - 1)


def smooth_sign(diff):
    return diff * lax.rsqrt(diff * diff + SMOOTH_WIDTH * SMOOTH_WIDTH)


def pair_sums(own, far):
    spread = [None] * len(own)

    def add(at, term):
        spread[at] = term if spread[at] is None else spread[at] + term

    for a in range(len(own)):
        for b in range(a + 1, len(own)):
            q = smooth_sign(own[a] - own[b])
            add(a, q)
            add(b, -q)
        for other in far:
            add(a, smooth_sign(own[a] - other))
    return spread


def gradients(own, spread, target, scale):
    return [
        (scale * (smooth_sign(value - target) - SPREAD * others)).astype(jnp.bfloat16)
        for value, others in zip(own, spread, strict=True)
    ]


def column(row, rows):
    n = row.shape[1]
    at = lax.broadcasted_iota(jnp.int32, (rows, n), 0)
    lane = lax.broadcasted_iota(jnp.int32, (rows, n), 1)
    return jnp.sum(jnp.where(at == lane, row, 0.0), axis=1, keepdims=True)


def main_kernel(
    latent, w_hbm, bias_hbm, level_hbm, tgt, area_hbm, src_hbm,
    lg, ag,
    lat, w_ref, bias_ref, level_ref, area_ref, src_ref,
    wpad, tv, tt, last8, asked, tq, rq, tslot, bcol, wcol,
    psend, pmate, prem, gl, gx, mlat, acc, bsum, rs, sent, sp,
    lat_sem, small_sem, tgt_sem, ask_s, ask_r, tq_s, tq_r,
    ps_far, pr_far, ps_mate, pr_mate, ms, mr, gs, gr, ar_s, ar_r,
):
    i = lax.axis_index("mem")
    pts = lax.axis_index("pts")
    xh = lax.div(i, 2)
    c = lax.rem(i, 2)
    xl = lax.div(pts, 16)
    me = xh * PTS + pts
    mate = (xh * 2 + (1 - c), pts)
    far = ((1 - xh) * 2 + c, pts)
    far_mate = ((1 - xh) * 2 + (1 - c), pts)
    halves = (c, 1 - c)

    def lat_copy(e, k):
        off = pl.multiple_of(halves[e] * HALF + k * CH, CH)
        return pltpu.make_async_copy(
            latent.at[:, pl.ds(off, CH)], lat.at[e, k], lat_sem.at[e * NK + k]
        )

    small = [
        pltpu.make_async_copy(src, dst, small_sem.at[n])
        for n, (src, dst) in enumerate(
            (
                (w_hbm, w_ref), (bias_hbm, bias_ref), (level_hbm, level_ref),
                (area_hbm, area_ref), (src_hbm, src_ref),
            )
        )
    ]
    tgt_copy = pltpu.make_async_copy(tgt, tv, tgt_sem)
    for copy in small:
        copy.start()
    for k in range(NK):
        for e in range(2):
            lat_copy(e, k).start()
        if k == 0:
            tgt_copy.start()

    barrier = pltpu.get_barrier_semaphore()

    def group_device(n):
        q = lax.rem(me + n, GROUP)
        q_xh = lax.div(q, PTS)
        q_pts = lax.rem(q, PTS)
        return q, q_xh, q_pts, (q_xh * 2 + c, q_pts)

    pl.semaphore_signal(barrier, inc=1, device_id=far_mate, device_id_type=MESH)
    pl.semaphore_signal(barrier, inc=1, device_id=mate, device_id_type=MESH)

    def greet(n, _):
        pl.semaphore_signal(barrier, inc=1, device_id=group_device(n)[3], device_id_type=MESH)
        return 0

    lax.fori_loop(1, GROUP, greet, 0)

    for copy in small:
        copy.wait()
    wpad[...] = jnp.zeros_like(wpad)
    wpad[0:F, :] = w_ref[...]
    bcol[...] = jnp.broadcast_to(column(bias_ref[...].astype(jnp.float32), FP), bcol.shape)
    level = (level_ref[...].astype(jnp.float32) + 1.0) / 7.0
    wcol[...] = jnp.broadcast_to(column(level, FP), wcol.shape)
    acc[...] = jnp.zeros_like(acc)
    bsum[...] = jnp.zeros_like(bsum)

    def far_copy(e, k):
        return pltpu.make_async_remote_copy(
            src_ref=psend.at[e, k],
            dst_ref=prem.at[e, k],
            send_sem=ps_far.at[e * NK + k],
            recv_sem=pr_far.at[e * NK + k],
            device_id=far if e == 0 else far_mate,
            device_id_type=MESH,
        )

    def mate_copy(k):
        return pltpu.make_async_remote_copy(
            src_ref=psend.at[1, k],
            dst_ref=pmate.at[k],
            send_sem=ps_mate.at[k],
            recv_sem=pr_mate.at[k],
            device_id=mate,
            device_id_type=MESH,
        )

    def predict(e, k):
        lat_copy(e, k).wait()
        rest = []
        for m in range(2):
            pred = lax.dot_general(
                wpad[...], lat[e, k, m], (((1,), (1,)), ((), ())),
                preferred_element_type=jnp.float32,
            )[0:FP]
            pred = pred + bcol[:, 0:1]
            psend[e, k, m * MAIN : (m + 1) * MAIN, :] = pred[0:MAIN].astype(jnp.bfloat16)
            rest.append(pred[MAIN:FP])
        psend[e, k, 2 * MAIN :, :] = jnp.concatenate(rest, axis=0).astype(jnp.bfloat16)

    def send(e, k):
        far_copy(e, k).start()
        if e == 1:
            mate_copy(k).start()

    for e in range(2):
        predict(e, 0)

    pl.semaphore_wait(barrier, GROUP + 1)
    def owner_of(n):
        p = lax.rem(pts + n, PTS)
        differ = lax.rem(lax.div(p, 16) + xl, 2)
        return p, (lax.rem(xh + c * differ, 2) * 2 + c, p)

    def ask(n, _):
        pltpu.make_async_remote_copy(
            src_ref=src_ref.at[pl.ds(pl.multiple_of(8 * c, 8), 8)],
            dst_ref=asked.at[pts],
            send_sem=ask_s,
            recv_sem=ask_r,
            device_id=owner_of(n)[1],
            device_id_type=MESH,
        ).start()
        return 0

    lax.fori_loop(1, PTS, ask, 0)
    for e in range(2):
        send(e, 0)

    asked[pts] = src_ref[pl.ds(pl.multiple_of(8 * c, 8), 8), :]

    for k in range(1, NK):
        for e in range(2):
            predict(e, k)

    def lend(e, k):
        lanes = pl.ds(pl.multiple_of((1 - c) * WIDE, WIDE), WIDE)
        return pltpu.make_async_remote_copy(
            src_ref=lat.at[e, k, :, :, lanes],
            dst_ref=mlat.at[1 - e, k],
            send_sem=ms.at[e * NK + k],
            recv_sem=mr.at[(1 - e) * NK + k],
            device_id=mate,
            device_id_type=MESH,
        )

    def lent(e, k):
        return pltpu.make_async_copy(mlat.at[e, k], mlat.at[e, k], mr.at[e * NK + k])

    for e in range(2):
        lend(e, 0).start()

    tgt_copy.wait()
    tt[FP:128, :] = jnp.zeros((128 - FP, SLOTS), jnp.bfloat16)
    tt[128 + FP :, :] = jnp.zeros((128 - FP, SLOTS), jnp.bfloat16)
    last8[...] = jnp.zeros_like(last8)
    last8[0 : F - MAIN, :] = tv[MAIN:F, :]
    last8[F - MAIN : F - MAIN + 1, :] = area_ref[...]

    def split(value, at):
        high = value.astype(jnp.bfloat16)
        tt[at : at + value.shape[0], :] = high
        low = (value - high.astype(jnp.float32)).astype(jnp.bfloat16)
        tt[128 + at : 128 + at + value.shape[0], :] = low

    for at in range(0, MAIN, 32):
        split(tv[at : at + 32, :], at)
    split(last8[...], MAIN)


    def asked_bytes(sem):
        return pltpu.make_async_copy(
            asked.at[pl.ds(0, PTS - 1)], asked.at[pl.ds(0, PTS - 1)], sem
        )

    asked_bytes(ask_r).wait()
    for e in range(2):
        send(e, 1)
    found = asked[...].reshape(PTS * 8, 128) - pts * SLOTS
    lane = lax.broadcasted_iota(jnp.int32, (PTS * 8, 128), 1)
    row = lax.broadcasted_iota(jnp.int32, (PTS * 8, 128), 0)
    found = jnp.where(lax.rem(lane, 32) == pts, found, 0)
    spread_row = lax.broadcasted_iota(jnp.int32, (128, 128), 0)
    spread_lane = lax.broadcasted_iota(jnp.int32, (128, 128), 1)
    spread = jnp.where(lax.div(spread_row, 32) == lax.div(spread_lane, 32), 1.0, 0.0)
    spread = spread.astype(jnp.bfloat16)
    high = lax.shift_right_logical(found, 6).astype(jnp.float32).astype(jnp.bfloat16)
    low = lax.bitwise_and(found, 63).astype(jnp.float32).astype(jnp.bfloat16)
    wide = 64.0 * jnp.dot(high, spread, preferred_element_type=jnp.float32) + jnp.dot(
        low, spread, preferred_element_type=jnp.float32
    )
    wide = jnp.where(lax.rem(lane, 32) == lax.rem(row, 32), wide, 0.0)
    wanted = jnp.sum(wide.reshape(8, 32, 128), axis=1)
    for half in range(4):
        cols = jnp.concatenate(
            [column(wanted[2 * half + b : 2 * half + b + 1, :], 128) for b in range(2)], axis=0
        ).astype(jnp.int32)
        place = lax.broadcasted_iota(jnp.int32, (256, SLOTS), 1)
        onehot = jnp.where(place == cols, 1.0, 0.0).astype(jnp.bfloat16)
        got = lax.dot_general(
            onehot, tt[...], (((1,), (1,)), ((), ())), preferred_element_type=jnp.float32
        )
        got = got[:, 0:128] + got[:, 128:256]
        tq[2 * half : 2 * half + 2] = got.reshape(2, 4, 4, 8, 128)

    def answer(n, _):
        p, device = owner_of(n)
        pltpu.make_async_remote_copy(
            src_ref=tq.at[lax.div(p, 4), :, lax.rem(p, 4)],
            dst_ref=rq.at[:, pts],
            send_sem=tq_s,
            recv_sem=tq_r,
            device_id=device,
            device_id_type=MESH,
        ).start()
        return 0

    lax.fori_loop(1, PTS, answer, 0)
    rq[:, pts] = tq[lax.div(pts, 4), :, lax.rem(pts, 4)]

    for k in range(2, NK):
        for e in range(2):
            send(e, k)
    for k in range(1, NK):
        for e in range(2):
            lend(e, k).start()

    def grad_copy(k):
        return pltpu.make_async_remote_copy(
            src_ref=gl.at[k],
            dst_ref=gx.at[k],
            send_sem=gs.at[k],
            recv_sem=gr.at[k],
            device_id=mate,
            device_id_type=MESH,
        )

    def near_buffers(k):
        return psend.at[0, k], pmate.at[k]

    def far_buffers(k):
        return prem.at[0, k], prem.at[1, k]

    def main_rows(buffers, t, lanes):
        return [
            buffer[pl.ds(pl.multiple_of(m * MAIN + 16 * t, 16), 16), lanes].astype(jnp.float32)
            for m in range(2)
            for buffer in buffers
        ]

    def rest_rows(buffers, lanes):
        rest = [buffer[2 * MAIN : ROWS, lanes].astype(jnp.float32) for buffer in buffers]
        return [value[8 * m : 8 * m + 8] for m in range(2) for value in rest]

    def blocks(k):
        for part in range(CH // 128):
            yield slice(128 * part, 128 * (part + 1)), k * CH + 128 * part

    def pairs_chunk(k):
        mate_copy(k).wait_recv()
        far_copy(0, k).wait_recv()
        far_copy(1, k).wait_recv()
        for lanes, at in blocks(k):

            def step(t, _):
                sums = pair_sums(
                    main_rows(near_buffers(k), t, lanes), main_rows(far_buffers(k), t, lanes)
                )
                for n in range(4):
                    sp[n, pl.ds(pl.multiple_of(16 * t, 16), 16), at : at + 128] = sums[n]
                return 0

            lax.fori_loop(0, MAIN // 16, step, 0)
            sums = pair_sums(rest_rows(near_buffers(k), lanes), rest_rows(far_buffers(k), lanes))
            for n in range(4):
                sp[n, MAIN:FP, at : at + 128] = sums[n]

    def grads_chunk(k):
        for lanes, at in blocks(k):

            def grads_of(own, rows):
                return gradients(
                    own, [sp[n, rows, at : at + 128] for n in range(4)],
                    tslot[rows, at : at + 128], wcol[rows, :] * tslot[F : F + 1, at : at + 128],
                )

            def step(t, _):
                rows = pl.ds(pl.multiple_of(16 * t, 16), 16)
                grads = grads_of(main_rows(near_buffers(k), t, lanes), rows)
                for n in range(4):
                    gl[k, ORDER[n], rows, lanes] = grads[n]
                bsum[rows, :] += sum(grad.astype(jnp.float32) for grad in grads)
                return 0

            lax.fori_loop(0, MAIN // 16, step, 0)
            grads = grads_of(rest_rows(near_buffers(k), lanes), slice(MAIN, FP))
            none = jnp.zeros((8, 128), jnp.float32)
            for n in range(4):
                full = jnp.concatenate([grads[n].astype(jnp.float32), none], axis=0)
                gl[k, ORDER[n], MAIN:FB, lanes] = full.astype(jnp.bfloat16)
            bsum[MAIN:FP, :] += sum(grad.astype(jnp.float32) for grad in grads)

    def own_grads(e, k, m):
        return gl[k, m] if e == 0 else gx[k, 2 + m]

    def latent_grad(e, k):
        for m in range(2):
            part = pl.ds(pl.multiple_of(halves[e] * HALF + k * CH, CH), CH)
            lg[m, part, :] = lax.dot_general(
                own_grads(e, k, m), wpad[...], (((0,), (0,)), ((), ())),
                preferred_element_type=jnp.float32,
            ).astype(jnp.bfloat16)

    def accumulate(e, k):
        lent(e, k).wait()
        lanes = pl.ds(pl.multiple_of(c * WIDE, WIDE), WIDE)
        for m in range(2):
            own, other = (gl[k, m], gl[k, 2 + m]) if e == 0 else (gx[k, 2 + m], gx[k, m])
            acc[...] += jnp.dot(
                own, lat[e, k, m, :, lanes], preferred_element_type=jnp.float32
            ) + jnp.dot(other, mlat[e, k, m], preferred_element_type=jnp.float32)

    for k in range(EARLY):
        pairs_chunk(k)

    def rq_bytes(sem):
        return pltpu.make_async_copy(
            rq.at[:, pl.ds(0, PTS - 1)], rq.at[:, pl.ds(0, PTS - 1)], sem
        )

    rq_bytes(tq_r).wait()
    for r in range(8):
        rows = jnp.concatenate([rq[a, :, r, :] for a in range(4)], axis=0)
        tslot[:, 128 * r : 128 * (r + 1)] = rows.T[0:FP]

    for k in range(NK):
        if k >= EARLY:
            pairs_chunk(k)
        grads_chunk(k)
        grad_copy(k).start()
        accumulate(0, k)
        if k > 0:
            grad_copy(k - 1).wait_recv()
            accumulate(1, k - 1)
    grad_copy(NK - 1).wait_recv()
    accumulate(1, NK - 1)

    at = lax.broadcasted_iota(jnp.int32, (FP, 128), 0)
    lane_at = lax.broadcasted_iota(jnp.int32, (FP, 128), 1)
    bias = jnp.sum(bsum[...], axis=1, keepdims=True)
    bias = jnp.sum(jnp.where(at == lane_at, bias, 0.0), axis=0, keepdims=True)
    acc[MAIN:FP, 0:128] += jnp.where(at[0 : FP - MAIN] == F - MAIN, bias, 0.0)
    y = lax.rem(lax.div(pts, 4), 4)
    z = lax.rem(pts, 4)
    x = xh * 2 + xl
    slot = z * 16 + y * 4 + x

    def tile_at(q_xh, q_y, q_z):
        full = lax.div(q_z, 3) * lax.div(q_y, 2) == 0
        return q_z * 8 + q_y * 2 + q_xh, full, lax.rem(c + q_y + q_z, 2)

    tile, full, tile_xl = tile_at(xh, y, z)
    owns = jnp.logical_and(full, tile_xl == xl)

    def acc_tile(q):
        rows = pl.ds(pl.multiple_of(lax.div(q, 4) * TILE, TILE), TILE)
        return rows, pl.ds(pl.multiple_of(lax.rem(q, 4) * 128, 128), 128)

    ys = [lax.rem(y + d, 4) for d in range(4)]
    xs = [lax.rem(x + d, 4) for d in range(4)]
    far_first = (2, 1, 3, 0)

    def scatter(n, _):
        q_z = lax.rem(z + n + 2, 4)
        for dy in far_first:
            for q_xh in (1 - xh, xh):
                q, q_full, q_xl = tile_at(q_xh, ys[dy], q_z)
                there = q_full
                if dy == 0 and q_xh is xh:
                    there = jnp.logical_and(there, jnp.logical_or(n != 2, q_xl != xl))

                @pl.when(there)
                def _(q=q, q_xh=q_xh, q_xl=q_xl, dy=dy):
                    rows, lanes = acc_tile(q)
                    pltpu.make_async_remote_copy(
                        src_ref=acc.at[rows, lanes], dst_ref=rs.at[slot], send_sem=ar_s.at[0],
                        recv_sem=ar_r.at[0],
                        device_id=(q_xh * 2 + c, q_xl * 16 + ys[dy] * 4 + q_z),
                        device_id_type=MESH,
                    ).start()

        return 0

    lax.fori_loop(0, 4, scatter, 0)
    for e in range(2):
        for k in range(NK):
            latent_grad(e, k)

    def tiles(ref, count, sem):
        return pltpu.make_async_copy(ref.at[pl.ds(0, count)], ref.at[pl.ds(0, count)], sem)

    @pl.when(owns)
    def _():
        rows, lanes = acc_tile(tile)
        rs[slot] = acc[rows, lanes]
        tiles(rs, CHIPS - 1, ar_r.at[0]).wait()
        mine = c * TILES + tile
        ag[mine] = jnp.sum(rs[...], axis=0).astype(jnp.bfloat16)

        def share(device):
            pltpu.make_async_remote_copy(
                src_ref=ag.at[mine], dst_ref=ag.at[mine], send_sem=ar_s.at[1],
                recv_sem=ar_r.at[1], device_id=device, device_id_type=MESH,
            ).start()

        def gather(n, _):
            q_z = lax.rem(z + n + 2, 4)

            def chip(dy, dx):
                q_mem = lax.div(xs[dx], 2) * 2
                q_pts = lax.rem(xs[dx], 2) * 16 + ys[dy] * 4 + q_z
                for core in range(2):
                    share((q_mem + core, q_pts))

            for dy in far_first:
                for dx in far_first:
                    if dy == 0 and dx == 0:
                        pl.when(n != 2)(lambda: chip(0, 0))
                    else:
                        chip(dy, dx)
            return 0

        lax.fori_loop(0, 4, gather, 0)
        share(mate)

    for k in range(NK):
        for e in range(2):
            far_copy(e, k).wait_send()
            lend(e, k).wait_send()
        mate_copy(k).wait_send()
        grad_copy(k).wait_send()
    asked_bytes(ask_s).wait()
    rq_bytes(tq_s).wait()

    @pl.when(owns)
    def _():
        tiles(rs, TILES - 1, ar_s.at[0]).wait()
        tiles(ag, 2 * TILES - 1, ar_r.at[1]).wait()
        tiles(sent, 2 * CHIPS - 1, ar_s.at[1]).wait()

    @pl.when(jnp.logical_not(owns))
    def _():
        tiles(rs, TILES, ar_s.at[0]).wait()
        tiles(ag, 2 * TILES, ar_r.at[1]).wait()


def output_kernel(lg, ag, lg_out, wg_out, bg_out, wg, bg, sem):
    norm = float(M * SLOTS * PTS) ** (-0.5)
    parts = 4
    size = SLOTS // parts
    copies = [
        pltpu.make_async_copy(
            lg.at[m, pl.ds(size * n, size)], lg_out.at[m, pl.ds(size * n, size)],
            sem.at[parts * m + n],
        )
        for m in range(2) for n in range(parts)
    ]
    for copy in copies:
        copy.start()
    for q in range(2 * TILES):
        t, lb = q % TILES // 4, q // TILES * 4 + q % 4
        rows = min(F, TILE * (t + 1)) - TILE * t
        tile_sum = ag[q].astype(jnp.float32) * norm
        wg[TILE * t : TILE * t + rows, 128 * lb : 128 * (lb + 1)] = tile_sum[0:rows]
    last = MAIN // TILE * 4
    pair = ag[last].astype(jnp.float32) + ag[TILES + last].astype(jnp.float32)
    bg[...] = pair[F - MAIN : F - MAIN + 1, 0:F] * norm
    for n, (src, dst) in enumerate(((wg, wg_out), (bg, bg_out))):
        copies.append(pltpu.make_async_copy(src, dst, sem.at[2 * parts + n]))
        copies[-1].start()
    for copy in copies:
        copy.wait()


def per_device(latent, head_weight, head_bias, targets, cell_area, field_level, source):
    vmem = pl.BlockSpec(memory_space=pltpu.VMEM)
    hbm = pl.BlockSpec(memory_space=pltpu.HBM)
    bf16, f32 = jnp.bfloat16, jnp.float32
    dma = pltpu.SemaphoreType.DMA
    operands = (
        latent, head_weight, head_bias.reshape(1, F), field_level.reshape(1, F), targets,
        cell_area.reshape(1, SLOTS), source.reshape(16, 128),
    )
    latents, sums = pl.pallas_call(
        main_kernel,
        out_shape=(
            pltpu.VMEM((2, SLOTS, L), bf16),
            pltpu.VMEM((2 * TILES, TILE, 128), bf16),
        ),
        in_specs=[hbm] * 7,
        out_specs=(vmem, vmem),
        scratch_shapes=[
            pltpu.VMEM((2, NK, 2, CH, L), bf16),
            pltpu.VMEM((F, L), bf16),
            pltpu.VMEM((1, F), bf16),
            pltpu.VMEM((1, F), jnp.int32),
            pltpu.VMEM((1, SLOTS), f32),
            pltpu.VMEM((16, 128), jnp.int32),
            pltpu.VMEM((FB, L), bf16),
            pltpu.VMEM((F, SLOTS), f32),
            pltpu.VMEM((256, SLOTS), bf16),
            pltpu.VMEM((8, SLOTS), f32),
            pltpu.VMEM((PTS, 8, 128), jnp.int32),
            pltpu.VMEM((8, 4, 4, 8, 128), f32),
            pltpu.VMEM((4, PTS, 8, 128), f32),
            pltpu.VMEM((FP, HALF), f32),
            pltpu.VMEM((FP, 128), f32),
            pltpu.VMEM((FP, 128), f32),
            pltpu.VMEM((2, NK, ROWS, CH), bf16),
            pltpu.VMEM((NK, ROWS, CH), bf16),
            pltpu.VMEM((2, NK, ROWS, CH), bf16),
            pltpu.VMEM((NK, 4, FB, CH), bf16),
            pltpu.VMEM((NK, 4, FB, CH), bf16),
            pltpu.VMEM((2, NK, 2, CH, WIDE), bf16),
            pltpu.VMEM((FB, WIDE), f32),
            pltpu.VMEM((FP, 128), f32),
            pltpu.VMEM((CHIPS, TILE, 128), f32),
            pltpu.VMEM((2 * CHIPS, TILE, 128), bf16),
            pltpu.VMEM((4, FP, HALF), f32),
            dma((2 * NK,)),
            dma((5,)),
            dma,
            dma, dma, dma, dma,
            dma((2 * NK,)), dma((2 * NK,)),
            dma((NK,)), dma((NK,)),
            dma((2 * NK,)), dma((2 * NK,)),
            dma((NK,)), dma((NK,)),
            dma((2,)), dma((2,)),
        ],
        compiler_params=pltpu.CompilerParams(
            collective_id=0, has_side_effects=True, vmem_limit_bytes=VMEM
        ),
    )(*(pltpu.with_memory_space_constraint(x, pltpu.HBM) for x in operands))
    latent_grad, weight_grad, bias_grad = pl.pallas_call(
        output_kernel,
        in_specs=[vmem, vmem],
        out_specs=(hbm, hbm, hbm),
        out_shape=(
            jax.ShapeDtypeStruct((2, SLOTS, L), bf16),
            jax.ShapeDtypeStruct((F, L), f32),
            jax.ShapeDtypeStruct((1, F), f32),
        ),
        scratch_shapes=[pltpu.VMEM((F, L), f32), pltpu.VMEM((1, F), f32), dma((10,))],
        compiler_params=pltpu.CompilerParams(vmem_limit_bytes=8 * 2**20),
    )(latents, sums)
    return latent_grad, weight_grad, bias_grad.reshape(F)


def solution(mesh):
    return jax.shard_map(
        per_device,
        mesh=mesh,
        in_specs=(P("mem", "pts", None), P(), P(), P(None, "pts"), P("pts"), P(), P("pts")),
        out_specs=(P("mem", "pts", None), P(), P()),
        check_vma=False,
    )
```

```python
import jax
import jax.numpy as jnp
from jax import lax
from jax.experimental import pallas as pl
from jax.experimental.pallas import tpu as pltpu
from jax.sharding import PartitionSpec as P

M = 8
F = 102
L = 1024
FP = 104
FB = 112
MAIN = 96
SLOTS = 2048
HALF = 1024
CH = 256
NK = HALF // CH
ROWS = 208
PTS = 32
GROUP = 64
TILE = 16
WIDE = L // 2
TILES = (FB // TILE) * (WIDE // 128)
CHIPS = 64
VMEM = 40 * 2**20
EARLY = 2
ORDER = (0, 2, 1, 3)
MESH = pl.DeviceIdType.MESH

FAIR_ALPHA = 0.95
SMOOTH_WIDTH = 0.25
SPREAD = (1.0 - (1.0 - FAIR_ALPHA) / M) / (M - 1)


def smooth_sign(diff):
    return diff * lax.rsqrt(diff * diff + SMOOTH_WIDTH * SMOOTH_WIDTH)


def pair_sums(own, far):
    spread = [None] * len(own)

    def add(at, term):
        spread[at] = term if spread[at] is None else spread[at] + term

    for a in range(len(own)):
        for b in range(a + 1, len(own)):
            q = smooth_sign(own[a] - own[b])
            add(a, q)
            add(b, -q)
        for other in far:
            add(a, smooth_sign(own[a] - other))
    return spread


def gradients(own, spread, target, scale):
    return [
        (scale * (smooth_sign(value - target) - SPREAD * others)).astype(jnp.bfloat16)
        for value, others in zip(own, spread, strict=True)
    ]


def column(row, rows):
    n = row.shape[1]
    at = lax.broadcasted_iota(jnp.int32, (rows, n), 0)
    lane = lax.broadcasted_iota(jnp.int32, (rows, n), 1)
    return jnp.sum(jnp.where(at == lane, row, 0.0), axis=1, keepdims=True)


def main_kernel(
    latent, w_hbm, bias_hbm, level_hbm, tgt, area_hbm, src_hbm,
    lg, ag,
    lat, w_ref, bias_ref, level_ref, area_ref, src_ref,
    wpad, tv, tt, last8, asked, tq, rq, tslot, bcol, wcol,
    psend, pmate, prem, gl, gx, mlat, acc, bsum, rs, accb, sent, sp,
    lat_sem, small_sem, tgt_sem, ask_s, ask_r, tq_s, tq_r,
    ps_far, pr_far, ps_mate, pr_mate, ms, mr, gs, gr, ar_s, ar_r,
):
    i = lax.axis_index("mem")
    pts = lax.axis_index("pts")
    xh = lax.div(i, 2)
    c = lax.rem(i, 2)
    xl = lax.div(pts, 16)
    me = xh * PTS + pts
    mate = (xh * 2 + (1 - c), pts)
    far = ((1 - xh) * 2 + c, pts)
    far_mate = ((1 - xh) * 2 + (1 - c), pts)
    halves = (c, 1 - c)

    def lat_copy(e, k):
        off = pl.multiple_of(halves[e] * HALF + k * CH, CH)
        return pltpu.make_async_copy(
            latent.at[:, pl.ds(off, CH)], lat.at[e, k], lat_sem.at[e * NK + k]
        )

    small = [
        pltpu.make_async_copy(src, dst, small_sem.at[n])
        for n, (src, dst) in enumerate(
            (
                (w_hbm, w_ref), (bias_hbm, bias_ref), (level_hbm, level_ref),
                (area_hbm, area_ref), (src_hbm, src_ref),
            )
        )
    ]
    tgt_copy = pltpu.make_async_copy(tgt, tv, tgt_sem)
    for copy in small:
        copy.start()
    for k in range(NK):
        for e in range(2):
            lat_copy(e, k).start()
        if k == 0:
            tgt_copy.start()

    barrier = pltpu.get_barrier_semaphore()

    def group_device(n):
        q = lax.rem(me + n, GROUP)
        q_xh = lax.div(q, PTS)
        q_pts = lax.rem(q, PTS)
        return q, q_xh, q_pts, (q_xh * 2 + c, q_pts)

    pl.semaphore_signal(barrier, inc=1, device_id=far_mate, device_id_type=MESH)
    pl.semaphore_signal(barrier, inc=1, device_id=mate, device_id_type=MESH)

    def greet(n, _):
        pl.semaphore_signal(barrier, inc=1, device_id=group_device(n)[3], device_id_type=MESH)
        return 0

    lax.fori_loop(1, GROUP, greet, 0)

    for copy in small:
        copy.wait()
    wpad[...] = jnp.zeros_like(wpad)
    wpad[0:F, :] = w_ref[...]
    bcol[...] = jnp.broadcast_to(column(bias_ref[...].astype(jnp.float32), FP), bcol.shape)
    level = (level_ref[...].astype(jnp.float32) + 1.0) / 7.0
    wcol[...] = jnp.broadcast_to(column(level, FP), wcol.shape)
    acc[...] = jnp.zeros_like(acc)
    bsum[...] = jnp.zeros_like(bsum)

    def far_copy(e, k):
        return pltpu.make_async_remote_copy(
            src_ref=psend.at[e, k],
            dst_ref=prem.at[e, k],
            send_sem=ps_far.at[e * NK + k],
            recv_sem=pr_far.at[e * NK + k],
            device_id=far if e == 0 else far_mate,
            device_id_type=MESH,
        )

    def mate_copy(k):
        return pltpu.make_async_remote_copy(
            src_ref=psend.at[1, k],
            dst_ref=pmate.at[k],
            send_sem=ps_mate.at[k],
            recv_sem=pr_mate.at[k],
            device_id=mate,
            device_id_type=MESH,
        )

    def predict(e, k):
        lat_copy(e, k).wait()
        rest = []
        for m in range(2):
            pred = lax.dot_general(
                wpad[...], lat[e, k, m], (((1,), (1,)), ((), ())),
                preferred_element_type=jnp.float32,
            )[0:FP]
            pred = pred + bcol[:, 0:1]
            psend[e, k, m * MAIN : (m + 1) * MAIN, :] = pred[0:MAIN].astype(jnp.bfloat16)
            rest.append(pred[MAIN:FP])
        psend[e, k, 2 * MAIN :, :] = jnp.concatenate(rest, axis=0).astype(jnp.bfloat16)

    def send(e, k):
        far_copy(e, k).start()
        if e == 1:
            mate_copy(k).start()

    for e in range(2):
        predict(e, 0)

    pl.semaphore_wait(barrier, GROUP + 1)

    def owner_of(n):
        p = lax.rem(pts + n, PTS)
        differ = lax.rem(lax.div(p, 16) + xl, 2)
        return p, (lax.rem(xh + c * differ, 2) * 2 + c, p)

    def across_first(n):
        return 1 + lax.rem(n + 14, PTS - 1)

    def ask(n, _):
        pltpu.make_async_remote_copy(
            src_ref=src_ref.at[pl.ds(pl.multiple_of(8 * c, 8), 8)],
            dst_ref=asked.at[pts],
            send_sem=ask_s,
            recv_sem=ask_r,
            device_id=owner_of(across_first(n))[1],
            device_id_type=MESH,
        ).start()
        return 0

    lax.fori_loop(1, PTS, ask, 0)
    for e in range(2):
        send(e, 0)

    asked[pts] = src_ref[pl.ds(pl.multiple_of(8 * c, 8), 8), :]

    for k in range(1, NK):
        for e in range(2):
            predict(e, k)

    def lend(e, k):
        lanes = pl.ds(pl.multiple_of((1 - c) * WIDE, WIDE), WIDE)
        return pltpu.make_async_remote_copy(
            src_ref=lat.at[e, k, :, :, lanes],
            dst_ref=mlat.at[1 - e, k],
            send_sem=ms.at[e * NK + k],
            recv_sem=mr.at[(1 - e) * NK + k],
            device_id=mate,
            device_id_type=MESH,
        )

    def lent(e, k):
        return pltpu.make_async_copy(mlat.at[e, k], mlat.at[e, k], mr.at[e * NK + k])

    for e in range(2):
        lend(e, 0).start()

    tgt_copy.wait()
    tt[FP:128, :] = jnp.zeros((128 - FP, SLOTS), jnp.bfloat16)
    tt[128 + FP :, :] = jnp.zeros((128 - FP, SLOTS), jnp.bfloat16)
    last8[...] = jnp.zeros_like(last8)
    last8[0 : F - MAIN, :] = tv[MAIN:F, :]
    last8[F - MAIN : F - MAIN + 1, :] = area_ref[...]

    def split(value, at):
        high = value.astype(jnp.bfloat16)
        tt[at : at + value.shape[0], :] = high
        low = (value - high.astype(jnp.float32)).astype(jnp.bfloat16)
        tt[128 + at : 128 + at + value.shape[0], :] = low

    for at in range(0, MAIN, 32):
        split(tv[at : at + 32, :], at)
    split(last8[...], MAIN)


    def asked_bytes(sem):
        return pltpu.make_async_copy(
            asked.at[pl.ds(0, PTS - 1)], asked.at[pl.ds(0, PTS - 1)], sem
        )

    asked_bytes(ask_r).wait()
    for e in range(2):
        send(e, 1)
    found = asked[...].reshape(PTS * 8, 128) - pts * SLOTS
    lane = lax.broadcasted_iota(jnp.int32, (PTS * 8, 128), 1)
    row = lax.broadcasted_iota(jnp.int32, (PTS * 8, 128), 0)
    found = jnp.where(lax.rem(lane, 32) == pts, found, 0)
    spread_row = lax.broadcasted_iota(jnp.int32, (128, 128), 0)
    spread_lane = lax.broadcasted_iota(jnp.int32, (128, 128), 1)
    spread = jnp.where(lax.div(spread_row, 32) == lax.div(spread_lane, 32), 1.0, 0.0)
    spread = spread.astype(jnp.bfloat16)
    high = lax.shift_right_logical(found, 6).astype(jnp.float32).astype(jnp.bfloat16)
    low = lax.bitwise_and(found, 63).astype(jnp.float32).astype(jnp.bfloat16)
    wide = 64.0 * jnp.dot(high, spread, preferred_element_type=jnp.float32) + jnp.dot(
        low, spread, preferred_element_type=jnp.float32
    )
    wide = jnp.where(lax.rem(lane, 32) == lax.rem(row, 32), wide, 0.0)
    wanted = jnp.sum(wide.reshape(8, 32, 128), axis=1)
    for half in range(4):
        cols = jnp.concatenate(
            [column(wanted[2 * half + b : 2 * half + b + 1, :], 128) for b in range(2)], axis=0
        ).astype(jnp.int32)
        place = lax.broadcasted_iota(jnp.int32, (256, SLOTS), 1)
        onehot = jnp.where(place == cols, 1.0, 0.0).astype(jnp.bfloat16)
        got = lax.dot_general(
            onehot, tt[...], (((1,), (1,)), ((), ())), preferred_element_type=jnp.float32
        )
        got = got[:, 0:128] + got[:, 128:256]
        tq[2 * half : 2 * half + 2] = got.reshape(2, 4, 4, 8, 128)

    def answer(n, _):
        p, device = owner_of(across_first(n))
        pltpu.make_async_remote_copy(
            src_ref=tq.at[lax.div(p, 4), :, lax.rem(p, 4)],
            dst_ref=rq.at[:, pts],
            send_sem=tq_s,
            recv_sem=tq_r,
            device_id=device,
            device_id_type=MESH,
        ).start()
        return 0

    lax.fori_loop(1, PTS, answer, 0)
    rq[:, pts] = tq[lax.div(pts, 4), :, lax.rem(pts, 4)]

    for k in range(2, NK):
        for e in range(2):
            send(e, k)
    for k in range(1, NK):
        for e in range(2):
            lend(e, k).start()

    def grad_copy(k):
        return pltpu.make_async_remote_copy(
            src_ref=gl.at[k],
            dst_ref=gx.at[k],
            send_sem=gs.at[k],
            recv_sem=gr.at[k],
            device_id=mate,
            device_id_type=MESH,
        )

    def near_buffers(k):
        return psend.at[0, k], pmate.at[k]

    def far_buffers(k):
        return prem.at[0, k], prem.at[1, k]

    def main_rows(buffers, t, lanes):
        return [
            buffer[pl.ds(pl.multiple_of(m * MAIN + 16 * t, 16), 16), lanes].astype(jnp.float32)
            for m in range(2)
            for buffer in buffers
        ]

    def rest_rows(buffers, lanes):
        rest = [buffer[2 * MAIN : ROWS, lanes].astype(jnp.float32) for buffer in buffers]
        return [value[8 * m : 8 * m + 8] for m in range(2) for value in rest]

    def blocks(k):
        for part in range(CH // 128):
            yield slice(128 * part, 128 * (part + 1)), k * CH + 128 * part

    def pairs_chunk(k):
        mate_copy(k).wait_recv()
        far_copy(0, k).wait_recv()
        far_copy(1, k).wait_recv()
        for lanes, at in blocks(k):

            def step(t, _):
                sums = pair_sums(
                    main_rows(near_buffers(k), t, lanes), main_rows(far_buffers(k), t, lanes)
                )
                for n in range(4):
                    sp[n, pl.ds(pl.multiple_of(16 * t, 16), 16), at : at + 128] = sums[n]
                return 0

            lax.fori_loop(0, MAIN // 16, step, 0)
            sums = pair_sums(rest_rows(near_buffers(k), lanes), rest_rows(far_buffers(k), lanes))
            for n in range(4):
                sp[n, MAIN:FP, at : at + 128] = sums[n]

    def grads_chunk(k):
        for lanes, at in blocks(k):

            def grads_of(own, rows):
                return gradients(
                    own, [sp[n, rows, at : at + 128] for n in range(4)],
                    tslot[rows, at : at + 128], wcol[rows, :] * tslot[F : F + 1, at : at + 128],
                )

            def step(t, _):
                rows = pl.ds(pl.multiple_of(16 * t, 16), 16)
                grads = grads_of(main_rows(near_buffers(k), t, lanes), rows)
                for n in range(4):
                    gl[k, ORDER[n], rows, lanes] = grads[n]
                bsum[rows, :] += sum(grad.astype(jnp.float32) for grad in grads)
                return 0

            lax.fori_loop(0, MAIN // 16, step, 0)
            grads = grads_of(rest_rows(near_buffers(k), lanes), slice(MAIN, FP))
            none = jnp.zeros((8, 128), jnp.float32)
            for n in range(4):
                full = jnp.concatenate([grads[n].astype(jnp.float32), none], axis=0)
                gl[k, ORDER[n], MAIN:FB, lanes] = full.astype(jnp.bfloat16)
            bsum[MAIN:FP, :] += sum(grad.astype(jnp.float32) for grad in grads)

    def own_grads(e, k, m):
        return gl[k, m] if e == 0 else gx[k, 2 + m]

    def latent_grad(e, k):
        for m in range(2):
            part = pl.ds(pl.multiple_of(halves[e] * HALF + k * CH, CH), CH)
            lg[m, part, :] = lax.dot_general(
                own_grads(e, k, m), wpad[...], (((0,), (0,)), ((), ())),
                preferred_element_type=jnp.float32,
            ).astype(jnp.bfloat16)

    def accumulate(e, k):
        lent(e, k).wait()
        lanes = pl.ds(pl.multiple_of(c * WIDE, WIDE), WIDE)
        for m in range(2):
            own, other = (gl[k, m], gl[k, 2 + m]) if e == 0 else (gx[k, 2 + m], gx[k, m])
            acc[...] += jnp.dot(
                own, lat[e, k, m, :, lanes], preferred_element_type=jnp.float32
            ) + jnp.dot(other, mlat[e, k, m], preferred_element_type=jnp.float32)

    for k in range(EARLY):
        pairs_chunk(k)

    def rq_bytes(sem):
        return pltpu.make_async_copy(
            rq.at[:, pl.ds(0, PTS - 1)], rq.at[:, pl.ds(0, PTS - 1)], sem
        )

    rq_bytes(tq_r).wait()
    for r in range(8):
        rows = jnp.concatenate([rq[a, :, r, :] for a in range(4)], axis=0)
        tslot[:, 128 * r : 128 * (r + 1)] = rows.T[0:FP]

    for k in range(NK):
        if k >= EARLY:
            pairs_chunk(k)
        grads_chunk(k)
        grad_copy(k).start()
        accumulate(0, k)
        if k > 0:
            grad_copy(k - 1).wait_recv()
            accumulate(1, k - 1)
    grad_copy(NK - 1).wait_recv()
    accumulate(1, NK - 1)

    at = lax.broadcasted_iota(jnp.int32, (FP, 128), 0)
    lane_at = lax.broadcasted_iota(jnp.int32, (FP, 128), 1)
    bias = jnp.sum(bsum[...], axis=1, keepdims=True)
    bias = jnp.sum(jnp.where(at == lane_at, bias, 0.0), axis=0, keepdims=True)
    acc[MAIN:FP, 0:128] += jnp.where(at[0 : FP - MAIN] == F - MAIN, bias, 0.0)
    y = lax.rem(lax.div(pts, 4), 4)
    z = lax.rem(pts, 4)
    x = xh * 2 + xl
    slot = z * 16 + y * 4 + x

    def tile_at(q_xh, q_y, q_z):
        full = lax.div(q_z, 3) * lax.div(q_y, 2) == 0
        return q_z * 8 + q_y * 2 + q_xh, full, lax.rem(c + q_y + q_z, 2)

    tile, full, tile_xl = tile_at(xh, y, z)
    owns = jnp.logical_and(full, tile_xl == xl)

    def acc_tile(q):
        rows = pl.ds(pl.multiple_of(lax.div(q, 4) * TILE, TILE), TILE)
        return rows, pl.ds(pl.multiple_of(lax.rem(q, 4) * 128, 128), 128)

    ys = [lax.rem(y + d, 4) for d in range(4)]
    xs = [lax.rem(x + d, 4) for d in range(4)]
    far_first = (2, 1, 3, 0)

    def scatter(n, _):
        q_z = lax.rem(z + n + 2, 4)
        for dy in far_first:
            for q_xh in (1 - xh, xh):
                q, q_full, q_xl = tile_at(q_xh, ys[dy], q_z)
                there = q_full
                if dy == 0 and q_xh is xh:
                    there = jnp.logical_and(there, jnp.logical_or(n != 2, q_xl != xl))

                @pl.when(there)
                def _(q=q, q_xh=q_xh, q_xl=q_xl, dy=dy):
                    rows, lanes = acc_tile(q)
                    pltpu.make_async_remote_copy(
                        src_ref=accb.at[rows, lanes], dst_ref=rs.at[slot], send_sem=ar_s.at[0],
                        recv_sem=ar_r.at[0],
                        device_id=(q_xh * 2 + c, q_xl * 16 + ys[dy] * 4 + q_z),
                        device_id_type=MESH,
                    ).start()

        return 0

    accb[...] = acc[...].astype(jnp.bfloat16)
    lax.fori_loop(0, 4, scatter, 0)
    for e in range(2):
        for k in range(NK):
            latent_grad(e, k)

    def tiles(ref, count, sem):
        return pltpu.make_async_copy(ref.at[pl.ds(0, count)], ref.at[pl.ds(0, count)], sem)

    @pl.when(owns)
    def _():
        rows, lanes = acc_tile(tile)
        rs[slot] = accb[rows, lanes]
        tiles(rs, CHIPS - 1, ar_r.at[0]).wait()
        mine = c * TILES + tile
        ag[mine] = jnp.sum(rs[...].astype(jnp.float32), axis=0).astype(jnp.bfloat16)

        def share(device):
            pltpu.make_async_remote_copy(
                src_ref=ag.at[mine], dst_ref=ag.at[mine], send_sem=ar_s.at[1],
                recv_sem=ar_r.at[1], device_id=device, device_id_type=MESH,
            ).start()

        def gather(n, _):
            q_z = lax.rem(z + n + 2, 4)

            def chip(dy, dx):
                q_mem = lax.div(xs[dx], 2) * 2
                q_pts = lax.rem(xs[dx], 2) * 16 + ys[dy] * 4 + q_z
                for core in range(2):
                    share((q_mem + core, q_pts))

            for dy in far_first:
                for dx in far_first:
                    if dy == 0 and dx == 0:
                        pl.when(n != 2)(lambda: chip(0, 0))
                    else:
                        chip(dy, dx)
            return 0

        lax.fori_loop(0, 4, gather, 0)
        share(mate)

    for k in range(NK):
        for e in range(2):
            far_copy(e, k).wait_send()
            lend(e, k).wait_send()
        mate_copy(k).wait_send()
        grad_copy(k).wait_send()
    asked_bytes(ask_s).wait()
    rq_bytes(tq_s).wait()

    @pl.when(owns)
    def _():
        tiles(rs, TILES - 1, ar_s.at[0]).wait()
        tiles(ag, 2 * TILES - 1, ar_r.at[1]).wait()
        tiles(sent, 2 * CHIPS - 1, ar_s.at[1]).wait()

    @pl.when(jnp.logical_not(owns))
    def _():
        tiles(rs, TILES, ar_s.at[0]).wait()
        tiles(ag, 2 * TILES, ar_r.at[1]).wait()


def output_kernel(lg, ag, lg_out, wg_out, bg_out, wg, bg, sem):
    norm = float(M * SLOTS * PTS) ** (-0.5)
    parts = 4
    size = SLOTS // parts
    copies = [
        pltpu.make_async_copy(
            lg.at[m, pl.ds(size * n, size)], lg_out.at[m, pl.ds(size * n, size)],
            sem.at[parts * m + n],
        )
        for m in range(2) for n in range(parts)
    ]
    for copy in copies:
        copy.start()
    for q in range(2 * TILES):
        t, lb = q % TILES // 4, q // TILES * 4 + q % 4
        rows = min(F, TILE * (t + 1)) - TILE * t
        tile_sum = ag[q].astype(jnp.float32) * norm
        wg[TILE * t : TILE * t + rows, 128 * lb : 128 * (lb + 1)] = tile_sum[0:rows]
    last = MAIN // TILE * 4
    pair = ag[last].astype(jnp.float32) + ag[TILES + last].astype(jnp.float32)
    bg[...] = pair[F - MAIN : F - MAIN + 1, 0:F] * norm
    for n, (src, dst) in enumerate(((wg, wg_out), (bg, bg_out))):
        copies.append(pltpu.make_async_copy(src, dst, sem.at[2 * parts + n]))
        copies[-1].start()
    for copy in copies:
        copy.wait()


def per_device(latent, head_weight, head_bias, targets, cell_area, field_level, source):
    vmem = pl.BlockSpec(memory_space=pltpu.VMEM)
    hbm = pl.BlockSpec(memory_space=pltpu.HBM)
    bf16, f32 = jnp.bfloat16, jnp.float32
    dma = pltpu.SemaphoreType.DMA
    operands = (
        latent, head_weight, head_bias.reshape(1, F), field_level.reshape(1, F), targets,
        cell_area.reshape(1, SLOTS), source.reshape(16, 128),
    )
    latents, sums = pl.pallas_call(
        main_kernel,
        out_shape=(
            pltpu.VMEM((2, SLOTS, L), bf16),
            pltpu.VMEM((2 * TILES, TILE, 128), bf16),
        ),
        in_specs=[hbm] * 7,
        out_specs=(vmem, vmem),
        scratch_shapes=[
            pltpu.VMEM((2, NK, 2, CH, L), bf16),
            pltpu.VMEM((F, L), bf16),
            pltpu.VMEM((1, F), bf16),
            pltpu.VMEM((1, F), jnp.int32),
            pltpu.VMEM((1, SLOTS), f32),
            pltpu.VMEM((16, 128), jnp.int32),
            pltpu.VMEM((FB, L), bf16),
            pltpu.VMEM((F, SLOTS), f32),
            pltpu.VMEM((256, SLOTS), bf16),
            pltpu.VMEM((8, SLOTS), f32),
            pltpu.VMEM((PTS, 8, 128), jnp.int32),
            pltpu.VMEM((8, 4, 4, 8, 128), f32),
            pltpu.VMEM((4, PTS, 8, 128), f32),
            pltpu.VMEM((FP, HALF), f32),
            pltpu.VMEM((FP, 128), f32),
            pltpu.VMEM((FP, 128), f32),
            pltpu.VMEM((2, NK, ROWS, CH), bf16),
            pltpu.VMEM((NK, ROWS, CH), bf16),
            pltpu.VMEM((2, NK, ROWS, CH), bf16),
            pltpu.VMEM((NK, 4, FB, CH), bf16),
            pltpu.VMEM((NK, 4, FB, CH), bf16),
            pltpu.VMEM((2, NK, 2, CH, WIDE), bf16),
            pltpu.VMEM((FB, WIDE), f32),
            pltpu.VMEM((FP, 128), f32),
            pltpu.VMEM((CHIPS, TILE, 128), bf16),
            pltpu.VMEM((FB, WIDE), bf16),
            pltpu.VMEM((2 * CHIPS, TILE, 128), bf16),
            pltpu.VMEM((4, FP, HALF), f32),
            dma((2 * NK,)),
            dma((5,)),
            dma,
            dma, dma, dma, dma,
            dma((2 * NK,)), dma((2 * NK,)),
            dma((NK,)), dma((NK,)),
            dma((2 * NK,)), dma((2 * NK,)),
            dma((NK,)), dma((NK,)),
            dma((2,)), dma((2,)),
        ],
        compiler_params=pltpu.CompilerParams(
            collective_id=0, has_side_effects=True, vmem_limit_bytes=VMEM
        ),
    )(*(pltpu.with_memory_space_constraint(x, pltpu.HBM) for x in operands))
    latent_grad, weight_grad, bias_grad = pl.pallas_call(
        output_kernel,
        in_specs=[vmem, vmem],
        out_specs=(hbm, hbm, hbm),
        out_shape=(
            jax.ShapeDtypeStruct((2, SLOTS, L), bf16),
            jax.ShapeDtypeStruct((F, L), f32),
            jax.ShapeDtypeStruct((1, F), f32),
        ),
        scratch_shapes=[pltpu.VMEM((F, L), f32), pltpu.VMEM((1, F), f32), dma((10,))],
        compiler_params=pltpu.CompilerParams(vmem_limit_bytes=8 * 2**20),
    )(latents, sums)
    return latent_grad, weight_grad, bias_grad.reshape(F)


def solution(mesh):
    return jax.shard_map(
        per_device,
        mesh=mesh,
        in_specs=(P("mem", "pts", None), P(), P(), P(None, "pts"), P("pts"), P(), P("pts")),
        out_specs=(P("mem", "pts", None), P(), P()),
        check_vma=False,
    )
```

```python
import jax
import jax.numpy as jnp
from jax import lax
from jax.experimental import pallas as pl
from jax.experimental.pallas import tpu as pltpu
from jax.sharding import PartitionSpec as P

M = 8
F = 102
L = 1024
FP = 104
FB = 112
MAIN = 96
SLOTS = 2048
HALF = 1024
CH = 256
NK = HALF // CH
ROWS = 208
PTS = 32
GROUP = 64
TILE = 16
WIDE = L // 2
TILES = (FB // TILE) * (WIDE // 128)
CHIPS = 64
VMEM = 40 * 2**20
EARLY = 2
SUMS = (((0, 0),), ((0, 1), (1, 0)), (), ((1, 1), (0, 2), (1, 2), (0, 3), (1, 3)))
ORDER = (0, 2, 1, 3)
MESH = pl.DeviceIdType.MESH

FAIR_ALPHA = 0.95
SMOOTH_WIDTH = 0.25
SPREAD = (1.0 - (1.0 - FAIR_ALPHA) / M) / (M - 1)


def smooth_sign(diff):
    return diff * lax.rsqrt(diff * diff + SMOOTH_WIDTH * SMOOTH_WIDTH)


def pair_sums(own, far):
    spread = [None] * len(own)

    def add(at, term):
        spread[at] = term if spread[at] is None else spread[at] + term

    for a in range(len(own)):
        for b in range(a + 1, len(own)):
            q = smooth_sign(own[a] - own[b])
            add(a, q)
            add(b, -q)
        for other in far:
            add(a, smooth_sign(own[a] - other))
    return spread


def gradients(own, spread, target, scale):
    return [
        (scale * (smooth_sign(value - target) - SPREAD * others)).astype(jnp.bfloat16)
        for value, others in zip(own, spread, strict=True)
    ]


def column(row, rows):
    n = row.shape[1]
    at = lax.broadcasted_iota(jnp.int32, (rows, n), 0)
    lane = lax.broadcasted_iota(jnp.int32, (rows, n), 1)
    return jnp.sum(jnp.where(at == lane, row, 0.0), axis=1, keepdims=True)


def main_kernel(
    latent, w_hbm, bias_hbm, level_hbm, tgt, area_hbm, src_hbm,
    lg, ag,
    lat, w_ref, bias_ref, level_ref, area_ref, src_ref,
    wpad, tv, tt, last8, asked, tq, rq, tslot, bcol, wcol,
    psend, pmate, prem, gl, gx, mlat, acc, bsum, rs, accb, sent, sp,
    lat_sem, small_sem, tgt_sem, ask_s, ask_r, tq_s, tq_r,
    ps_far, pr_far, ps_mate, pr_mate, ms, mr, gs, gr, ar_s, ar_r,
):
    i = lax.axis_index("mem")
    pts = lax.axis_index("pts")
    xh = lax.div(i, 2)
    c = lax.rem(i, 2)
    xl = lax.div(pts, 16)
    me = xh * PTS + pts
    mate = (xh * 2 + (1 - c), pts)
    far = ((1 - xh) * 2 + c, pts)
    far_mate = ((1 - xh) * 2 + (1 - c), pts)
    halves = (c, 1 - c)

    def lat_copy(e, k):
        off = pl.multiple_of(halves[e] * HALF + k * CH, CH)
        return pltpu.make_async_copy(
            latent.at[:, pl.ds(off, CH)], lat.at[e, k], lat_sem.at[e * NK + k]
        )

    small = [
        pltpu.make_async_copy(src, dst, small_sem.at[n])
        for n, (src, dst) in enumerate(
            (
                (w_hbm, w_ref), (bias_hbm, bias_ref), (level_hbm, level_ref),
                (area_hbm, area_ref), (src_hbm, src_ref),
            )
        )
    ]
    tgt_copy = pltpu.make_async_copy(tgt, tv, tgt_sem)
    for copy in small:
        copy.start()
    for k in range(NK):
        for e in range(2):
            lat_copy(e, k).start()
        if k == 0:
            tgt_copy.start()

    barrier = pltpu.get_barrier_semaphore()

    def group_device(n):
        q = lax.rem(me + n, GROUP)
        q_xh = lax.div(q, PTS)
        q_pts = lax.rem(q, PTS)
        return q, q_xh, q_pts, (q_xh * 2 + c, q_pts)

    pl.semaphore_signal(barrier, inc=1, device_id=far_mate, device_id_type=MESH)
    pl.semaphore_signal(barrier, inc=1, device_id=mate, device_id_type=MESH)

    def greet(n, _):
        pl.semaphore_signal(barrier, inc=1, device_id=group_device(n)[3], device_id_type=MESH)
        return 0

    lax.fori_loop(1, GROUP, greet, 0)

    for copy in small:
        copy.wait()
    wpad[...] = jnp.zeros_like(wpad)
    wpad[0:F, :] = w_ref[...]
    bcol[...] = jnp.broadcast_to(column(bias_ref[...].astype(jnp.float32), FP), bcol.shape)
    level = (level_ref[...].astype(jnp.float32) + 1.0) / 7.0
    wcol[...] = jnp.broadcast_to(column(level, FP), wcol.shape)
    acc[...] = jnp.zeros_like(acc)
    bsum[...] = jnp.zeros_like(bsum)

    def far_copy(e, k):
        return pltpu.make_async_remote_copy(
            src_ref=psend.at[e, k],
            dst_ref=prem.at[e, k],
            send_sem=ps_far.at[e * NK + k],
            recv_sem=pr_far.at[e * NK + k],
            device_id=far if e == 0 else far_mate,
            device_id_type=MESH,
        )

    def mate_copy(k):
        return pltpu.make_async_remote_copy(
            src_ref=psend.at[1, k],
            dst_ref=pmate.at[k],
            send_sem=ps_mate.at[k],
            recv_sem=pr_mate.at[k],
            device_id=mate,
            device_id_type=MESH,
        )

    def predict(e, k):
        lat_copy(e, k).wait()
        rest = []
        for m in range(2):
            pred = lax.dot_general(
                wpad[...], lat[e, k, m], (((1,), (1,)), ((), ())),
                preferred_element_type=jnp.float32,
            )[0:FP]
            pred = pred + bcol[:, 0:1]
            psend[e, k, m * MAIN : (m + 1) * MAIN, :] = pred[0:MAIN].astype(jnp.bfloat16)
            rest.append(pred[MAIN:FP])
        psend[e, k, 2 * MAIN :, :] = jnp.concatenate(rest, axis=0).astype(jnp.bfloat16)

    def send(e, k):
        far_copy(e, k).start()
        if e == 1:
            mate_copy(k).start()

    for e in range(2):
        predict(e, 0)

    pl.semaphore_wait(barrier, GROUP + 1)

    def owner_of(n):
        p = lax.rem(pts + n, PTS)
        differ = lax.rem(lax.div(p, 16) + xl, 2)
        return p, (lax.rem(xh + c * differ, 2) * 2 + c, p)

    def across_first(n):
        return 1 + lax.rem(n + 14, PTS - 1)

    def ask(n, _):
        pltpu.make_async_remote_copy(
            src_ref=src_ref.at[pl.ds(pl.multiple_of(8 * c, 8), 8)],
            dst_ref=asked.at[pts],
            send_sem=ask_s,
            recv_sem=ask_r,
            device_id=owner_of(across_first(n))[1],
            device_id_type=MESH,
        ).start()
        return 0

    lax.fori_loop(1, PTS, ask, 0)
    for e in range(2):
        send(e, 0)

    asked[pts] = src_ref[pl.ds(pl.multiple_of(8 * c, 8), 8), :]

    for k in range(1, NK):
        for e in range(2):
            predict(e, k)

    def lend(e, k):
        lanes = pl.ds(pl.multiple_of((1 - c) * WIDE, WIDE), WIDE)
        return pltpu.make_async_remote_copy(
            src_ref=lat.at[e, k, :, :, lanes],
            dst_ref=mlat.at[1 - e, k],
            send_sem=ms.at[e * NK + k],
            recv_sem=mr.at[(1 - e) * NK + k],
            device_id=mate,
            device_id_type=MESH,
        )

    def lent(e, k):
        return pltpu.make_async_copy(mlat.at[e, k], mlat.at[e, k], mr.at[e * NK + k])

    for e in range(2):
        lend(e, 0).start()

    tgt_copy.wait()
    tt[FP:128, :] = jnp.zeros((128 - FP, SLOTS), jnp.bfloat16)
    tt[128 + FP :, :] = jnp.zeros((128 - FP, SLOTS), jnp.bfloat16)
    last8[...] = jnp.zeros_like(last8)
    last8[0 : F - MAIN, :] = tv[MAIN:F, :]
    last8[F - MAIN : F - MAIN + 1, :] = area_ref[...]

    def split(value, at):
        high = value.astype(jnp.bfloat16)
        tt[at : at + value.shape[0], :] = high
        low = (value - high.astype(jnp.float32)).astype(jnp.bfloat16)
        tt[128 + at : 128 + at + value.shape[0], :] = low

    for at in range(0, MAIN, 32):
        split(tv[at : at + 32, :], at)
    split(last8[...], MAIN)


    def asked_bytes(sem):
        return pltpu.make_async_copy(
            asked.at[pl.ds(0, PTS - 1)], asked.at[pl.ds(0, PTS - 1)], sem
        )

    asked_bytes(ask_r).wait()
    for e in range(2):
        send(e, 1)
    found = asked[...].reshape(PTS * 8, 128) - pts * SLOTS
    lane = lax.broadcasted_iota(jnp.int32, (PTS * 8, 128), 1)
    row = lax.broadcasted_iota(jnp.int32, (PTS * 8, 128), 0)
    found = jnp.where(lax.rem(lane, 32) == pts, found, 0)
    spread_row = lax.broadcasted_iota(jnp.int32, (128, 128), 0)
    spread_lane = lax.broadcasted_iota(jnp.int32, (128, 128), 1)
    spread = jnp.where(lax.div(spread_row, 32) == lax.div(spread_lane, 32), 1.0, 0.0)
    spread = spread.astype(jnp.bfloat16)
    high = lax.shift_right_logical(found, 6).astype(jnp.float32).astype(jnp.bfloat16)
    low = lax.bitwise_and(found, 63).astype(jnp.float32).astype(jnp.bfloat16)
    wide = 64.0 * jnp.dot(high, spread, preferred_element_type=jnp.float32) + jnp.dot(
        low, spread, preferred_element_type=jnp.float32
    )
    wide = jnp.where(lax.rem(lane, 32) == lax.rem(row, 32), wide, 0.0)
    wanted = jnp.sum(wide.reshape(8, 32, 128), axis=1)
    for half in range(4):
        cols = jnp.concatenate(
            [column(wanted[2 * half + b : 2 * half + b + 1, :], 128) for b in range(2)], axis=0
        ).astype(jnp.int32)
        place = lax.broadcasted_iota(jnp.int32, (256, SLOTS), 1)
        onehot = jnp.where(place == cols, 1.0, 0.0).astype(jnp.bfloat16)
        got = lax.dot_general(
            onehot, tt[...], (((1,), (1,)), ((), ())), preferred_element_type=jnp.float32
        )
        got = got[:, 0:128] + got[:, 128:256]
        tq[2 * half : 2 * half + 2] = got.reshape(2, 4, 4, 8, 128)

    def answer(n, _):
        p, device = owner_of(across_first(n))
        pltpu.make_async_remote_copy(
            src_ref=tq.at[lax.div(p, 4), :, lax.rem(p, 4)],
            dst_ref=rq.at[:, pts],
            send_sem=tq_s,
            recv_sem=tq_r,
            device_id=device,
            device_id_type=MESH,
        ).start()
        return 0

    lax.fori_loop(1, PTS, answer, 0)
    rq[:, pts] = tq[lax.div(pts, 4), :, lax.rem(pts, 4)]

    for k in range(2, NK):
        for e in range(2):
            send(e, k)
    for k in range(1, NK):
        for e in range(2):
            lend(e, k).start()

    def grad_copy(k):
        return pltpu.make_async_remote_copy(
            src_ref=gl.at[k],
            dst_ref=gx.at[k],
            send_sem=gs.at[k],
            recv_sem=gr.at[k],
            device_id=mate,
            device_id_type=MESH,
        )

    def near_buffers(k):
        return psend.at[0, k], pmate.at[k]

    def far_buffers(k):
        return prem.at[0, k], prem.at[1, k]

    def main_rows(buffers, t, lanes):
        return [
            buffer[pl.ds(pl.multiple_of(m * MAIN + 16 * t, 16), 16), lanes].astype(jnp.float32)
            for m in range(2)
            for buffer in buffers
        ]

    def rest_rows(buffers, lanes):
        rest = [buffer[2 * MAIN : ROWS, lanes].astype(jnp.float32) for buffer in buffers]
        return [value[8 * m : 8 * m + 8] for m in range(2) for value in rest]

    def blocks(k):
        for part in range(CH // 128):
            yield slice(128 * part, 128 * (part + 1)), k * CH + 128 * part

    def pairs_chunk(k):
        mate_copy(k).wait_recv()
        far_copy(0, k).wait_recv()
        far_copy(1, k).wait_recv()
        for lanes, at in blocks(k):

            def step(t, _):
                sums = pair_sums(
                    main_rows(near_buffers(k), t, lanes), main_rows(far_buffers(k), t, lanes)
                )
                for n in range(4):
                    sp[n, pl.ds(pl.multiple_of(16 * t, 16), 16), at : at + 128] = sums[n]
                return 0

            lax.fori_loop(0, MAIN // 16, step, 0, unroll=3)
            sums = pair_sums(rest_rows(near_buffers(k), lanes), rest_rows(far_buffers(k), lanes))
            for n in range(4):
                sp[n, MAIN:FP, at : at + 128] = sums[n]

    def grads_chunk(k):
        for lanes, at in blocks(k):

            def grads_of(own, rows):
                return gradients(
                    own, [sp[n, rows, at : at + 128] for n in range(4)],
                    tslot[rows, at : at + 128], wcol[rows, :] * tslot[F : F + 1, at : at + 128],
                )

            def step(t, _):
                rows = pl.ds(pl.multiple_of(16 * t, 16), 16)
                grads = grads_of(main_rows(near_buffers(k), t, lanes), rows)
                for n in range(4):
                    gl[k, ORDER[n], rows, lanes] = grads[n]
                bsum[rows, :] += sum(grad.astype(jnp.float32) for grad in grads)
                return 0

            lax.fori_loop(0, MAIN // 16, step, 0, unroll=3)
            grads = grads_of(rest_rows(near_buffers(k), lanes), slice(MAIN, FP))
            none = jnp.zeros((8, 128), jnp.float32)
            for n in range(4):
                full = jnp.concatenate([grads[n].astype(jnp.float32), none], axis=0)
                gl[k, ORDER[n], MAIN:FB, lanes] = full.astype(jnp.bfloat16)
            bsum[MAIN:FP, :] += sum(grad.astype(jnp.float32) for grad in grads)

    def own_grads(e, k, m):
        return gl[k, m] if e == 0 else gx[k, 2 + m]

    def latent_grad(e, k):
        for m in range(2):
            part = pl.ds(pl.multiple_of(halves[e] * HALF + k * CH, CH), CH)
            lg[m, part, :] = lax.dot_general(
                own_grads(e, k, m), wpad[...], (((0,), (0,)), ((), ())),
                preferred_element_type=jnp.float32,
            ).astype(jnp.bfloat16)

    def accumulate(e, k):
        lent(e, k).wait()
        lanes = pl.ds(pl.multiple_of(c * WIDE, WIDE), WIDE)
        for m in range(2):
            own, other = (gl[k, m], gl[k, 2 + m]) if e == 0 else (gx[k, 2 + m], gx[k, m])
            acc[...] += jnp.dot(
                own, lat[e, k, m, :, lanes], preferred_element_type=jnp.float32
            ) + jnp.dot(other, mlat[e, k, m], preferred_element_type=jnp.float32)

    for k in range(EARLY):
        pairs_chunk(k)

    def rq_bytes(sem):
        return pltpu.make_async_copy(
            rq.at[:, pl.ds(0, PTS - 1)], rq.at[:, pl.ds(0, PTS - 1)], sem
        )

    rq_bytes(tq_r).wait()
    for r in range(8):
        rows = jnp.concatenate([rq[a, :, r, :] for a in range(4)], axis=0)
        tslot[:, 128 * r : 128 * (r + 1)] = rows.T[0:FP]

    for k in range(NK):
        if k >= EARLY:
            pairs_chunk(k)
        grads_chunk(k)
        grad_copy(k).start()
        for e, done in SUMS[k]:
            if e == 1:
                grad_copy(done).wait_recv()
            accumulate(e, done)

    at = lax.broadcasted_iota(jnp.int32, (FP, 128), 0)
    lane_at = lax.broadcasted_iota(jnp.int32, (FP, 128), 1)
    bias = jnp.sum(bsum[...], axis=1, keepdims=True)
    bias = jnp.sum(jnp.where(at == lane_at, bias, 0.0), axis=0, keepdims=True)
    acc[MAIN:FP, 0:128] += jnp.where(at[0 : FP - MAIN] == F - MAIN, bias, 0.0)
    y = lax.rem(lax.div(pts, 4), 4)
    z = lax.rem(pts, 4)
    x = xh * 2 + xl
    slot = z * 16 + y * 4 + x

    def tile_at(q_xh, q_y, q_z):
        full = lax.div(q_z, 3) * lax.div(q_y, 2) == 0
        return q_z * 8 + q_y * 2 + q_xh, full, lax.rem(c + q_y + q_z, 2)

    tile, full, tile_xl = tile_at(xh, y, z)
    owns = jnp.logical_and(full, tile_xl == xl)

    def acc_tile(q):
        rows = pl.ds(pl.multiple_of(lax.div(q, 4) * TILE, TILE), TILE)
        return rows, pl.ds(pl.multiple_of(lax.rem(q, 4) * 128, 128), 128)

    ys = [lax.rem(y + d, 4) for d in range(4)]
    xs = [lax.rem(x + d, 4) for d in range(4)]
    far_first = (2, 1, 3, 0)

    def scatter(n, _):
        q_z = lax.rem(z + n + 2, 4)
        for dy in far_first:
            for q_xh in (1 - xh, xh):
                q, q_full, q_xl = tile_at(q_xh, ys[dy], q_z)
                there = q_full
                if dy == 0 and q_xh is xh:
                    there = jnp.logical_and(there, jnp.logical_or(n != 2, q_xl != xl))

                @pl.when(there)
                def _(q=q, q_xh=q_xh, q_xl=q_xl, dy=dy):
                    rows, lanes = acc_tile(q)
                    pltpu.make_async_remote_copy(
                        src_ref=accb.at[rows, lanes], dst_ref=rs.at[slot], send_sem=ar_s.at[0],
                        recv_sem=ar_r.at[0],
                        device_id=(q_xh * 2 + c, q_xl * 16 + ys[dy] * 4 + q_z),
                        device_id_type=MESH,
                    ).start()

        return 0

    accb[...] = acc[...].astype(jnp.bfloat16)
    lax.fori_loop(0, 4, scatter, 0)
    for e in range(2):
        for k in range(NK):
            latent_grad(e, k)

    def tiles(ref, count, sem):
        return pltpu.make_async_copy(ref.at[pl.ds(0, count)], ref.at[pl.ds(0, count)], sem)

    @pl.when(owns)
    def _():
        rows, lanes = acc_tile(tile)
        rs[slot] = accb[rows, lanes]
        tiles(rs, CHIPS - 1, ar_r.at[0]).wait()
        mine = c * TILES + tile
        ag[mine] = jnp.sum(rs[...].astype(jnp.float32), axis=0).astype(jnp.bfloat16)

        def share(device):
            pltpu.make_async_remote_copy(
                src_ref=ag.at[mine], dst_ref=ag.at[mine], send_sem=ar_s.at[1],
                recv_sem=ar_r.at[1], device_id=device, device_id_type=MESH,
            ).start()

        def gather(n, _):
            q_z = lax.rem(z + n + 2, 4)

            def chip(dy, dx):
                q_mem = lax.div(xs[dx], 2) * 2
                q_pts = lax.rem(xs[dx], 2) * 16 + ys[dy] * 4 + q_z
                for core in range(2):
                    share((q_mem + core, q_pts))

            for dy in far_first:
                for dx in far_first:
                    if dy == 0 and dx == 0:
                        pl.when(n != 2)(lambda: chip(0, 0))
                    else:
                        chip(dy, dx)
            return 0

        lax.fori_loop(0, 4, gather, 0)
        share(mate)

    for k in range(NK):
        for e in range(2):
            far_copy(e, k).wait_send()
            lend(e, k).wait_send()
        mate_copy(k).wait_send()
        grad_copy(k).wait_send()
    asked_bytes(ask_s).wait()
    rq_bytes(tq_s).wait()

    @pl.when(owns)
    def _():
        tiles(rs, TILES - 1, ar_s.at[0]).wait()
        tiles(ag, 2 * TILES - 1, ar_r.at[1]).wait()
        tiles(sent, 2 * CHIPS - 1, ar_s.at[1]).wait()

    @pl.when(jnp.logical_not(owns))
    def _():
        tiles(rs, TILES, ar_s.at[0]).wait()
        tiles(ag, 2 * TILES, ar_r.at[1]).wait()


def output_kernel(lg, ag, lg_out, wg_out, bg_out, wg, bg, sem):
    norm = float(M * SLOTS * PTS) ** (-0.5)
    parts = 4
    size = SLOTS // parts
    copies = [
        pltpu.make_async_copy(
            lg.at[m, pl.ds(size * n, size)], lg_out.at[m, pl.ds(size * n, size)],
            sem.at[parts * m + n],
        )
        for m in range(2) for n in range(parts)
    ]
    for copy in copies:
        copy.start()
    for q in range(2 * TILES):
        t, lb = q % TILES // 4, q // TILES * 4 + q % 4
        rows = min(F, TILE * (t + 1)) - TILE * t
        tile_sum = ag[q].astype(jnp.float32) * norm
        wg[TILE * t : TILE * t + rows, 128 * lb : 128 * (lb + 1)] = tile_sum[0:rows]
    last = MAIN // TILE * 4
    pair = ag[last].astype(jnp.float32) + ag[TILES + last].astype(jnp.float32)
    bg[...] = pair[F - MAIN : F - MAIN + 1, 0:F] * norm
    for n, (src, dst) in enumerate(((wg, wg_out), (bg, bg_out))):
        copies.append(pltpu.make_async_copy(src, dst, sem.at[2 * parts + n]))
        copies[-1].start()
    for copy in copies:
        copy.wait()


def per_device(latent, head_weight, head_bias, targets, cell_area, field_level, source):
    vmem = pl.BlockSpec(memory_space=pltpu.VMEM)
    hbm = pl.BlockSpec(memory_space=pltpu.HBM)
    bf16, f32 = jnp.bfloat16, jnp.float32
    dma = pltpu.SemaphoreType.DMA
    operands = (
        latent, head_weight, head_bias.reshape(1, F), field_level.reshape(1, F), targets,
        cell_area.reshape(1, SLOTS), source.reshape(16, 128),
    )
    latents, sums = pl.pallas_call(
        main_kernel,
        out_shape=(
            pltpu.VMEM((2, SLOTS, L), bf16),
            pltpu.VMEM((2 * TILES, TILE, 128), bf16),
        ),
        in_specs=[hbm] * 7,
        out_specs=(vmem, vmem),
        scratch_shapes=[
            pltpu.VMEM((2, NK, 2, CH, L), bf16),
            pltpu.VMEM((F, L), bf16),
            pltpu.VMEM((1, F), bf16),
            pltpu.VMEM((1, F), jnp.int32),
            pltpu.VMEM((1, SLOTS), f32),
            pltpu.VMEM((16, 128), jnp.int32),
            pltpu.VMEM((FB, L), bf16),
            pltpu.VMEM((F, SLOTS), f32),
            pltpu.VMEM((256, SLOTS), bf16),
            pltpu.VMEM((8, SLOTS), f32),
            pltpu.VMEM((PTS, 8, 128), jnp.int32),
            pltpu.VMEM((8, 4, 4, 8, 128), f32),
            pltpu.VMEM((4, PTS, 8, 128), f32),
            pltpu.VMEM((FP, HALF), f32),
            pltpu.VMEM((FP, 128), f32),
            pltpu.VMEM((FP, 128), f32),
            pltpu.VMEM((2, NK, ROWS, CH), bf16),
            pltpu.VMEM((NK, ROWS, CH), bf16),
            pltpu.VMEM((2, NK, ROWS, CH), bf16),
            pltpu.VMEM((NK, 4, FB, CH), bf16),
            pltpu.VMEM((NK, 4, FB, CH), bf16),
            pltpu.VMEM((2, NK, 2, CH, WIDE), bf16),
            pltpu.VMEM((FB, WIDE), f32),
            pltpu.VMEM((FP, 128), f32),
            pltpu.VMEM((CHIPS, TILE, 128), bf16),
            pltpu.VMEM((FB, WIDE), bf16),
            pltpu.VMEM((2 * CHIPS, TILE, 128), bf16),
            pltpu.VMEM((4, FP, HALF), f32),
            dma((2 * NK,)),
            dma((5,)),
            dma,
            dma, dma, dma, dma,
            dma((2 * NK,)), dma((2 * NK,)),
            dma((NK,)), dma((NK,)),
            dma((2 * NK,)), dma((2 * NK,)),
            dma((NK,)), dma((NK,)),
            dma((2,)), dma((2,)),
        ],
        compiler_params=pltpu.CompilerParams(
            collective_id=0, has_side_effects=True, vmem_limit_bytes=VMEM
        ),
    )(*(pltpu.with_memory_space_constraint(x, pltpu.HBM) for x in operands))
    latent_grad, weight_grad, bias_grad = pl.pallas_call(
        output_kernel,
        in_specs=[vmem, vmem],
        out_specs=(hbm, hbm, hbm),
        out_shape=(
            jax.ShapeDtypeStruct((2, SLOTS, L), bf16),
            jax.ShapeDtypeStruct((F, L), f32),
            jax.ShapeDtypeStruct((1, F), f32),
        ),
        scratch_shapes=[pltpu.VMEM((F, L), f32), pltpu.VMEM((1, F), f32), dma((10,))],
        compiler_params=pltpu.CompilerParams(vmem_limit_bytes=8 * 2**20),
    )(latents, sums)
    return latent_grad, weight_grad, bias_grad.reshape(F)


def solution(mesh):
    return jax.shard_map(
        per_device,
        mesh=mesh,
        in_specs=(P("mem", "pts", None), P(), P(), P(None, "pts"), P("pts"), P(), P("pts")),
        out_specs=(P("mem", "pts", None), P(), P()),
        check_vma=False,
    )
```

```python
import jax
import jax.numpy as jnp
from jax import lax
from jax.experimental import pallas as pl
from jax.experimental.pallas import tpu as pltpu
from jax.sharding import PartitionSpec as P

M = 8
F = 102
L = 1024
FP = 104
FB = 112
MAIN = 96
SLOTS = 2048
HALF = 1024
CH = 256
NK = HALF // CH
ROWS = 208
PTS = 32
GROUP = 64
TILE = 16
WIDE = L // 2
TILES = (FB // TILE) * (WIDE // 128)
CHIPS = 64
VMEM = 40 * 2**20
EARLY = 2
SUMS = (((0, 0),), ((0, 1), (1, 0)), (), ((1, 1), (0, 2), (1, 2), (0, 3), (1, 3)))
ORDER = (0, 2, 1, 3)
MESH = pl.DeviceIdType.MESH

FAIR_ALPHA = 0.95
SMOOTH_WIDTH = 0.25
SPREAD = (1.0 - (1.0 - FAIR_ALPHA) / M) / (M - 1)


def smooth_sign(diff):
    return diff * lax.rsqrt(diff * diff + SMOOTH_WIDTH * SMOOTH_WIDTH)


def pair_sums(own, far):
    spread = [None] * len(own)

    def add(at, term):
        spread[at] = term if spread[at] is None else spread[at] + term

    for a in range(len(own)):
        for b in range(a + 1, len(own)):
            q = smooth_sign(own[a] - own[b])
            add(a, q)
            add(b, -q)
        for other in far:
            add(a, smooth_sign(own[a] - other))
    return spread


def gradients(own, spread, target, scale):
    return [
        (scale * (smooth_sign(value - target) - SPREAD * others)).astype(jnp.bfloat16)
        for value, others in zip(own, spread, strict=True)
    ]


def column(row, rows):
    n = row.shape[1]
    at = lax.broadcasted_iota(jnp.int32, (rows, n), 0)
    lane = lax.broadcasted_iota(jnp.int32, (rows, n), 1)
    return jnp.sum(jnp.where(at == lane, row, 0.0), axis=1, keepdims=True)


def main_kernel(
    latent, w_hbm, bias_hbm, level_hbm, tgt, area_hbm, src_hbm,
    lg, ag,
    lat, w_ref, bias_ref, level_ref, area_ref, src_ref,
    wpad, tv, tt, last8, asked, tq, rq, tslot, bcol, wcol,
    psend, pmate, prem, gl, gx, mlat, acc, bsum, rs, accb, sent, sp,
    lat_sem, small_sem, tgt_sem, ask_s, ask_r, tq_s, tq_r,
    ps_far, pr_far, ps_mate, pr_mate, ms, mr, gs, gr, ar_s, ar_r,
):
    i = lax.axis_index("mem")
    pts = lax.axis_index("pts")
    xh = lax.div(i, 2)
    c = lax.rem(i, 2)
    xl = lax.div(pts, 16)
    me = xh * PTS + pts
    mate = (xh * 2 + (1 - c), pts)
    far = ((1 - xh) * 2 + c, pts)
    far_mate = ((1 - xh) * 2 + (1 - c), pts)
    halves = (c, 1 - c)

    def lat_copy(e, k):
        off = pl.multiple_of(halves[e] * HALF + k * CH, CH)
        return pltpu.make_async_copy(
            latent.at[:, pl.ds(off, CH)], lat.at[e, k], lat_sem.at[e * NK + k]
        )

    small = [
        pltpu.make_async_copy(src, dst, small_sem.at[n])
        for n, (src, dst) in enumerate(
            (
                (w_hbm, w_ref), (bias_hbm, bias_ref), (level_hbm, level_ref),
                (area_hbm, area_ref), (src_hbm, src_ref),
            )
        )
    ]
    tgt_copy = pltpu.make_async_copy(tgt, tv, tgt_sem)
    for copy in small:
        copy.start()
    for k in range(NK):
        for e in range(2):
            lat_copy(e, k).start()
        if k == 0:
            tgt_copy.start()

    barrier = pltpu.get_barrier_semaphore()

    def group_device(n):
        q = lax.rem(me + n, GROUP)
        q_xh = lax.div(q, PTS)
        q_pts = lax.rem(q, PTS)
        return q, q_xh, q_pts, (q_xh * 2 + c, q_pts)

    pl.semaphore_signal(barrier, inc=1, device_id=far_mate, device_id_type=MESH)
    pl.semaphore_signal(barrier, inc=1, device_id=mate, device_id_type=MESH)

    def greet(n, _):
        pl.semaphore_signal(barrier, inc=1, device_id=group_device(n)[3], device_id_type=MESH)
        return 0

    lax.fori_loop(1, GROUP, greet, 0)

    for copy in small:
        copy.wait()
    wpad[...] = jnp.zeros_like(wpad)
    wpad[0:F, :] = w_ref[...]
    bcol[...] = jnp.broadcast_to(column(bias_ref[...].astype(jnp.float32), FP), bcol.shape)
    level = (level_ref[...].astype(jnp.float32) + 1.0) / 7.0
    wcol[...] = jnp.broadcast_to(column(level, FP), wcol.shape)
    acc[...] = jnp.zeros_like(acc)
    bsum[...] = jnp.zeros_like(bsum)

    def far_copy(e, k):
        return pltpu.make_async_remote_copy(
            src_ref=psend.at[e, k],
            dst_ref=prem.at[e, k],
            send_sem=ps_far.at[e * NK + k],
            recv_sem=pr_far.at[e * NK + k],
            device_id=far if e == 0 else far_mate,
            device_id_type=MESH,
        )

    def mate_copy(k):
        return pltpu.make_async_remote_copy(
            src_ref=psend.at[1, k],
            dst_ref=pmate.at[k],
            send_sem=ps_mate.at[k],
            recv_sem=pr_mate.at[k],
            device_id=mate,
            device_id_type=MESH,
        )

    def predict(e, k):
        lat_copy(e, k).wait()
        rest = []
        for m in range(2):
            pred = lax.dot_general(
                wpad[...], lat[e, k, m], (((1,), (1,)), ((), ())),
                preferred_element_type=jnp.float32,
            )[0:FP]
            pred = pred + bcol[:, 0:1]
            psend[e, k, m * MAIN : (m + 1) * MAIN, :] = pred[0:MAIN].astype(jnp.bfloat16)
            rest.append(pred[MAIN:FP])
        psend[e, k, 2 * MAIN :, :] = jnp.concatenate(rest, axis=0).astype(jnp.bfloat16)

    def send(e, k):
        far_copy(e, k).start()
        if e == 1:
            mate_copy(k).start()

    for e in range(2):
        predict(e, 0)

    pl.semaphore_wait(barrier, GROUP + 1)

    def owner_of(n):
        p = lax.rem(pts + n, PTS)
        differ = lax.rem(lax.div(p, 16) + xl, 2)
        return p, (lax.rem(xh + c * differ, 2) * 2 + c, p)

    def across_first(n):
        return 1 + lax.rem(n + 14, PTS - 1)

    def ask(n, _):
        pltpu.make_async_remote_copy(
            src_ref=src_ref.at[pl.ds(pl.multiple_of(8 * c, 8), 8)],
            dst_ref=asked.at[pts],
            send_sem=ask_s,
            recv_sem=ask_r,
            device_id=owner_of(across_first(n))[1],
            device_id_type=MESH,
        ).start()
        return 0

    lax.fori_loop(1, PTS, ask, 0)
    for e in range(2):
        send(e, 0)

    asked[pts] = src_ref[pl.ds(pl.multiple_of(8 * c, 8), 8), :]

    for k in range(1, NK):
        for e in range(2):
            predict(e, k)

    def lend(e, k):
        lanes = pl.ds(pl.multiple_of((1 - c) * WIDE, WIDE), WIDE)
        return pltpu.make_async_remote_copy(
            src_ref=lat.at[e, k, :, :, lanes],
            dst_ref=mlat.at[1 - e, k],
            send_sem=ms.at[e * NK + k],
            recv_sem=mr.at[(1 - e) * NK + k],
            device_id=mate,
            device_id_type=MESH,
        )

    def lent(e, k):
        return pltpu.make_async_copy(mlat.at[e, k], mlat.at[e, k], mr.at[e * NK + k])

    for e in range(2):
        lend(e, 0).start()

    tgt_copy.wait()
    tt[FP:128, :] = jnp.zeros((128 - FP, SLOTS), jnp.bfloat16)
    tt[128 + FP :, :] = jnp.zeros((128 - FP, SLOTS), jnp.bfloat16)
    last8[...] = jnp.zeros_like(last8)
    last8[0 : F - MAIN, :] = tv[MAIN:F, :]
    last8[F - MAIN : F - MAIN + 1, :] = area_ref[...]

    def split(value, at):
        high = value.astype(jnp.bfloat16)
        tt[at : at + value.shape[0], :] = high
        low = (value - high.astype(jnp.float32)).astype(jnp.bfloat16)
        tt[128 + at : 128 + at + value.shape[0], :] = low

    for at in range(0, MAIN, 32):
        split(tv[at : at + 32, :], at)
    split(last8[...], MAIN)


    def asked_bytes(sem):
        return pltpu.make_async_copy(
            asked.at[pl.ds(0, PTS - 1)], asked.at[pl.ds(0, PTS - 1)], sem
        )

    asked_bytes(ask_r).wait()
    for e in range(2):
        send(e, 1)
    found = asked[...].reshape(PTS * 8, 128) - pts * SLOTS
    lane = lax.broadcasted_iota(jnp.int32, (PTS * 8, 128), 1)
    row = lax.broadcasted_iota(jnp.int32, (PTS * 8, 128), 0)
    found = jnp.where(lax.rem(lane, 32) == pts, found, 0)
    spread_row = lax.broadcasted_iota(jnp.int32, (128, 128), 0)
    spread_lane = lax.broadcasted_iota(jnp.int32, (128, 128), 1)
    spread = jnp.where(lax.div(spread_row, 32) == lax.div(spread_lane, 32), 1.0, 0.0)
    spread = spread.astype(jnp.bfloat16)
    high = lax.shift_right_logical(found, 6).astype(jnp.float32).astype(jnp.bfloat16)
    low = lax.bitwise_and(found, 63).astype(jnp.float32).astype(jnp.bfloat16)
    wide = 64.0 * jnp.dot(high, spread, preferred_element_type=jnp.float32) + jnp.dot(
        low, spread, preferred_element_type=jnp.float32
    )
    wide = jnp.where(lax.rem(lane, 32) == lax.rem(row, 32), wide, 0.0)
    wanted = jnp.sum(wide.reshape(8, 32, 128), axis=1)
    for half in range(4):
        cols = jnp.concatenate(
            [column(wanted[2 * half + b : 2 * half + b + 1, :], 128) for b in range(2)], axis=0
        ).astype(jnp.int32)
        place = lax.broadcasted_iota(jnp.int32, (256, SLOTS), 1)
        onehot = jnp.where(place == cols, 1.0, 0.0).astype(jnp.bfloat16)
        got = lax.dot_general(
            onehot, tt[...], (((1,), (1,)), ((), ())), preferred_element_type=jnp.float32
        )
        got = got[:, 0:128] + got[:, 128:256]
        tq[2 * half : 2 * half + 2] = got.reshape(2, 4, 4, 8, 128)

    def answer(n, _):
        p, device = owner_of(across_first(n))
        pltpu.make_async_remote_copy(
            src_ref=tq.at[lax.div(p, 4), :, lax.rem(p, 4)],
            dst_ref=rq.at[:, pts],
            send_sem=tq_s,
            recv_sem=tq_r,
            device_id=device,
            device_id_type=MESH,
        ).start()
        return 0

    lax.fori_loop(1, PTS, answer, 0)
    rq[:, pts] = tq[lax.div(pts, 4), :, lax.rem(pts, 4)]

    for k in range(2, NK):
        for e in range(2):
            send(e, k)
    for k in range(1, NK):
        for e in range(2):
            lend(e, k).start()

    def grad_copy(k):
        return pltpu.make_async_remote_copy(
            src_ref=gl.at[k],
            dst_ref=gx.at[k],
            send_sem=gs.at[k],
            recv_sem=gr.at[k],
            device_id=mate,
            device_id_type=MESH,
        )

    def near_buffers(k):
        return psend.at[0, k], pmate.at[k]

    def far_buffers(k):
        return prem.at[0, k], prem.at[1, k]

    def main_rows(buffers, t, lanes):
        return [
            buffer[pl.ds(pl.multiple_of(m * MAIN + 16 * t, 16), 16), lanes].astype(jnp.float32)
            for m in range(2)
            for buffer in buffers
        ]

    def rest_rows(buffers, lanes):
        rest = [buffer[2 * MAIN : ROWS, lanes].astype(jnp.float32) for buffer in buffers]
        return [value[8 * m : 8 * m + 8] for m in range(2) for value in rest]

    def blocks(k):
        for part in range(CH // 128):
            yield slice(128 * part, 128 * (part + 1)), k * CH + 128 * part

    def pairs_chunk(k):
        mate_copy(k).wait_recv()
        far_copy(0, k).wait_recv()
        far_copy(1, k).wait_recv()
        for lanes, at in blocks(k):

            def step(t, _):
                sums = pair_sums(
                    main_rows(near_buffers(k), t, lanes), main_rows(far_buffers(k), t, lanes)
                )
                for n in range(4):
                    sp[n, pl.ds(pl.multiple_of(16 * t, 16), 16), at : at + 128] = sums[n]
                return 0

            lax.fori_loop(0, MAIN // 16, step, 0, unroll=6)
            sums = pair_sums(rest_rows(near_buffers(k), lanes), rest_rows(far_buffers(k), lanes))
            for n in range(4):
                sp[n, MAIN:FP, at : at + 128] = sums[n]

    def grads_chunk(k):
        for lanes, at in blocks(k):

            def grads_of(own, rows):
                return gradients(
                    own, [sp[n, rows, at : at + 128] for n in range(4)],
                    tslot[rows, at : at + 128], wcol[rows, :] * tslot[F : F + 1, at : at + 128],
                )

            def step(t, _):
                rows = pl.ds(pl.multiple_of(16 * t, 16), 16)
                grads = grads_of(main_rows(near_buffers(k), t, lanes), rows)
                for n in range(4):
                    gl[k, ORDER[n], rows, lanes] = grads[n]
                bsum[rows, :] += sum(grad.astype(jnp.float32) for grad in grads)
                return 0

            lax.fori_loop(0, MAIN // 16, step, 0, unroll=6)
            grads = grads_of(rest_rows(near_buffers(k), lanes), slice(MAIN, FP))
            none = jnp.zeros((8, 128), jnp.float32)
            for n in range(4):
                full = jnp.concatenate([grads[n].astype(jnp.float32), none], axis=0)
                gl[k, ORDER[n], MAIN:FB, lanes] = full.astype(jnp.bfloat16)
            bsum[MAIN:FP, :] += sum(grad.astype(jnp.float32) for grad in grads)

    def own_grads(e, k, m):
        return gl[k, m] if e == 0 else gx[k, 2 + m]

    def latent_grad(e, k):
        for m in range(2):
            part = pl.ds(pl.multiple_of(halves[e] * HALF + k * CH, CH), CH)
            lg[m, part, :] = lax.dot_general(
                own_grads(e, k, m), wpad[...], (((0,), (0,)), ((), ())),
                preferred_element_type=jnp.float32,
            ).astype(jnp.bfloat16)

    def accumulate(e, k):
        lent(e, k).wait()
        lanes = pl.ds(pl.multiple_of(c * WIDE, WIDE), WIDE)
        for m in range(2):
            own, other = (gl[k, m], gl[k, 2 + m]) if e == 0 else (gx[k, 2 + m], gx[k, m])
            acc[...] += jnp.dot(
                own, lat[e, k, m, :, lanes], preferred_element_type=jnp.float32
            ) + jnp.dot(other, mlat[e, k, m], preferred_element_type=jnp.float32)

    for k in range(EARLY):
        pairs_chunk(k)

    def rq_bytes(sem):
        return pltpu.make_async_copy(
            rq.at[:, pl.ds(0, PTS - 1)], rq.at[:, pl.ds(0, PTS - 1)], sem
        )

    rq_bytes(tq_r).wait()
    for r in range(8):
        rows = jnp.concatenate([rq[a, :, r, :] for a in range(4)], axis=0)
        tslot[:, 128 * r : 128 * (r + 1)] = rows.T[0:FP]

    for k in range(NK):
        if k >= EARLY:
            pairs_chunk(k)
        grads_chunk(k)
        grad_copy(k).start()
        for e, done in SUMS[k]:
            if e == 1:
                grad_copy(done).wait_recv()
            accumulate(e, done)

    at = lax.broadcasted_iota(jnp.int32, (FP, 128), 0)
    lane_at = lax.broadcasted_iota(jnp.int32, (FP, 128), 1)
    bias = jnp.sum(bsum[...], axis=1, keepdims=True)
    bias = jnp.sum(jnp.where(at == lane_at, bias, 0.0), axis=0, keepdims=True)
    acc[MAIN:FP, 0:128] += jnp.where(at[0 : FP - MAIN] == F - MAIN, bias, 0.0)
    y = lax.rem(lax.div(pts, 4), 4)
    z = lax.rem(pts, 4)
    x = xh * 2 + xl
    slot = z * 16 + y * 4 + x

    def tile_at(q_xh, q_y, q_z):
        full = lax.div(q_z, 3) * lax.div(q_y, 2) == 0
        return q_z * 8 + q_y * 2 + q_xh, full, lax.rem(c + q_y + q_z, 2)

    tile, full, tile_xl = tile_at(xh, y, z)
    owns = jnp.logical_and(full, tile_xl == xl)

    def acc_tile(q):
        rows = pl.ds(pl.multiple_of(lax.div(q, 4) * TILE, TILE), TILE)
        return rows, pl.ds(pl.multiple_of(lax.rem(q, 4) * 128, 128), 128)

    ys = [lax.rem(y + d, 4) for d in range(4)]
    xs = [lax.rem(x + d, 4) for d in range(4)]
    far_first = (2, 1, 3, 0)

    def scatter(n, _):
        q_z = lax.rem(z + n + 2, 4)
        for dy in far_first:
            for q_xh in (1 - xh, xh):
                q, q_full, q_xl = tile_at(q_xh, ys[dy], q_z)
                there = q_full
                if dy == 0 and q_xh is xh:
                    there = jnp.logical_and(there, jnp.logical_or(n != 2, q_xl != xl))

                @pl.when(there)
                def _(q=q, q_xh=q_xh, q_xl=q_xl, dy=dy):
                    rows, lanes = acc_tile(q)
                    pltpu.make_async_remote_copy(
                        src_ref=accb.at[rows, lanes], dst_ref=rs.at[slot], send_sem=ar_s.at[0],
                        recv_sem=ar_r.at[0],
                        device_id=(q_xh * 2 + c, q_xl * 16 + ys[dy] * 4 + q_z),
                        device_id_type=MESH,
                    ).start()

        return 0

    accb[...] = acc[...].astype(jnp.bfloat16)
    lax.fori_loop(0, 4, scatter, 0)
    for e in range(2):
        for k in range(NK):
            latent_grad(e, k)

    def tiles(ref, count, sem):
        return pltpu.make_async_copy(ref.at[pl.ds(0, count)], ref.at[pl.ds(0, count)], sem)

    @pl.when(owns)
    def _():
        rows, lanes = acc_tile(tile)
        rs[slot] = accb[rows, lanes]
        tiles(rs, CHIPS - 1, ar_r.at[0]).wait()
        mine = c * TILES + tile
        ag[mine] = jnp.sum(rs[...].astype(jnp.float32), axis=0).astype(jnp.bfloat16)

        def share(device):
            pltpu.make_async_remote_copy(
                src_ref=ag.at[mine], dst_ref=ag.at[mine], send_sem=ar_s.at[1],
                recv_sem=ar_r.at[1], device_id=device, device_id_type=MESH,
            ).start()

        def gather(n, _):
            q_z = lax.rem(z + n + 2, 4)

            def chip(dy, dx):
                q_mem = lax.div(xs[dx], 2) * 2
                q_pts = lax.rem(xs[dx], 2) * 16 + ys[dy] * 4 + q_z
                for core in range(2):
                    share((q_mem + core, q_pts))

            for dy in far_first:
                for dx in far_first:
                    if dy == 0 and dx == 0:
                        pl.when(n != 2)(lambda: chip(0, 0))
                    else:
                        chip(dy, dx)
            return 0

        lax.fori_loop(0, 4, gather, 0)
        share(mate)

    for k in range(NK):
        for e in range(2):
            far_copy(e, k).wait_send()
            lend(e, k).wait_send()
        mate_copy(k).wait_send()
        grad_copy(k).wait_send()
    asked_bytes(ask_s).wait()
    rq_bytes(tq_s).wait()

    @pl.when(owns)
    def _():
        tiles(rs, TILES - 1, ar_s.at[0]).wait()
        tiles(ag, 2 * TILES - 1, ar_r.at[1]).wait()
        tiles(sent, 2 * CHIPS - 1, ar_s.at[1]).wait()

    @pl.when(jnp.logical_not(owns))
    def _():
        tiles(rs, TILES, ar_s.at[0]).wait()
        tiles(ag, 2 * TILES, ar_r.at[1]).wait()


def output_kernel(lg, ag, lg_out, wg_out, bg_out, wg, bg, sem):
    norm = float(M * SLOTS * PTS) ** (-0.5)
    parts = 4
    size = SLOTS // parts
    copies = [
        pltpu.make_async_copy(
            lg.at[m, pl.ds(size * n, size)], lg_out.at[m, pl.ds(size * n, size)],
            sem.at[parts * m + n],
        )
        for m in range(2) for n in range(parts)
    ]
    for copy in copies:
        copy.start()
    for q in range(2 * TILES):
        t, lb = q % TILES // 4, q // TILES * 4 + q % 4
        rows = min(F, TILE * (t + 1)) - TILE * t
        tile_sum = ag[q].astype(jnp.float32) * norm
        wg[TILE * t : TILE * t + rows, 128 * lb : 128 * (lb + 1)] = tile_sum[0:rows]
    last = MAIN // TILE * 4
    pair = ag[last].astype(jnp.float32) + ag[TILES + last].astype(jnp.float32)
    bg[...] = pair[F - MAIN : F - MAIN + 1, 0:F] * norm
    for n, (src, dst) in enumerate(((wg, wg_out), (bg, bg_out))):
        copies.append(pltpu.make_async_copy(src, dst, sem.at[2 * parts + n]))
        copies[-1].start()
    for copy in copies:
        copy.wait()


def per_device(latent, head_weight, head_bias, targets, cell_area, field_level, source):
    vmem = pl.BlockSpec(memory_space=pltpu.VMEM)
    hbm = pl.BlockSpec(memory_space=pltpu.HBM)
    bf16, f32 = jnp.bfloat16, jnp.float32
    dma = pltpu.SemaphoreType.DMA
    operands = (
        latent, head_weight, head_bias.reshape(1, F), field_level.reshape(1, F), targets,
        cell_area.reshape(1, SLOTS), source.reshape(16, 128),
    )
    latents, sums = pl.pallas_call(
        main_kernel,
        out_shape=(
            pltpu.VMEM((2, SLOTS, L), bf16),
            pltpu.VMEM((2 * TILES, TILE, 128), bf16),
        ),
        in_specs=[hbm] * 7,
        out_specs=(vmem, vmem),
        scratch_shapes=[
            pltpu.VMEM((2, NK, 2, CH, L), bf16),
            pltpu.VMEM((F, L), bf16),
            pltpu.VMEM((1, F), bf16),
            pltpu.VMEM((1, F), jnp.int32),
            pltpu.VMEM((1, SLOTS), f32),
            pltpu.VMEM((16, 128), jnp.int32),
            pltpu.VMEM((FB, L), bf16),
            pltpu.VMEM((F, SLOTS), f32),
            pltpu.VMEM((256, SLOTS), bf16),
            pltpu.VMEM((8, SLOTS), f32),
            pltpu.VMEM((PTS, 8, 128), jnp.int32),
            pltpu.VMEM((8, 4, 4, 8, 128), f32),
            pltpu.VMEM((4, PTS, 8, 128), f32),
            pltpu.VMEM((FP, HALF), f32),
            pltpu.VMEM((FP, 128), f32),
            pltpu.VMEM((FP, 128), f32),
            pltpu.VMEM((2, NK, ROWS, CH), bf16),
            pltpu.VMEM((NK, ROWS, CH), bf16),
            pltpu.VMEM((2, NK, ROWS, CH), bf16),
            pltpu.VMEM((NK, 4, FB, CH), bf16),
            pltpu.VMEM((NK, 4, FB, CH), bf16),
            pltpu.VMEM((2, NK, 2, CH, WIDE), bf16),
            pltpu.VMEM((FB, WIDE), f32),
            pltpu.VMEM((FP, 128), f32),
            pltpu.VMEM((CHIPS, TILE, 128), bf16),
            pltpu.VMEM((FB, WIDE), bf16),
            pltpu.VMEM((2 * CHIPS, TILE, 128), bf16),
            pltpu.VMEM((4, FP, HALF), f32),
            dma((2 * NK,)),
            dma((5,)),
            dma,
            dma, dma, dma, dma,
            dma((2 * NK,)), dma((2 * NK,)),
            dma((NK,)), dma((NK,)),
            dma((2 * NK,)), dma((2 * NK,)),
            dma((NK,)), dma((NK,)),
            dma((2,)), dma((2,)),
        ],
        compiler_params=pltpu.CompilerParams(
            collective_id=0, has_side_effects=True, vmem_limit_bytes=VMEM
        ),
    )(*(pltpu.with_memory_space_constraint(x, pltpu.HBM) for x in operands))
    latent_grad, weight_grad, bias_grad = pl.pallas_call(
        output_kernel,
        in_specs=[vmem, vmem],
        out_specs=(hbm, hbm, hbm),
        out_shape=(
            jax.ShapeDtypeStruct((2, SLOTS, L), bf16),
            jax.ShapeDtypeStruct((F, L), f32),
            jax.ShapeDtypeStruct((1, F), f32),
        ),
        scratch_shapes=[pltpu.VMEM((F, L), f32), pltpu.VMEM((1, F), f32), dma((10,))],
        compiler_params=pltpu.CompilerParams(vmem_limit_bytes=8 * 2**20),
    )(latents, sums)
    return latent_grad, weight_grad, bias_grad.reshape(F)


def solution(mesh):
    return jax.shard_map(
        per_device,
        mesh=mesh,
        in_specs=(P("mem", "pts", None), P(), P(), P(None, "pts"), P("pts"), P(), P("pts")),
        out_specs=(P("mem", "pts", None), P(), P()),
        check_vma=False,
    )
```
